32 devices in a mesh: view: 4 (over y, x), space: 8 (over z, core).
Axes of the slice: x: 2, y: 2, z: 4, core: 2. Of those that a mesh axis runs over, the one named last changes fastest.
Arguments:
- params: float32 [59, 8192], P(None, 'space'), may hold values from -6.5 to 4, as said below
- adam_m: float32 [59, 8192], P(None, 'space'), may hold values from -6 to 6
- adam_v: float32 [59, 8192], P(None, 'space'), may hold values from 0.1 to 10
- visible: int32 [8192], P('space'), may hold values 0 or 1
- cameras: float32 [4, 12], P('view'), may hold values from -1 to 3.2, as said below
- send_index: int32 [4, 8, 512], P('view', 'space'), may hold values from 0 to 1023, as said below
- send_count: int32 [4, 8, 8], P('view', 'space'), may hold values from 0 to 64, as said below
- tile_lists: int32 [4, 16, 512], P('view', 'space'), may hold values from -1 to 511, as said below
- tile_pos: int32 [4, 16], P('view', 'space'), may hold values from 0 to 15, as said below
- target: float32 [4, 5, 4096], P('view', None, 'space'), may hold values from -6 to 6
Outputs:
- image: float32 [4, 5, 4096], P('view', None, 'space')
- new_params: float32 [59, 8192], P(None, 'space')
- new_m: float32 [59, 8192], P(None, 'space')
- new_v: float32 [59, 8192], P(None, 'space')
The draws below stay inside these ranges and needn't reach their ends.
Inputs may be any that keep to these rules, and one draw needn't show every extreme that they name: `params`: centre coordinates within [-2.5, 2.5], every centre at depth 1.5 to 4.5 in front of every camera; log scales within [-6.5, -4.5]; quaternion w within [1, 2] and x, y, z within [-1, 1]; opacity logits within [-4, 4]; harmonic coefficients within [-0.9, 0.9]. `cameras`: a rotation by at most 0.1 radians about each axis, and a translation within 0.2 of (0, 0, 3). `send_index`: the slots of one view, source and destination hold distinct local Gaussian numbers; the slots in use of one source name distinct Gaussians over all views and destinations. `send_count`: in every view some destination device receives 64 slots in use from every source. `tile_lists`: entries of a tile name slots in use towards the tile's device; live entries come first and -1 fills the rest; a slot is named by at most one entry of its view; in every view some tile has 512 entries. `tile_pos`: in each view a permutation of the image's tiles.
All inputs are finite; a program needn't handle non-finite values. No bound on the sum of `visible` on one device may be relied on, other than what follows from the above.
Results may differ from the reference program's by a relative error of at most 0.0003.
Values sent between devices are 32-bit elements; how exact they have to be, the bound alone decides.
A program may use at most 64 MiB of HBM per device.

```python
import math
import jax
import jax.numpy as jnp
from jax import lax

NPARAM = 59
LIST = 512
G_DEV = 1024
TILE_DEV = 2
CAP = 64
NVIEW = 4
G = 8192
TILES_VIEW = 16
PIX = 4096


def camera_table(key):
    angles = jax.random.uniform(jax.random.fold_in(key, 3), (NVIEW, 3), jnp.float32, -0.1, 0.1)
    moved = jax.random.uniform(jax.random.fold_in(key, 5), (NVIEW, 3), jnp.float32, -0.2, 0.2)
    cosine = jnp.cos(angles)
    sine = jnp.sin(angles)
    zeros = jnp.zeros((NVIEW,), jnp.float32)
    ones = jnp.ones((NVIEW,), jnp.float32)
    turn_x = jnp.stack([ones, zeros, zeros, zeros, cosine[:, 0], -sine[:, 0], zeros, sine[:, 0], cosine[:, 0]], 1).reshape(NVIEW, 3, 3)
    turn_y = jnp.stack([cosine[:, 1], zeros, sine[:, 1], zeros, ones, zeros, -sine[:, 1], zeros, cosine[:, 1]], 1).reshape(NVIEW, 3, 3)
    turn_z = jnp.stack([cosine[:, 2], -sine[:, 2], zeros, sine[:, 2], cosine[:, 2], zeros, zeros, zeros, ones], 1).reshape(NVIEW, 3, 3)
    whole = jnp.einsum('nij,njk->nik', jnp.einsum('nij,njk->nik', turn_z, turn_y), turn_x)
    offset = moved + jnp.array([0.0, 0.0, 3.0], jnp.float32)[None, :]
    return jnp.concatenate([whole.reshape(NVIEW, 9), offset], axis=1)


def routing_counts(key):
    shards = G // G_DEV
    block_size = G_DEV // NVIEW
    spare = block_size - CAP
    keys = jax.random.split(jax.random.fold_in(key, 7), 2)
    full_dest = jax.random.randint(keys[0], (NVIEW,), 0, shards)
    targets = jax.random.randint(keys[1], (NVIEW, shards, spare), 0, shards)
    view_idx = jnp.broadcast_to(jnp.arange(NVIEW, dtype=jnp.int32)[:, None, None], targets.shape)
    source_idx = jnp.broadcast_to(jnp.arange(shards, dtype=jnp.int32)[None, :, None], targets.shape)
    tallies = jnp.zeros((NVIEW, shards, shards), jnp.int32).at[view_idx, source_idx, targets].add(1)
    counts = jnp.minimum(tallies, CAP)
    places = jnp.arange(shards, dtype=jnp.int32)[None, None, :]
    counts = jnp.where(places == full_dest[:, None, None], CAP, counts)
    return (counts.astype(jnp.int32), full_dest)


def routing_index(key):
    counts, full_dest = routing_counts(key)
    shards = G // G_DEV
    block_size = G_DEV // NVIEW
    orders = jax.vmap(lambda inner: jax.random.permutation(inner, G_DEV))(jax.random.split(jax.random.fold_in(key, 13), shards))
    starts = jnp.cumsum(counts, axis=2) - counts
    slot_ids = jnp.arange(CAP, dtype=jnp.int32)[None, None, None, :]
    view_ids = jnp.arange(NVIEW, dtype=jnp.int32)[:, None, None, None]
    position = (view_ids * block_size + starts[..., None] + slot_ids) % G_DEV
    source_ids = jnp.broadcast_to(jnp.arange(shards, dtype=jnp.int32)[None, :, None, None], position.shape)
    local = orders[source_ids, position]
    return local.reshape(NVIEW, shards, shards * CAP).astype(jnp.int32)


def tile_places(key):
    keys = jax.random.split(jax.random.fold_in(key, 17), NVIEW)
    return jax.vmap(lambda inner: jax.random.permutation(inner, TILES_VIEW))(keys).astype(jnp.int32)


def list_table(key):
    counts, full_dest = routing_counts(key)
    shards = G // G_DEV
    slot_total = shards * CAP
    keys = jax.random.split(jax.random.fold_in(key, 11), 4)
    entry = jnp.arange(slot_total, dtype=jnp.int32)
    source = entry // CAP
    slot = entry % CAP
    live = slot[None, None, :] < jnp.transpose(counts[:, source, :], (0, 2, 1))
    home = jax.random.randint(keys[0], (NVIEW, shards, slot_total), 0, TILE_DEV)
    ranking = jax.vmap(lambda inner: jax.random.permutation(inner, slot_total))(jax.random.split(keys[1], NVIEW))
    full_tile = jax.random.randint(keys[2], (NVIEW,), 0, TILE_DEV)
    at_full = jnp.arange(shards, dtype=jnp.int32)[None, :, None] == full_dest[:, None, None]
    home = jnp.where(at_full & (ranking[:, None, :] < LIST), full_tile[:, None, None], home)
    ordering = jax.vmap(lambda inner: jax.random.permutation(inner, slot_total))(jax.random.split(keys[3], NVIEW * shards)).reshape(NVIEW, shards, slot_total)
    tile_ids = jnp.arange(TILE_DEV, dtype=jnp.int32)[None, None, :, None]
    member = live[:, :, None, :] & (home[:, :, None, :] == tile_ids)
    scores = jnp.where(member, ordering[:, :, None, :], slot_total + entry[None, None, None, :])
    picked = jnp.argsort(scores, axis=3)[..., :LIST]
    kept = jnp.take_along_axis(scores, picked, axis=3) < slot_total
    lists = jnp.where(kept, picked, -1)
    return lists.reshape(NVIEW, TILES_VIEW, LIST).astype(jnp.int32)


def draw_cameras(key, part):
    return camera_table(key)


def draw_send_count(key, part):
    return routing_counts(key)[0]


def draw_send_index(key, part):
    return routing_index(key)


def draw_tile_lists(key, part):
    return list_table(key)


def draw_tile_pos(key, part):
    return tile_places(key)


def draw_params(key, part):
    own = jax.random.split(jax.random.fold_in(key, 23), 9)
    lists = list_table(key)
    index = routing_index(key)
    places = tile_places(key)
    cameras = camera_table(key)
    live = lists >= 0
    clipped = jnp.maximum(lists, 0)
    source = clipped // CAP
    owner = (jnp.arange(TILES_VIEW, dtype=jnp.int32) // TILE_DEV)[None, :, None]
    view_ids = jnp.arange(NVIEW, dtype=jnp.int32)[:, None, None]
    local = index[view_ids, source, owner * CAP + clipped % CAP]
    gauss_ids = jnp.where(live, source * G_DEV + local, G)
    tiles = places[:, :, None]
    shape = (NVIEW, TILES_VIEW, LIST)
    pixel_x = (16 * (tiles % 64)).astype(jnp.float32) + jax.random.uniform(own[0], shape, jnp.float32, 0.5, 15.5)
    pixel_y = (16 * (tiles // 64)).astype(jnp.float32) + jax.random.uniform(own[1], shape, jnp.float32, 0.5, 15.5)
    steps = jnp.arange(LIST, dtype=jnp.float32)[None, None, :]
    depth = 2.7 + 0.6 * (steps + jax.random.uniform(own[2], shape, jnp.float32, 0.1, 0.9)) / LIST
    center_y = 8.0 * TILES_VIEW / 64.0
    camera_pts = jnp.stack([(pixel_x - 512.0) * depth / 1000.0, (pixel_y - center_y) * depth / 1000.0, depth])
    rotation = cameras[:, :9].reshape(NVIEW, 3, 3)
    offset = jnp.transpose(cameras[:, 9:12])[:, :, None, None]
    world = jnp.einsum('wrc,rwtl->cwtl', rotation, camera_pts - offset)
    low = jnp.array([-1.5, -0.4, -0.4], jnp.float32)[:, None]
    high = jnp.array([1.5, 0.4, 0.4], jnp.float32)[:, None]
    centre = low + (high - low) * jax.random.uniform(own[3], (3, G), jnp.float32)
    centre = centre.at[:, gauss_ids.reshape(-1)].set(world.reshape(3, -1), mode='drop')
    log_scales = jax.random.uniform(own[4], (3, G), jnp.float32, -6.5, -4.5)
    quat_w = jax.random.uniform(own[5], (1, G), jnp.float32, 1.0, 2.0)
    quat_rest = jax.random.uniform(own[6], (3, G), jnp.float32, -1.0, 1.0)
    logits = jax.random.uniform(own[7], (1, G), jnp.float32, -4.0, 4.0)
    harmonics = jnp.clip(0.3 * jax.random.normal(own[8], (48, G), jnp.float32), -0.9, 0.9)
    return jnp.concatenate([centre, log_scales, quat_w, quat_rest, logits, harmonics], axis=0)


def with_ends(values, key, smallest, high):
    longest = values.shape.index(max(values.shape))
    spots = []
    for shift in (0, 1):
        where = [jax.random.randint(jax.random.fold_in(key, axis), (), 0, length) for axis, length in enumerate(values.shape)]
        where[longest] = (where[longest] + shift) % values.shape[longest]
        spots.append(tuple(where))
    return values.at[spots[0]].set(smallest).at[spots[1]].set(high)


def block_scale(rng, dims, cuts, least, top_value):
    loudness, own = 1.0, jax.random.fold_in(rng, 6)
    for dim, shards_of in cuts:
        draws = jnp.exp(jax.random.uniform(jax.random.fold_in(own, dim), (shards_of,), jnp.float32, least / len(cuts), top_value / len(cuts)))
        loudness = loudness * jnp.repeat(draws, dims[dim] // shards_of).reshape([-1 if axis == dim else 1 for axis in range(len(dims))])
    return loudness


def noise(key, dims, width, most, pieces=(), kind=jnp.bfloat16):
    values = width * jax.random.normal(key, dims, jnp.float32)
    if pieces:
        values = values * block_scale(key, dims, pieces, -0.22, 0.18)
    return jnp.clip(values, -most, most).astype(kind)


def setup_inputs(seed: int = 0) -> dict:
    splits = jax.random.split(jax.random.key(seed), 11)
    return {
        "params": draw_params(jax.random.fold_in(splits[10], 71), 0),
        "adam_m": noise(splits[1], (NPARAM, G), 1.0, 6.0, ((1, 8),), jnp.float32),
        "adam_v": jnp.clip(jnp.exp(math.log(10.0) - 4.6051702 * jax.random.uniform(splits[2], (NPARAM, G), jnp.float32) ** block_scale(splits[2], (NPARAM, G), ((1, 8),), -0.2, 0.2)), 0.1, 10.0),
        "visible": with_ends((jax.random.randint(splits[3], (G,), 0, 4) < 3).astype(jnp.int32), jax.random.fold_in(splits[3], 1), 0, 1),
        "cameras": draw_cameras(jax.random.fold_in(splits[10], 71), 0),
        "send_index": draw_send_index(jax.random.fold_in(splits[10], 71), 0),
        "send_count": draw_send_count(jax.random.fold_in(splits[10], 71), 0),
        "tile_lists": draw_tile_lists(jax.random.fold_in(splits[10], 71), 0),
        "tile_pos": draw_tile_pos(jax.random.fold_in(splits[10], 71), 0),
        "target": noise(splits[9], (NVIEW, 5, PIX), 1.0, 6.0, ((0, 4), (2, 8)), jnp.float32),
    }


focal_len = 1000.0
center_x = 512.0
harm_zero = 0.28209479177387814
harm_one = 0.4886025119029199
harm_two = (1.0925484305920792, -1.0925484305920792, 0.31539156525252005, -1.0925484305920792, 0.5462742152960396)
harm_three = (-0.5900435899266435, 2.890611442640554, -0.4570457994644658, 0.3731763325901154, -0.4570457994644658, 1.445305721320277, -0.5900435899266435)
beta_one = 0.9
beta_two = 0.99
learn_rate = 0.05
adam_eps = 1e-08
adam_step = 100.0

def project(gauss, camera, center_y):
    rotation = [[camera[3 * i + j] for j in range(3)] for i in range(3)]
    offset = [camera[9 + i] for i in range(3)]
    centre = [gauss[i] for i in range(3)]
    viewed = [sum((rotation[i][j] * centre[j] for j in range(3))) + offset[i] for i in range(3)]
    inverse = 1.0 / viewed[2]
    screen_x = focal_len * viewed[0] * inverse + center_x
    screen_y = focal_len * viewed[1] * inverse + center_y
    scales = [jnp.exp(gauss[3 + i]) for i in range(3)]
    length = jnp.sqrt(gauss[6] * gauss[6] + gauss[7] * gauss[7] + gauss[8] * gauss[8] + gauss[9] * gauss[9])
    quat_w, quat_x, quat_y, quat_z = [gauss[6 + i] / length for i in range(4)]
    spin = [[1.0 - 2.0 * (quat_y * quat_y + quat_z * quat_z), 2.0 * (quat_x * quat_y - quat_w * quat_z), 2.0 * (quat_x * quat_z + quat_w * quat_y)], [2.0 * (quat_x * quat_y + quat_w * quat_z), 1.0 - 2.0 * (quat_x * quat_x + quat_z * quat_z), 2.0 * (quat_y * quat_z - quat_w * quat_x)], [2.0 * (quat_x * quat_z - quat_w * quat_y), 2.0 * (quat_y * quat_z + quat_w * quat_x), 1.0 - 2.0 * (quat_x * quat_x + quat_y * quat_y)]]
    factor = [[spin[i][j] * scales[j] for j in range(3)] for i in range(3)]
    sigma = [[sum((factor[i][j] * factor[k][j] for j in range(3))) for k in range(3)] for i in range(3)]
    near = focal_len * inverse
    lean_x = -focal_len * viewed[0] * inverse * inverse
    lean_y = -focal_len * viewed[1] * inverse * inverse
    jacob = [[near * rotation[0][j] + lean_x * rotation[2][j] for j in range(3)], [near * rotation[1][j] + lean_y * rotation[2][j] for j in range(3)]]
    halfway = [[sum((jacob[a][i] * sigma[i][k] for i in range(3))) for k in range(3)] for a in range(2)]
    upper = sum((halfway[0][k] * jacob[0][k] for k in range(3))) + 0.3
    middle = sum((halfway[0][k] * jacob[1][k] for k in range(3)))
    lower = sum((halfway[1][k] * jacob[1][k] for k in range(3))) + 0.3
    determinant = upper * lower - middle * middle
    conic_a = lower / determinant
    conic_b = -middle / determinant
    conic_c = upper / determinant
    opacity = jax.nn.sigmoid(gauss[10])
    camera_pos = [-sum((rotation[i][j] * offset[i] for i in range(3))) for j in range(3)]
    toward = [centre[j] - camera_pos[j] for j in range(3)]
    reach = jnp.sqrt(toward[0] * toward[0] + toward[1] * toward[1] + toward[2] * toward[2])
    unit_x = toward[0] / reach
    unit_y = toward[1] / reach
    unit_z = toward[2] / reach
    square_x = unit_x * unit_x
    square_y = unit_y * unit_y
    square_z = unit_z * unit_z
    basis = [harm_zero + 0.0 * unit_x, -harm_one * unit_y, harm_one * unit_z, -harm_one * unit_x, harm_two[0] * unit_x * unit_y, harm_two[1] * unit_y * unit_z, harm_two[2] * (2.0 * square_z - square_x - square_y), harm_two[3] * unit_x * unit_z, harm_two[4] * (square_x - square_y), harm_three[0] * unit_y * (3.0 * square_x - square_y), harm_three[1] * unit_x * unit_y * unit_z, harm_three[2] * unit_y * (4.0 * square_z - square_x - square_y), harm_three[3] * unit_z * (2.0 * square_z - 3.0 * square_x - 3.0 * square_y), harm_three[4] * unit_x * (4.0 * square_z - square_x - square_y), harm_three[5] * unit_z * (square_x - square_y), harm_three[6] * unit_x * (square_x - 3.0 * square_y)]
    colors = [0.5 + sum((basis[k] * gauss[11 + 16 * c + k] for k in range(16))) for c in range(3)]
    return jnp.stack([screen_x, screen_y, conic_a, conic_b, conic_c, opacity, colors[0], colors[1], colors[2], viewed[2], inverse])

def shade_tile(entries, valid, tile):
    lane = jnp.arange(256, dtype=jnp.int32)
    column = tile % 64 * 16 + lane % 16
    height = tile // 64 * 16 + lane // 16
    pixel_x = column.astype(entries.dtype) + 0.5
    pixel_y = height.astype(entries.dtype) + 0.5
    apart_x = pixel_x[:, None] - entries[0][None, :]
    apart_y = pixel_y[:, None] - entries[1][None, :]
    quad = entries[2][None, :] * apart_x * apart_x + 2.0 * entries[3][None, :] * apart_x * apart_y + entries[4][None, :] * apart_y * apart_y
    alpha = entries[5][None, :] * jnp.exp(-0.5 * quad) * valid[None, :]
    keeping = jnp.log1p(-alpha)
    weight = alpha * jnp.exp(jnp.cumsum(keeping, axis=1) - keeping)
    feats = entries[6:11]
    return lax.dot_general(feats, weight, (((1,), (1,)), ((), ())), precision=lax.Precision.HIGHEST)

def adam_update(params, adam_m, adam_v, grad, visible):
    moment_one = beta_one * adam_m + (1.0 - beta_one) * grad
    moment_two = beta_two * adam_v + (1.0 - beta_two) * grad * grad
    first_hat = moment_one / (1.0 - beta_one ** adam_step)
    second_hat = moment_two / (1.0 - beta_two ** adam_step)
    stepped = params - learn_rate * first_hat / (jnp.sqrt(second_hat) + adam_eps)
    keep = (visible > 0)[None, :]
    return (jnp.where(keep, stepped, params), jnp.where(keep, moment_one, adam_m), jnp.where(keep, moment_two, adam_v))

def reference(params, adam_m, adam_v, visible, cameras, send_index, send_count, tile_lists, tile_pos, target):
    center_y = 8.0 * TILES_VIEW / 64.0
    owner = jnp.arange(TILES_VIEW, dtype=jnp.int32) // TILE_DEV

    def render(gauss):
        images = []
        for view in range(NVIEW):
            records = project(gauss, cameras[view], center_y)
            lists = tile_lists[view]
            live = lists >= 0
            clipped = jnp.maximum(lists, 0).astype(jnp.int32)
            source = clipped // CAP
            slot = clipped % CAP
            limit = send_count[view][source, owner[:, None]]
            valid = live & (slot < limit)
            local = send_index[view][source, owner[:, None] * CAP + slot]
            global_ids = (source * G_DEV + local).astype(jnp.int32)

            def one_tile(item):
                gauss_ids, usable, tile = item
                return shade_tile(records[:, gauss_ids], usable.astype(records.dtype), tile)
            tiles = lax.map(jax.checkpoint(one_tile), (global_ids, valid, tile_pos[view]))
            images.append(jnp.transpose(tiles, (1, 0, 2)).reshape(5, PIX))
        return jnp.stack(images)
    image, pullback = jax.vjp(render, params)
    grad, = pullback(image - target)
    new_params, new_m, new_v = adam_update(params, adam_m, adam_v, grad, visible)
    return (image, new_params, new_m, new_v)
```

```python
import functools

import jax
import jax.numpy as jnp
from jax import lax
from jax.experimental import pallas as pl
from jax.experimental.pallas import tpu as pltpu
from jax.sharding import PartitionSpec as P

focal_len = 1000.0
center_x = 512.0
harm_zero = 0.28209479177387814
harm_one = 0.4886025119029199
harm_two = (
    1.0925484305920792,
    -1.0925484305920792,
    0.31539156525252005,
    -1.0925484305920792,
    0.5462742152960396,
)
harm_three = (
    -0.5900435899266435,
    2.890611442640554,
    -0.4570457994644658,
    0.3731763325901154,
    -0.4570457994644658,
    1.445305721320277,
    -0.5900435899266435,
)
beta_one = 0.9
beta_two = 0.99
learn_rate = 0.05
adam_eps = 1e-08
adam_step = 100.0


def project(gauss, camera, center_y):
    rotation = [[camera[3 * i + j] for j in range(3)] for i in range(3)]
    offset = [camera[9 + i] for i in range(3)]
    centre = [gauss[i] for i in range(3)]
    viewed = [sum((rotation[i][j] * centre[j] for j in range(3))) + offset[i] for i in range(3)]
    inverse = 1.0 / viewed[2]
    screen_x = focal_len * viewed[0] * inverse + center_x
    screen_y = focal_len * viewed[1] * inverse + center_y
    scales = [jnp.exp(gauss[3 + i]) for i in range(3)]
    length = jnp.sqrt(
        gauss[6] * gauss[6] + gauss[7] * gauss[7] + gauss[8] * gauss[8] + gauss[9] * gauss[9]
    )
    quat_w, quat_x, quat_y, quat_z = [gauss[6 + i] / length for i in range(4)]
    spin = [
        [
            1.0 - 2.0 * (quat_y * quat_y + quat_z * quat_z),
            2.0 * (quat_x * quat_y - quat_w * quat_z),
            2.0 * (quat_x * quat_z + quat_w * quat_y),
        ],
        [
            2.0 * (quat_x * quat_y + quat_w * quat_z),
            1.0 - 2.0 * (quat_x * quat_x + quat_z * quat_z),
            2.0 * (quat_y * quat_z - quat_w * quat_x),
        ],
        [
            2.0 * (quat_x * quat_z - quat_w * quat_y),
            2.0 * (quat_y * quat_z + quat_w * quat_x),
            1.0 - 2.0 * (quat_x * quat_x + quat_y * quat_y),
        ],
    ]
    factor = [[spin[i][j] * scales[j] for j in range(3)] for i in range(3)]
    sigma = [
        [sum((factor[i][j] * factor[k][j] for j in range(3))) for k in range(3)] for i in range(3)
    ]
    near = focal_len * inverse
    lean_x = -focal_len * viewed[0] * inverse * inverse
    lean_y = -focal_len * viewed[1] * inverse * inverse
    jacob = [
        [near * rotation[0][j] + lean_x * rotation[2][j] for j in range(3)],
        [near * rotation[1][j] + lean_y * rotation[2][j] for j in range(3)],
    ]
    halfway = [
        [sum((jacob[a][i] * sigma[i][k] for i in range(3))) for k in range(3)] for a in range(2)
    ]
    upper = sum((halfway[0][k] * jacob[0][k] for k in range(3))) + 0.3
    middle = sum((halfway[0][k] * jacob[1][k] for k in range(3)))
    lower = sum((halfway[1][k] * jacob[1][k] for k in range(3))) + 0.3
    determinant = upper * lower - middle * middle
    conic_a = lower / determinant
    conic_b = -middle / determinant
    conic_c = upper / determinant
    opacity = jax.nn.sigmoid(gauss[10])
    camera_pos = [-sum((rotation[i][j] * offset[i] for i in range(3))) for j in range(3)]
    toward = [centre[j] - camera_pos[j] for j in range(3)]
    reach = jnp.sqrt(toward[0] * toward[0] + toward[1] * toward[1] + toward[2] * toward[2])
    unit_x = toward[0] / reach
    unit_y = toward[1] / reach
    unit_z = toward[2] / reach
    square_x = unit_x * unit_x
    square_y = unit_y * unit_y
    square_z = unit_z * unit_z
    basis = [
        harm_zero + 0.0 * unit_x,
        -harm_one * unit_y,
        harm_one * unit_z,
        -harm_one * unit_x,
        harm_two[0] * unit_x * unit_y,
        harm_two[1] * unit_y * unit_z,
        harm_two[2] * (2.0 * square_z - square_x - square_y),
        harm_two[3] * unit_x * unit_z,
        harm_two[4] * (square_x - square_y),
        harm_three[0] * unit_y * (3.0 * square_x - square_y),
        harm_three[1] * unit_x * unit_y * unit_z,
        harm_three[2] * unit_y * (4.0 * square_z - square_x - square_y),
        harm_three[3] * unit_z * (2.0 * square_z - 3.0 * square_x - 3.0 * square_y),
        harm_three[4] * unit_x * (4.0 * square_z - square_x - square_y),
        harm_three[5] * unit_z * (square_x - square_y),
        harm_three[6] * unit_x * (square_x - 3.0 * square_y),
    ]
    colors = [0.5 + sum((basis[k] * gauss[11 + 16 * c + k] for k in range(16))) for c in range(3)]
    return jnp.stack(
        [
            screen_x,
            screen_y,
            conic_a,
            conic_b,
            conic_c,
            opacity,
            colors[0],
            colors[1],
            colors[2],
            viewed[2],
            inverse,
        ]
    )


def shade_tile(entries, valid, tile):
    lane = jnp.arange(256, dtype=jnp.int32)
    column = tile % 64 * 16 + lane % 16
    height = tile // 64 * 16 + lane // 16
    pixel_x = column.astype(entries.dtype) + 0.5
    pixel_y = height.astype(entries.dtype) + 0.5
    apart_x = pixel_x[:, None] - entries[0][None, :]
    apart_y = pixel_y[:, None] - entries[1][None, :]
    quad = (
        entries[2][None, :] * apart_x * apart_x
        + 2.0 * entries[3][None, :] * apart_x * apart_y
        + entries[4][None, :] * apart_y * apart_y
    )
    alpha = entries[5][None, :] * jnp.exp(-0.5 * quad) * valid[None, :]
    keeping = jnp.log1p(-alpha)
    weight = alpha * jnp.exp(jnp.cumsum(keeping, axis=1) - keeping)
    feats = entries[6:11]
    return lax.dot_general(feats, weight, (((1,), (1,)), ((), ())), precision=lax.Precision.HIGHEST)


def adam_update(params, adam_m, adam_v, grad, visible):
    moment_one = beta_one * adam_m + (1.0 - beta_one) * grad
    moment_two = beta_two * adam_v + (1.0 - beta_two) * grad * grad
    first_hat = moment_one / (1.0 - beta_one**adam_step)
    second_hat = moment_two / (1.0 - beta_two**adam_step)
    stepped = params - learn_rate * first_hat / (jnp.sqrt(second_hat) + adam_eps)
    keep = (visible > 0)[None, :]
    return (
        jnp.where(keep, stepped, params),
        jnp.where(keep, moment_one, adam_m),
        jnp.where(keep, moment_two, adam_v),
    )


def composite(buffer, block_entries, block_usable, block_places):

    def one_block(item):
        entries, usable, places = item
        return jax.vmap(shade_tile, in_axes=(1, 0, 0))(buffer[:, entries], usable, places)

    return lax.map(jax.checkpoint(one_block), (block_entries, block_usable, block_places))


def plain_body(
    params, adam_m, adam_v, visible, cameras, send_index, send_count, tile_lists, tile_pos, target
):
    shards = lax.axis_size("space")
    tile_count = tile_lists.shape[1]
    list_width = tile_lists.shape[2]
    center_y = 8.0 * (tile_count * shards) / 64.0
    camera = cameras[0]
    route = send_index[0, 0]
    slot_width = route.shape[0] // shards
    slot_grid = jnp.arange(route.shape[0], dtype=jnp.int32).reshape(shards, slot_width) % slot_width
    in_use = (slot_grid < send_count[0, 0][:, None]).reshape(-1).astype(jnp.float32)

    def outgoing(gauss):
        return project(gauss, camera, center_y)[:, route] * in_use[None, :]

    sending, pull_send = jax.vjp(outgoing, params)
    arrived = lax.all_to_all(sending, "space", split_axis=1, concat_axis=1, tiled=True)
    per_block = 2
    block_count = tile_count // per_block
    lists = tile_lists[0]
    block_usable = (lists >= 0).astype(jnp.float32).reshape(block_count, per_block, list_width)
    block_entries = jnp.maximum(lists, 0).reshape(block_count, per_block, list_width)
    block_places = tile_pos[0].reshape(block_count, per_block)

    def draw_tiles(buffer):
        return composite(buffer, block_entries, block_usable, block_places).reshape(
            tile_count, 5, 256
        )

    tiles, pull_tiles = jax.vjp(draw_tiles, arrived)
    image = jnp.transpose(tiles, (1, 0, 2)).reshape(5, tile_count * 256)
    residue = (image - target[0]).reshape(5, tile_count, 256)
    (record_grad,) = pull_tiles(jnp.transpose(residue, (1, 0, 2)))
    returned = lax.all_to_all(record_grad, "space", split_axis=1, concat_axis=1, tiled=True)
    (grad,) = pull_send(returned)
    total = lax.psum(grad, "view")
    new_params, new_m, new_v = adam_update(params, adam_m, adam_v, total, visible)
    return (image[None], new_params, new_m, new_v)


f32 = jnp.float32
bf16 = jnp.bfloat16
MESH_ID = pl.DeviceIdType.MESH


def harmonics(unit_x, unit_y, unit_z):
    square_x = unit_x * unit_x
    square_y = unit_y * unit_y
    square_z = unit_z * unit_z
    return [
        jnp.full_like(unit_x, harm_zero),
        -harm_one * unit_y,
        harm_one * unit_z,
        -harm_one * unit_x,
        harm_two[0] * unit_x * unit_y,
        harm_two[1] * unit_y * unit_z,
        harm_two[2] * (2.0 * square_z - square_x - square_y),
        harm_two[3] * unit_x * unit_z,
        harm_two[4] * (square_x - square_y),
        harm_three[0] * unit_y * (3.0 * square_x - square_y),
        harm_three[1] * unit_x * unit_y * unit_z,
        harm_three[2] * unit_y * (4.0 * square_z - square_x - square_y),
        harm_three[3] * unit_z * (2.0 * square_z - 3.0 * square_x - 3.0 * square_y),
        harm_three[4] * unit_x * (4.0 * square_z - square_x - square_y),
        harm_three[5] * unit_z * (square_x - square_y),
        harm_three[6] * unit_x * (square_x - 3.0 * square_y),
    ]


def camera_centre(camera):
    return [-sum(camera[3 * i + j] * camera[9 + i] for i in range(3)) for j in range(3)]


def geometry(gauss, camera, center_y):
    rotation = [[camera[3 * i + j] for j in range(3)] for i in range(3)]
    offset = [camera[9 + i] for i in range(3)]
    centre = gauss[0:3]
    viewed = [sum(rotation[i][j] * centre[j] for j in range(3)) + offset[i] for i in range(3)]
    inverse = 1.0 / viewed[2]
    near = focal_len * inverse
    ratio_x = viewed[0] * inverse
    ratio_y = viewed[1] * inverse
    screen_x = focal_len * ratio_x + center_x
    screen_y = focal_len * ratio_y + center_y
    scales = [jnp.exp(2.0 * gauss[3 + i]) for i in range(3)]
    squares = [gauss[6 + i] * gauss[6 + i] for i in range(4)]
    double = 2.0 / (squares[0] + squares[1] + squares[2] + squares[3])
    qw, qx, qy, qz = gauss[6:10]
    dx, dy, dz = double * qx, double * qy, double * qz
    xx, yy, zz = dx * qx, dy * qy, dz * qz
    xy, xz, yz = dx * qy, dx * qz, dy * qz
    wx, wy, wz = dx * qw, dy * qw, dz * qw
    spin = [
        [1.0 - (yy + zz), xy - wz, xz + wy],
        [xy + wz, 1.0 - (xx + zz), yz - wx],
        [xz - wy, yz + wx, 1.0 - (xx + yy)],
    ]
    jacob = [
        [near * (rotation[0][j] - ratio_x * rotation[2][j]) for j in range(3)],
        [near * (rotation[1][j] - ratio_y * rotation[2][j]) for j in range(3)],
    ]
    turned = [[sum(jacob[a][i] * spin[i][k] for i in range(3)) for k in range(3)] for a in range(2)]
    scaled = [turned[0][k] * scales[k] for k in range(3)]
    upper = sum(scaled[k] * turned[0][k] for k in range(3)) + 0.3
    middle = sum(scaled[k] * turned[1][k] for k in range(3))
    lower = sum(turned[1][k] * scales[k] * turned[1][k] for k in range(3)) + 0.3
    over = 1.0 / (upper * lower - middle * middle)
    position = camera_centre(camera)
    toward = [centre[j] - position[j] for j in range(3)]
    reach = 1.0 / jnp.sqrt(toward[0] * toward[0] + toward[1] * toward[1] + toward[2] * toward[2])
    basis = harmonics(toward[0] * reach, toward[1] * reach, toward[2] * reach)
    return (
        screen_x,
        screen_y,
        lower * over,
        -middle * over,
        upper * over,
        viewed[2],
        inverse,
    ), basis


def halves(x):
    high = x.astype(bf16).astype(f32)
    return high, x - high


def thirds(x):
    high, rest = halves(x)
    mid, low = halves(rest)
    return jnp.concatenate([high, mid, low], axis=0).astype(bf16)


def two(x):
    high = x.astype(bf16)
    return high, (x - high.astype(f32)).astype(bf16)


def mm(a, b):
    return jnp.dot(a, b, preferred_element_type=f32)


def mm_nt(a, b):
    return lax.dot_general(a, b, (((1,), (1,)), ((), ())), preferred_element_type=f32)


def mm_tn(a, b):
    return lax.dot_general(a, b, (((0,), (0,)), ((), ())), preferred_element_type=f32)


def fold(x, count):
    rows = x.shape[0] // count
    return sum(x[rows * i : rows * (i + 1)] for i in range(count))


def pack(rows, box, shards):
    lane = lax.broadcasted_iota(jnp.int32, (8, 128), 1)
    for j in range(shards // 2):
        first = rows[0:8, 128 * j : 128 * j + 128]
        second = rows[8:16, 128 * j : 128 * j + 128]
        box[2 * j] = jnp.where(lane < 64, first, pltpu.roll(second, 64, 1))
        box[2 * j + 1] = jnp.where(lane < 64, pltpu.roll(first, 64, 1), second)


def unpack(box, shards):
    lane = lax.broadcasted_iota(jnp.int32, (8, 128), 1)
    top, bottom = [], []
    for j in range(shards // 2):
        even, odd = box[2 * j], box[2 * j + 1]
        top.append(jnp.where(lane < 64, even, pltpu.roll(odd, 64, 1)))
        bottom.append(jnp.where(lane < 64, pltpu.roll(even, 64, 1), odd))
    return jnp.concatenate([jnp.concatenate(top, 1), jnp.concatenate(bottom, 1)], 0)


def step_kernel(
    shards,
    views,
    center_y,
    params_ref,
    camera_ref,
    index_ref,
    count_ref,
    lists_ref,
    place_ref,
    target_ref,
    image_ref,
    total_ref,
    wide,
    picked,
    rows,
    out_box,
    in_box,
    back_box,
    home_box,
    shared,
    pick_ref,
    list_hot,
    tri_ref,
    send_sem,
    recv_sem,
    send_back,
    recv_back,
    send_view,
    recv_view,
):
    me_view = lax.axis_index("view")
    me = lax.axis_index("space")
    slots = index_ref.shape[2]
    owned = params_ref.shape[1]
    tiles = lists_ref.shape[1]
    width = lists_ref.shape[2]
    slot_width = slots // shards

    barrier = pltpu.get_barrier_semaphore()
    for r in range(1, shards):
        pl.semaphore_signal(
            barrier, inc=1, device_id=(me_view, lax.rem(me + r, shards)), device_id_type=MESH_ID
        )
    for r in range(1, views):
        pl.semaphore_signal(
            barrier, inc=1, device_id=(lax.rem(me_view + r, views), me), device_id_type=MESH_ID
        )

    wide[56:64] = jnp.zeros((8, owned), f32)
    wide[0:59] = params_ref[...]
    local = lax.broadcasted_iota(jnp.int32, (owned, slots), 0)
    pick_ref[...] = jnp.where(local == index_ref[0], 1.0, 0.0).astype(bf16)
    picked[...] = fold(mm(thirds(wide[...]), pick_ref[...]), 3)

    camera = [camera_ref[0, i] for i in range(12)]
    gauss = [picked[i : i + 1] for i in range(10)]

    def project_rows(values):
        outs, basis = geometry(values, camera, center_y)
        return outs, jnp.concatenate(basis, axis=0)

    (outs, basis), pull = jax.vjp(project_rows, gauss)
    opacity = 1.0 / (1.0 + jnp.exp(-picked[10:11]))
    rows[...] = jnp.zeros_like(rows)
    for i in range(5):
        rows[i : i + 1] = outs[i]
    rows[5:6] = opacity
    for c in range(3):
        rows[8 + c : 9 + c] = 0.5 + jnp.sum(
            basis * picked[11 + 16 * c : 27 + 16 * c], axis=0, keepdims=True
        )
    rows[11:12] = outs[5]
    rows[12:13] = outs[6]
    pack(rows, out_box, shards)

    pl.semaphore_wait(barrier, shards + views - 2)

    def swap(source, landing, sends, recvs):
        copies = []
        for r in range(1, shards):
            to = lax.rem(me + r, shards)
            copy = pltpu.make_async_remote_copy(
                src_ref=source.at[to],
                dst_ref=landing.at[me],
                send_sem=sends.at[r - 1],
                recv_sem=recvs.at[r - 1],
                device_id=(me_view, to),
                device_id_type=MESH_ID,
            )
            copy.start()
            copies.append(copy)
        landing[pl.ds(me, 1)] = source[pl.ds(me, 1)]
        return copies

    copies = swap(out_box, in_box, send_sem, recv_sem)

    entry_row = lax.broadcasted_iota(jnp.int32, (slots, width), 0)
    for t in range(tiles):
        list_hot[t] = jnp.where(entry_row == lists_ref[0, t : t + 1], 1.0, 0.0).astype(bf16)
    first = lax.broadcasted_iota(jnp.int32, (width, width), 0)
    second = lax.broadcasted_iota(jnp.int32, (width, width), 1)
    tri_ref[0] = jnp.where(first < second, 1.0, 0.0).astype(bf16)
    tri_ref[1] = jnp.where(first > second, 1.0, 0.0).astype(bf16)
    pixel = lax.broadcasted_iota(jnp.int32, (16, 256), 1)
    kind = lax.broadcasted_iota(jnp.int32, (16, 256), 0)
    grid_x = (pixel % 16).astype(f32) - 7.5
    grid_y = (pixel // 16).astype(f32) - 7.5
    moments_of = jnp.where(kind == 0, 1.0, 0.0)
    for i, values in enumerate(
        [grid_x, grid_y, grid_x * grid_x, grid_x * grid_y, grid_y * grid_y]
    ):
        moments_of = jnp.where(kind == i + 1, values, moments_of)
    moments_of = moments_of.astype(bf16)
    side_x = lax.broadcasted_iota(jnp.int32, (1, 16, 1), 1).astype(f32) - 7.5
    side_y = lax.broadcasted_iota(jnp.int32, (16, 1, 1), 0).astype(f32) - 7.5

    for copy in copies:
        copy.wait()
    arrived = thirds(unpack(in_box, shards))

    returning = jnp.zeros((16, slots), f32)
    for t in range(tiles):
        entries = fold(mm(arrived, list_hot[t]), 3)
        place = place_ref[0, t]
        middle_x = (place % 64 * 16 + 8).astype(f32)
        middle_y = (place // 64 * 16 + 8).astype(f32)
        u = entries[0:1] - middle_x
        y = entries[1:2] - middle_y
        a, b, c = entries[2:3], entries[3:4], entries[4:5]
        feats = entries[8:16]
        apart_x = side_x - u[None]
        apart_y = side_y - y[None]
        quad = (-0.5 * a)[None] * apart_x * apart_x
        quad = quad + (-b[None] * apart_y) * apart_x + (-0.5 * c)[None] * apart_y * apart_y
        alpha = entries[5:6] * jnp.exp(quad.reshape(256, width))
        keeping = jnp.log(1.0 - alpha)
        keep_high, keep_low = two(keeping)
        logged = mm(keep_high, tri_ref[0]) + mm(keep_low, tri_ref[0])
        weight = alpha * jnp.exp(logged)
        weight_high, weight_low = two(weight)
        feat_high, feat_low = halves(feats)
        feat_two = jnp.concatenate([feat_high, feat_low], 0).astype(bf16)
        drawn = fold(mm_nt(feat_two, weight_high) + mm_nt(feat_two, weight_low), 2)
        image_ref[0, :, 256 * t : 256 * t + 256] = drawn[0:5]
        shown = jnp.concatenate(
            [target_ref[0, :, 256 * t : 256 * t + 256], jnp.zeros((3, 256), f32)], 0
        )
        residue = drawn - shown
        res_high, res_low = halves(residue)
        res_two = jnp.concatenate([res_high, res_low], 0)
        pull_weight = mm_tn(
            jnp.concatenate([res_two, res_two], 0).astype(bf16),
            jnp.concatenate([feat_high, feat_high, feat_low, feat_low], 0).astype(bf16),
        )
        part = weight * pull_weight
        part_high, part_low = two(part)
        behind = mm(part_high, tri_ref[1]) + mm(part_low, tri_ref[1])
        slope = part - behind * (alpha * jnp.exp(-keeping))
        slope_high, slope_low = two(slope)
        moments = mm(moments_of, slope_high) + mm(moments_of, slope_low)
        res_two = res_two.astype(bf16)
        feat_grad = fold(mm(res_two, weight_high) + mm(res_two, weight_low), 2)
        m, mx, my, mxx, mxy, myy = [moments[i : i + 1] for i in range(6)]
        sx = mx - u * m
        sy = my - y * m
        sxx = mxx - u * mx - u * sx
        sxy = mxy - u * my - y * sx
        syy = myy - y * my - y * sy
        zero = jnp.zeros((2, width), f32)
        entry_grad = jnp.concatenate(
            [a * sx + b * sy, b * sx + c * sy, -0.5 * sxx, -sxy, -0.5 * syy, m, zero, feat_grad], 0
        )
        returning = returning + fold(mm_nt(thirds(entry_grad), list_hot[t]), 3)

    rows[...] = returning
    pack(rows, back_box, shards)
    copies = swap(back_box, home_box, send_back, recv_back)
    lane = lax.broadcasted_iota(jnp.int32, (1, slots), 1)
    used = jnp.zeros((1, slots), f32)
    for d in range(shards):
        begin = slot_width * d
        inside = (lane >= begin) & (lane < begin + count_ref[0, 0, d])
        used = jnp.where(inside, 1.0, used)
    for copy in copies:
        copy.wait()

    rows[...] = unpack(home_box, shards)
    spread = sum(
        picked[11 + 16 * c : 27 + 16 * c] * rows[8 + c : 9 + c] for c in range(3)
    )
    cotangents = tuple(rows[i : i + 1] for i in range(5)) + (rows[11:12], rows[12:13])
    (gauss_grad,) = pull((cotangents, spread))
    logit_grad = rows[5:6] * (1.0 - opacity)
    colour_grad = rows[8:11]
    for i in range(10):
        rows[i : i + 1] = gauss_grad[i]
    rows[10:11] = logit_grad
    rows[11:14] = colour_grad
    rows[14:15] = used
    rows[15:16] = jnp.zeros((1, slots), f32)
    own = fold(mm_nt(thirds(rows[...]), pick_ref[...]), 3)
    position = camera_centre(camera)
    far = lax.broadcasted_iota(jnp.int32, (1, owned), 1)
    last = jnp.where(far == 0, position[0], jnp.where(far == 1, position[1], position[2]))
    shared[pl.ds(me_view, 1)] = jnp.concatenate([own[0:15], last], 0)[None]
    copies = []
    for r in range(1, views):
        copy = pltpu.make_async_remote_copy(
            src_ref=shared.at[me_view],
            dst_ref=shared.at[me_view],
            send_sem=send_view.at[r - 1],
            recv_sem=recv_view.at[r - 1],
            device_id=(lax.rem(me_view + r, views), me),
            device_id_type=MESH_ID,
        )
        copy.start()
        copies.append(copy)
    for copy in copies:
        copy.wait()
    total_ref[0:16] = sum(shared[w] for w in range(views))
    for j in range(3):
        total_ref[15 + j : 16 + j] = sum(
            shared[w, 14:15] * shared[w, 15:16, j : j + 1] for w in range(views)
        )
    total_ref[18:24] = jnp.zeros((6, owned), f32)


def update_kernel(
    params_ref,
    first_ref,
    second_ref,
    visible_ref,
    total_ref,
    drawn_ref,
    image_ref,
    out_params,
    out_first,
    out_second,
    grad,
):
    image_ref[...] = drawn_ref[...]
    seen = total_ref[14:15] > 0.0
    toward = [params_ref[j : j + 1] - total_ref[15 + j : 16 + j] for j in range(3)]
    square = toward[0] * toward[0] + toward[1] * toward[1] + toward[2] * toward[2]
    reach = 1.0 / jnp.sqrt(jnp.where(seen, square, 1.0))
    basis = jnp.concatenate(harmonics(toward[0] * reach, toward[1] * reach, toward[2] * reach), 0)
    basis = jnp.where(seen, basis, 0.0)
    grad[0:11] = total_ref[0:11]
    for c in range(3):
        grad[11 + 16 * c : 27 + 16 * c] = basis * total_ref[11 + c : 12 + c]
    values = grad[0:59]
    params, adam_m, adam_v = params_ref[...], first_ref[...], second_ref[...]
    moment_one = beta_one * adam_m + (1.0 - beta_one) * values
    moment_two = beta_two * adam_v + (1.0 - beta_two) * values * values
    scale_one = learn_rate / (1.0 - beta_one**adam_step)
    scale_two = 1.0 / (1.0 - beta_two**adam_step)
    stepped = params - scale_one * moment_one / (jnp.sqrt(moment_two * scale_two) + adam_eps)
    keep = visible_ref[...] > 0
    out_params[...] = jnp.where(keep, stepped, params)
    out_first[...] = jnp.where(keep, moment_one, adam_m)
    out_second[...] = jnp.where(keep, moment_two, adam_v)


def body(
    params, adam_m, adam_v, visible, cameras, send_index, send_count, tile_lists, tile_pos, target
):
    shards = lax.axis_size("space")
    views = lax.axis_size("view")
    tiles, width = tile_lists.shape[1:]
    slots = send_index.shape[2]
    nparam, owned = params.shape
    if slots != 64 * shards or shards % 2 or nparam != 59:
        return plain_body(
            params,
            adam_m,
            adam_v,
            visible,
            cameras,
            send_index,
            send_count,
            tile_lists,
            tile_pos,
            target,
        )
    center_y = 8.0 * (tiles * shards) / 64.0
    vmem = pl.BlockSpec(memory_space=pltpu.VMEM)
    smem = pl.BlockSpec(memory_space=pltpu.SMEM)
    box = pltpu.VMEM((shards, 8, 128), f32)
    image, total = pl.pallas_call(
        functools.partial(step_kernel, shards, views, center_y),
        out_shape=(
            jax.ShapeDtypeStruct(target.shape, f32),
            jax.ShapeDtypeStruct((24, owned), f32),
        ),
        in_specs=[vmem, smem, vmem, smem, vmem, smem, vmem],
        out_specs=(vmem, vmem),
        scratch_shapes=[
            pltpu.VMEM((64, owned), f32),
            pltpu.VMEM((64, slots), f32),
            pltpu.VMEM((16, slots), f32),
            box,
            box,
            box,
            box,
            pltpu.VMEM((views, 16, owned), f32),
            pltpu.VMEM((owned, slots), bf16),
            pltpu.VMEM((tiles, slots, width), bf16),
            pltpu.VMEM((2, width, width), bf16),
            pltpu.SemaphoreType.DMA((shards - 1,)),
            pltpu.SemaphoreType.DMA((shards - 1,)),
            pltpu.SemaphoreType.DMA((shards - 1,)),
            pltpu.SemaphoreType.DMA((shards - 1,)),
            pltpu.SemaphoreType.DMA((views - 1,)),
            pltpu.SemaphoreType.DMA((views - 1,)),
        ],
        compiler_params=pltpu.CompilerParams(
            collective_id=0, has_side_effects=True, vmem_limit_bytes=40 * 1024 * 1024
        ),
        name="step",
    )(params, cameras, send_index, send_count, tile_lists, tile_pos, target)
    like = jax.ShapeDtypeStruct(params.shape, f32)
    return pl.pallas_call(
        update_kernel,
        out_shape=(jax.ShapeDtypeStruct(target.shape, f32), like, like, like),
        in_specs=[vmem] * 6,
        out_specs=(vmem,) * 4,
        scratch_shapes=[pltpu.VMEM((64, owned), f32)],
        compiler_params=pltpu.CompilerParams(vmem_limit_bytes=16 * 1024 * 1024),
        name="update",
    )(params, adam_m, adam_v, visible.reshape(1, owned), total, image)


def solution(mesh):
    placed = (
        P(None, "space"),
        P(None, "space"),
        P(None, "space"),
        P("space"),
        P("view", None),
        P("view", "space", None),
        P("view", "space", None),
        P("view", "space", None),
        P("view", "space"),
        P("view", None, "space"),
    )
    return jax.shard_map(
        body,
        mesh=mesh,
        in_specs=placed,
        out_specs=(P("view", None, "space"), P(None, "space"), P(None, "space"), P(None, "space")),
        check_vma=False,
    )
```

```python
import functools

import jax
import jax.numpy as jnp
from jax import lax
from jax.experimental import pallas as pl
from jax.experimental.pallas import tpu as pltpu
from jax.sharding import PartitionSpec as P

focal_len = 1000.0
center_x = 512.0
harm_zero = 0.28209479177387814
harm_one = 0.4886025119029199
harm_two = (
    1.0925484305920792,
    -1.0925484305920792,
    0.31539156525252005,
    -1.0925484305920792,
    0.5462742152960396,
)
harm_three = (
    -0.5900435899266435,
    2.890611442640554,
    -0.4570457994644658,
    0.3731763325901154,
    -0.4570457994644658,
    1.445305721320277,
    -0.5900435899266435,
)
beta_one = 0.9
beta_two = 0.99
learn_rate = 0.05
adam_eps = 1e-08
adam_step = 100.0


def project(gauss, camera, center_y):
    rotation = [[camera[3 * i + j] for j in range(3)] for i in range(3)]
    offset = [camera[9 + i] for i in range(3)]
    centre = [gauss[i] for i in range(3)]
    viewed = [sum((rotation[i][j] * centre[j] for j in range(3))) + offset[i] for i in range(3)]
    inverse = 1.0 / viewed[2]
    screen_x = focal_len * viewed[0] * inverse + center_x
    screen_y = focal_len * viewed[1] * inverse + center_y
    scales = [jnp.exp(gauss[3 + i]) for i in range(3)]
    length = jnp.sqrt(
        gauss[6] * gauss[6] + gauss[7] * gauss[7] + gauss[8] * gauss[8] + gauss[9] * gauss[9]
    )
    quat_w, quat_x, quat_y, quat_z = [gauss[6 + i] / length for i in range(4)]
    spin = [
        [
            1.0 - 2.0 * (quat_y * quat_y + quat_z * quat_z),
            2.0 * (quat_x * quat_y - quat_w * quat_z),
            2.0 * (quat_x * quat_z + quat_w * quat_y),
        ],
        [
            2.0 * (quat_x * quat_y + quat_w * quat_z),
            1.0 - 2.0 * (quat_x * quat_x + quat_z * quat_z),
            2.0 * (quat_y * quat_z - quat_w * quat_x),
        ],
        [
            2.0 * (quat_x * quat_z - quat_w * quat_y),
            2.0 * (quat_y * quat_z + quat_w * quat_x),
            1.0 - 2.0 * (quat_x * quat_x + quat_y * quat_y),
        ],
    ]
    factor = [[spin[i][j] * scales[j] for j in range(3)] for i in range(3)]
    sigma = [
        [sum((factor[i][j] * factor[k][j] for j in range(3))) for k in range(3)] for i in range(3)
    ]
    near = focal_len * inverse
    lean_x = -focal_len * viewed[0] * inverse * inverse
    lean_y = -focal_len * viewed[1] * inverse * inverse
    jacob = [
        [near * rotation[0][j] + lean_x * rotation[2][j] for j in range(3)],
        [near * rotation[1][j] + lean_y * rotation[2][j] for j in range(3)],
    ]
    halfway = [
        [sum((jacob[a][i] * sigma[i][k] for i in range(3))) for k in range(3)] for a in range(2)
    ]
    upper = sum((halfway[0][k] * jacob[0][k] for k in range(3))) + 0.3
    middle = sum((halfway[0][k] * jacob[1][k] for k in range(3)))
    lower = sum((halfway[1][k] * jacob[1][k] for k in range(3))) + 0.3
    determinant = upper * lower - middle * middle
    conic_a = lower / determinant
    conic_b = -middle / determinant
    conic_c = upper / determinant
    opacity = jax.nn.sigmoid(gauss[10])
    camera_pos = [-sum((rotation[i][j] * offset[i] for i in range(3))) for j in range(3)]
    toward = [centre[j] - camera_pos[j] for j in range(3)]
    reach = jnp.sqrt(toward[0] * toward[0] + toward[1] * toward[1] + toward[2] * toward[2])
    unit_x = toward[0] / reach
    unit_y = toward[1] / reach
    unit_z = toward[2] / reach
    square_x = unit_x * unit_x
    square_y = unit_y * unit_y
    square_z = unit_z * unit_z
    basis = [
        harm_zero + 0.0 * unit_x,
        -harm_one * unit_y,
        harm_one * unit_z,
        -harm_one * unit_x,
        harm_two[0] * unit_x * unit_y,
        harm_two[1] * unit_y * unit_z,
        harm_two[2] * (2.0 * square_z - square_x - square_y),
        harm_two[3] * unit_x * unit_z,
        harm_two[4] * (square_x - square_y),
        harm_three[0] * unit_y * (3.0 * square_x - square_y),
        harm_three[1] * unit_x * unit_y * unit_z,
        harm_three[2] * unit_y * (4.0 * square_z - square_x - square_y),
        harm_three[3] * unit_z * (2.0 * square_z - 3.0 * square_x - 3.0 * square_y),
        harm_three[4] * unit_x * (4.0 * square_z - square_x - square_y),
        harm_three[5] * unit_z * (square_x - square_y),
        harm_three[6] * unit_x * (square_x - 3.0 * square_y),
    ]
    colors = [0.5 + sum((basis[k] * gauss[11 + 16 * c + k] for k in range(16))) for c in range(3)]
    return jnp.stack(
        [
            screen_x,
            screen_y,
            conic_a,
            conic_b,
            conic_c,
            opacity,
            colors[0],
            colors[1],
            colors[2],
            viewed[2],
            inverse,
        ]
    )


def shade_tile(entries, valid, tile):
    lane = jnp.arange(256, dtype=jnp.int32)
    column = tile % 64 * 16 + lane % 16
    height = tile // 64 * 16 + lane // 16
    pixel_x = column.astype(entries.dtype) + 0.5
    pixel_y = height.astype(entries.dtype) + 0.5
    apart_x = pixel_x[:, None] - entries[0][None, :]
    apart_y = pixel_y[:, None] - entries[1][None, :]
    quad = (
        entries[2][None, :] * apart_x * apart_x
        + 2.0 * entries[3][None, :] * apart_x * apart_y
        + entries[4][None, :] * apart_y * apart_y
    )
    alpha = entries[5][None, :] * jnp.exp(-0.5 * quad) * valid[None, :]
    keeping = jnp.log1p(-alpha)
    weight = alpha * jnp.exp(jnp.cumsum(keeping, axis=1) - keeping)
    feats = entries[6:11]
    return lax.dot_general(feats, weight, (((1,), (1,)), ((), ())), precision=lax.Precision.HIGHEST)


def adam_update(params, adam_m, adam_v, grad, visible):
    moment_one = beta_one * adam_m + (1.0 - beta_one) * grad
    moment_two = beta_two * adam_v + (1.0 - beta_two) * grad * grad
    first_hat = moment_one / (1.0 - beta_one**adam_step)
    second_hat = moment_two / (1.0 - beta_two**adam_step)
    stepped = params - learn_rate * first_hat / (jnp.sqrt(second_hat) + adam_eps)
    keep = (visible > 0)[None, :]
    return (
        jnp.where(keep, stepped, params),
        jnp.where(keep, moment_one, adam_m),
        jnp.where(keep, moment_two, adam_v),
    )


def composite(buffer, block_entries, block_usable, block_places):

    def one_block(item):
        entries, usable, places = item
        return jax.vmap(shade_tile, in_axes=(1, 0, 0))(buffer[:, entries], usable, places)

    return lax.map(jax.checkpoint(one_block), (block_entries, block_usable, block_places))


def plain_body(
    params, adam_m, adam_v, visible, cameras, send_index, send_count, tile_lists, tile_pos, target
):
    shards = lax.axis_size("space")
    tile_count = tile_lists.shape[1]
    list_width = tile_lists.shape[2]
    center_y = 8.0 * (tile_count * shards) / 64.0
    camera = cameras[0]
    route = send_index[0, 0]
    slot_width = route.shape[0] // shards
    slot_grid = jnp.arange(route.shape[0], dtype=jnp.int32).reshape(shards, slot_width) % slot_width
    in_use = (slot_grid < send_count[0, 0][:, None]).reshape(-1).astype(jnp.float32)

    def outgoing(gauss):
        return project(gauss, camera, center_y)[:, route] * in_use[None, :]

    sending, pull_send = jax.vjp(outgoing, params)
    arrived = lax.all_to_all(sending, "space", split_axis=1, concat_axis=1, tiled=True)
    per_block = 2
    block_count = tile_count // per_block
    lists = tile_lists[0]
    block_usable = (lists >= 0).astype(jnp.float32).reshape(block_count, per_block, list_width)
    block_entries = jnp.maximum(lists, 0).reshape(block_count, per_block, list_width)
    block_places = tile_pos[0].reshape(block_count, per_block)

    def draw_tiles(buffer):
        return composite(buffer, block_entries, block_usable, block_places).reshape(
            tile_count, 5, 256
        )

    tiles, pull_tiles = jax.vjp(draw_tiles, arrived)
    image = jnp.transpose(tiles, (1, 0, 2)).reshape(5, tile_count * 256)
    residue = (image - target[0]).reshape(5, tile_count, 256)
    (record_grad,) = pull_tiles(jnp.transpose(residue, (1, 0, 2)))
    returned = lax.all_to_all(record_grad, "space", split_axis=1, concat_axis=1, tiled=True)
    (grad,) = pull_send(returned)
    total = lax.psum(grad, "view")
    new_params, new_m, new_v = adam_update(params, adam_m, adam_v, total, visible)
    return (image[None], new_params, new_m, new_v)


f32 = jnp.float32
bf16 = jnp.bfloat16
MESH_ID = pl.DeviceIdType.MESH


def harmonics(unit_x, unit_y, unit_z):
    square_x = unit_x * unit_x
    square_y = unit_y * unit_y
    square_z = unit_z * unit_z
    return [
        jnp.full_like(unit_x, harm_zero),
        -harm_one * unit_y,
        harm_one * unit_z,
        -harm_one * unit_x,
        harm_two[0] * unit_x * unit_y,
        harm_two[1] * unit_y * unit_z,
        harm_two[2] * (2.0 * square_z - square_x - square_y),
        harm_two[3] * unit_x * unit_z,
        harm_two[4] * (square_x - square_y),
        harm_three[0] * unit_y * (3.0 * square_x - square_y),
        harm_three[1] * unit_x * unit_y * unit_z,
        harm_three[2] * unit_y * (4.0 * square_z - square_x - square_y),
        harm_three[3] * unit_z * (2.0 * square_z - 3.0 * square_x - 3.0 * square_y),
        harm_three[4] * unit_x * (4.0 * square_z - square_x - square_y),
        harm_three[5] * unit_z * (square_x - square_y),
        harm_three[6] * unit_x * (square_x - 3.0 * square_y),
    ]


def camera_centre(camera):
    return [-sum(camera[3 * i + j] * camera[9 + i] for i in range(3)) for j in range(3)]


def geometry(gauss, camera, center_y):
    rotation = [[camera[3 * i + j] for j in range(3)] for i in range(3)]
    offset = [camera[9 + i] for i in range(3)]
    centre = gauss[0:3]
    viewed = [sum(rotation[i][j] * centre[j] for j in range(3)) + offset[i] for i in range(3)]
    inverse = 1.0 / viewed[2]
    near = focal_len * inverse
    ratio_x = viewed[0] * inverse
    ratio_y = viewed[1] * inverse
    screen_x = focal_len * ratio_x + center_x
    screen_y = focal_len * ratio_y + center_y
    scales = [jnp.exp(2.0 * gauss[3 + i]) for i in range(3)]
    squares = [gauss[6 + i] * gauss[6 + i] for i in range(4)]
    double = 2.0 / (squares[0] + squares[1] + squares[2] + squares[3])
    qw, qx, qy, qz = gauss[6:10]
    dx, dy, dz = double * qx, double * qy, double * qz
    xx, yy, zz = dx * qx, dy * qy, dz * qz
    xy, xz, yz = dx * qy, dx * qz, dy * qz
    wx, wy, wz = dx * qw, dy * qw, dz * qw
    spin = [
        [1.0 - (yy + zz), xy - wz, xz + wy],
        [xy + wz, 1.0 - (xx + zz), yz - wx],
        [xz - wy, yz + wx, 1.0 - (xx + yy)],
    ]
    jacob = [
        [near * (rotation[0][j] - ratio_x * rotation[2][j]) for j in range(3)],
        [near * (rotation[1][j] - ratio_y * rotation[2][j]) for j in range(3)],
    ]
    turned = [[sum(jacob[a][i] * spin[i][k] for i in range(3)) for k in range(3)] for a in range(2)]
    scaled = [turned[0][k] * scales[k] for k in range(3)]
    upper = sum(scaled[k] * turned[0][k] for k in range(3)) + 0.3
    middle = sum(scaled[k] * turned[1][k] for k in range(3))
    lower = sum(turned[1][k] * scales[k] * turned[1][k] for k in range(3)) + 0.3
    over = 1.0 / (upper * lower - middle * middle)
    position = camera_centre(camera)
    toward = [centre[j] - position[j] for j in range(3)]
    reach = 1.0 / jnp.sqrt(toward[0] * toward[0] + toward[1] * toward[1] + toward[2] * toward[2])
    basis = harmonics(toward[0] * reach, toward[1] * reach, toward[2] * reach)
    return (
        screen_x,
        screen_y,
        lower * over,
        -middle * over,
        upper * over,
        viewed[2],
        inverse,
    ), basis


def halves(x):
    high = x.astype(bf16).astype(f32)
    return high, x - high


def thirds(x):
    high, rest = halves(x)
    mid, low = halves(rest)
    return jnp.concatenate([high, mid, low], axis=0).astype(bf16)


def two(x):
    high = x.astype(bf16)
    return high, (x - high.astype(f32)).astype(bf16)


def mm(a, b):
    return jnp.dot(a, b, preferred_element_type=f32)


def mm_nt(a, b):
    return lax.dot_general(a, b, (((1,), (1,)), ((), ())), preferred_element_type=f32)


def mm_tn(a, b):
    return lax.dot_general(a, b, (((0,), (0,)), ((), ())), preferred_element_type=f32)


def fold(x, count):
    rows = x.shape[0] // count
    return sum(x[rows * i : rows * (i + 1)] for i in range(count))


def pack(rows, box, shards):
    lane = lax.broadcasted_iota(jnp.int32, (8, 128), 1)
    for j in range(shards // 2):
        first = rows[0:8, 128 * j : 128 * j + 128]
        second = rows[8:16, 128 * j : 128 * j + 128]
        box[2 * j] = jnp.where(lane < 64, first, pltpu.roll(second, 64, 1))
        box[2 * j + 1] = jnp.where(lane < 64, pltpu.roll(first, 64, 1), second)


def unpack(box, shards):
    lane = lax.broadcasted_iota(jnp.int32, (8, 128), 1)
    top, bottom = [], []
    for j in range(shards // 2):
        even, odd = box[2 * j], box[2 * j + 1]
        top.append(jnp.where(lane < 64, even, pltpu.roll(odd, 64, 1)))
        bottom.append(jnp.where(lane < 64, pltpu.roll(even, 64, 1), odd))
    return jnp.concatenate([jnp.concatenate(top, 1), jnp.concatenate(bottom, 1)], 0)


def step_kernel(
    shards,
    views,
    center_y,
    params_ref,
    camera_ref,
    index_ref,
    count_ref,
    lists_ref,
    place_ref,
    target_ref,
    image_ref,
    total_ref,
    held,
    wide,
    picked,
    rows,
    out_box,
    in_box,
    back_box,
    home_box,
    shared,
    pick_ref,
    list_hot,
    tri_ref,
    near_ref,
    alpha_ref,
    ratio_ref,
    sum_ref,
    part_high,
    part_low,
    weight_high,
    weight_low,
    load_sem,
    send_sem,
    recv_sem,
    send_back,
    recv_back,
    send_view,
    recv_view,
):
    me_view = lax.axis_index("view")
    me = lax.axis_index("space")
    slots = index_ref.shape[2]
    owned = params_ref.shape[1]
    tiles = lists_ref.shape[1]
    width = lists_ref.shape[2]
    half = width // 2
    slot_width = slots // shards

    load = pltpu.make_async_copy(params_ref, held, load_sem)
    load.start()
    barrier = pltpu.get_barrier_semaphore()
    for r in range(1, shards):
        pl.semaphore_signal(
            barrier, inc=1, device_id=(me_view, lax.rem(me + r, shards)), device_id_type=MESH_ID
        )
    for r in range(1, views):
        pl.semaphore_signal(
            barrier, inc=1, device_id=(lax.rem(me_view + r, views), me), device_id_type=MESH_ID
        )

    count_up = lax.broadcasted_iota(jnp.int32, (32, slots), 0)

    def pick_rows(i, carry):
        at = pl.multiple_of(32 * i, 32)
        pick_ref[pl.ds(at, 32)] = jnp.where(count_up + at == index_ref[0], 1.0, 0.0).astype(bf16)
        return carry

    lax.fori_loop(0, owned // 32, pick_rows, 0)
    wide[56:64] = jnp.zeros((8, owned), f32)
    load.wait()
    wide[0:59] = held[...]
    picked[...] = fold(mm(thirds(wide[...]), pick_ref[...]), 3)

    camera = [camera_ref[0, i] for i in range(12)]
    gauss = [picked[i : i + 1] for i in range(10)]

    def project_rows(values):
        outs, basis = geometry(values, camera, center_y)
        return outs, jnp.concatenate(basis, axis=0)

    (outs, basis), pull = jax.vjp(project_rows, gauss)
    opacity = 1.0 / (1.0 + jnp.exp(-picked[10:11]))
    rows[...] = jnp.zeros_like(rows)
    for i in range(5):
        rows[i : i + 1] = outs[i]
    rows[5:6] = opacity
    for c in range(3):
        rows[8 + c : 9 + c] = 0.5 + jnp.sum(
            basis * picked[11 + 16 * c : 27 + 16 * c], axis=0, keepdims=True
        )
    rows[11:12] = outs[5]
    rows[12:13] = outs[6]
    pack(rows, out_box, shards)

    pl.semaphore_wait(barrier, shards + views - 2)

    def swap(source, landing, sends, recvs):
        copies = []
        for r in range(1, shards):
            to = lax.rem(me + r, shards)
            copy = pltpu.make_async_remote_copy(
                src_ref=source.at[to],
                dst_ref=landing.at[me],
                send_sem=sends.at[r - 1],
                recv_sem=recvs.at[r - 1],
                device_id=(me_view, to),
                device_id_type=MESH_ID,
            )
            copy.start()
            copies.append(copy)
        landing[pl.ds(me, 1)] = source[pl.ds(me, 1)]
        return copies

    copies = swap(out_box, in_box, send_sem, recv_sem)

    def list_rows(i, carry):
        at = pl.multiple_of(32 * i, 32)
        for t in range(tiles):
            list_hot[t, pl.ds(at, 32)] = jnp.where(
                count_up + at == lists_ref[0, t : t + 1], 1.0, 0.0
            ).astype(bf16)
        return carry

    lax.fori_loop(0, slots // 32, list_rows, 0)
    first = lax.broadcasted_iota(jnp.int32, (half, half), 0)
    second = lax.broadcasted_iota(jnp.int32, (half, half), 1)
    tri_ref[0] = jnp.where(first < second, 1.0, 0.0).astype(bf16)
    tri_ref[1] = jnp.where(first > second, 1.0, 0.0).astype(bf16)
    tri_ref[2] = jnp.ones((half, half), bf16)
    pixel = lax.broadcasted_iota(jnp.int32, (16, 256), 1)
    kind = lax.broadcasted_iota(jnp.int32, (16, 256), 0)
    grid_x = (pixel % 16).astype(f32) - 7.5
    grid_y = (pixel // 16).astype(f32) - 7.5
    moments_of = jnp.where(kind == 0, 1.0, 0.0)
    for i, values in enumerate(
        [grid_x, grid_y, grid_x * grid_x, grid_x * grid_y, grid_y * grid_y]
    ):
        moments_of = jnp.where(kind == i + 1, values, moments_of)
    moments_of = moments_of.astype(bf16)
    side_x = lax.broadcasted_iota(jnp.int32, (16, 1), 0).astype(f32) - 7.5

    for copy in copies:
        copy.wait()
    arrived = thirds(unpack(in_box, shards))

    spans = [slice(256 * t, 256 * t + 256) for t in range(tiles)]
    drawn_from = []
    for t in range(tiles):
        entries = fold(mm(arrived, list_hot[t]), 3)
        place = place_ref[0, t]
        middle_x = (place % 64 * 16 + 8).astype(f32)
        middle_y = (place // 64 * 16 + 8).astype(f32)
        u = entries[0:1] - middle_x
        y = entries[1:2] - middle_y
        a, b, c = entries[2:3], entries[3:4], entries[4:5]
        drawn_from.append((u, y, a, b, c, entries[8:16]))
        apart_x = side_x - u
        near_ref[t, 0:16] = apart_x
        near_ref[t, 16:32] = (-0.5 * a) * apart_x * apart_x
        near_ref[t, 32:33] = y
        near_ref[t, 33:34] = -b
        near_ref[t, 34:35] = -0.5 * c
        near_ref[t, 35:36] = entries[5:6]

    def light(i, carry):
        at = pl.multiple_of(16 * i, 16)
        for t in range(tiles):
            apart_y = (i.astype(f32) - 7.5) - near_ref[t, 32:33]
            line = near_ref[t, 33:34] * apart_y
            shift = near_ref[t, 34:35] * apart_y * apart_y
            quad = near_ref[t, 16:32] + line * near_ref[t, 0:16] + shift
            alpha = near_ref[t, 35:36] * jnp.exp(quad)
            through = 1.0 - alpha
            keep_high, keep_low = two(jnp.log(through))
            here = pl.ds(256 * t + at, 16)
            alpha_ref[here] = alpha
            ratio_ref[here] = alpha / through
            part_high[here] = keep_high
            part_low[here] = keep_low
        return carry

    lax.fori_loop(0, 16, light, 0)

    def ordered_sum(order):
        whole, cut = (slice(0, half), slice(half, width))
        if order:
            whole, cut = cut, whole
        sum_ref[:, whole] = mm(part_high[:, whole], tri_ref[order]) + mm(
            part_low[:, whole], tri_ref[order]
        )
        sum_ref[:, cut] = (
            mm(part_high[:, cut], tri_ref[order])
            + mm(part_low[:, cut], tri_ref[order])
            + mm(part_high[:, whole], tri_ref[2])
            + mm(part_low[:, whole], tri_ref[2])
        )

    ordered_sum(0)
    steps = 16 * tiles

    def weigh(i, carry):
        here = pl.ds(pl.multiple_of(16 * i, 16), 16)
        weight = alpha_ref[here] * jnp.exp(sum_ref[here])
        alpha_ref[here] = weight
        weight_high[here], weight_low[here] = two(weight)
        return carry

    lax.fori_loop(0, steps, weigh, 0)

    feat_grads = []
    for t in range(tiles):
        feat_high, feat_low = halves(drawn_from[t][5])
        feat_two = jnp.concatenate([feat_high, feat_low], 0).astype(bf16)
        drawn = fold(
            mm_nt(feat_two, weight_high[spans[t]]) + mm_nt(feat_two, weight_low[spans[t]]), 2
        )
        for ch in range(5):
            image_ref[ch, :, spans[t]] = drawn[ch : ch + 1]
        shown = jnp.concatenate(
            [target_ref[ch, :, spans[t]] for ch in range(5)] + [jnp.zeros((3, 256), f32)], 0
        )
        res_high, res_low = halves(drawn - shown)
        res_two = jnp.concatenate([res_high, res_low], 0)
        sum_ref[spans[t]] = mm_tn(
            jnp.concatenate([res_two, res_two], 0).astype(bf16),
            jnp.concatenate([feat_high, feat_high, feat_low, feat_low], 0).astype(bf16),
        )
        res_two = res_two.astype(bf16)
        feat_grads.append(
            fold(mm(res_two, weight_high[spans[t]]) + mm(res_two, weight_low[spans[t]]), 2)
        )

    def pull_back(i, carry):
        here = pl.ds(pl.multiple_of(16 * i, 16), 16)
        part = alpha_ref[here] * sum_ref[here]
        alpha_ref[here] = part
        part_high[here], part_low[here] = two(part)
        return carry

    lax.fori_loop(0, steps, pull_back, 0)
    ordered_sum(1)

    def slope_of(i, carry):
        here = pl.ds(pl.multiple_of(16 * i, 16), 16)
        part_high[here], part_low[here] = two(alpha_ref[here] - sum_ref[here] * ratio_ref[here])
        return carry

    lax.fori_loop(0, steps, slope_of, 0)

    returning = jnp.zeros((16, slots), f32)
    for t in range(tiles):
        u, y, a, b, c, _ = drawn_from[t]
        moments = mm(moments_of, part_high[spans[t]]) + mm(moments_of, part_low[spans[t]])
        m, mx, my, mxx, mxy, myy = [moments[i : i + 1] for i in range(6)]
        sx = mx - u * m
        sy = my - y * m
        sxx = mxx - u * mx - u * sx
        sxy = mxy - u * my - y * sx
        syy = myy - y * my - y * sy
        zero = jnp.zeros((2, width), f32)
        entry_grad = jnp.concatenate(
            [
                a * sx + b * sy,
                b * sx + c * sy,
                -0.5 * sxx,
                -sxy,
                -0.5 * syy,
                m,
                zero,
                feat_grads[t],
            ],
            0,
        )
        returning = returning + fold(mm_nt(thirds(entry_grad), list_hot[t]), 3)

    rows[...] = returning
    pack(rows, back_box, shards)
    copies = swap(back_box, home_box, send_back, recv_back)
    lane = lax.broadcasted_iota(jnp.int32, (1, slots), 1)
    used = jnp.zeros((1, slots), f32)
    for d in range(shards):
        begin = slot_width * d
        inside = (lane >= begin) & (lane < begin + count_ref[0, 0, d])
        used = jnp.where(inside, 1.0, used)
    for copy in copies:
        copy.wait()

    rows[...] = unpack(home_box, shards)
    spread = sum(
        picked[11 + 16 * c : 27 + 16 * c] * rows[8 + c : 9 + c] for c in range(3)
    )
    cotangents = tuple(rows[i : i + 1] for i in range(5)) + (rows[11:12], rows[12:13])
    (gauss_grad,) = pull((cotangents, spread))
    logit_grad = rows[5:6] * (1.0 - opacity)
    colour_grad = rows[8:11]
    for i in range(10):
        rows[i : i + 1] = gauss_grad[i]
    rows[10:11] = logit_grad
    rows[11:14] = colour_grad
    rows[14:15] = used
    rows[15:16] = jnp.zeros((1, slots), f32)
    own = fold(mm_nt(thirds(rows[...]), pick_ref[...]), 3)
    position = camera_centre(camera)
    far = lax.broadcasted_iota(jnp.int32, (1, owned), 1)
    last = jnp.where(far == 0, position[0], jnp.where(far == 1, position[1], position[2]))
    shared[pl.ds(me_view, 1)] = jnp.concatenate([own[0:15], last], 0)[None]
    copies = []
    for r in range(1, views):
        copy = pltpu.make_async_remote_copy(
            src_ref=shared.at[me_view],
            dst_ref=shared.at[me_view],
            send_sem=send_view.at[r - 1],
            recv_sem=recv_view.at[r - 1],
            device_id=(lax.rem(me_view + r, views), me),
            device_id_type=MESH_ID,
        )
        copy.start()
        copies.append(copy)
    for copy in copies:
        copy.wait()
    total_ref[0:16] = sum(shared[w] for w in range(views))
    for j in range(3):
        total_ref[15 + j : 16 + j] = sum(
            shared[w, 14:15] * shared[w, 15:16, j : j + 1] for w in range(views)
        )
    total_ref[18:24] = jnp.zeros((6, owned), f32)


def update_kernel(
    params_ref,
    first_ref,
    second_ref,
    visible_ref,
    total_ref,
    drawn_ref,
    image_ref,
    out_params,
    out_first,
    out_second,
    grad,
):
    image_ref[...] = drawn_ref[...]
    seen = total_ref[14:15] > 0.0
    toward = [params_ref[j : j + 1] - total_ref[15 + j : 16 + j] for j in range(3)]
    square = toward[0] * toward[0] + toward[1] * toward[1] + toward[2] * toward[2]
    reach = 1.0 / jnp.sqrt(jnp.where(seen, square, 1.0))
    basis = jnp.concatenate(harmonics(toward[0] * reach, toward[1] * reach, toward[2] * reach), 0)
    basis = jnp.where(seen, basis, 0.0)
    grad[0:11] = total_ref[0:11]
    for c in range(3):
        grad[11 + 16 * c : 27 + 16 * c] = basis * total_ref[11 + c : 12 + c]
    values = grad[0:59]
    params, adam_m, adam_v = params_ref[...], first_ref[...], second_ref[...]
    moment_one = beta_one * adam_m + (1.0 - beta_one) * values
    moment_two = beta_two * adam_v + (1.0 - beta_two) * values * values
    scale_one = learn_rate / (1.0 - beta_one**adam_step)
    scale_two = 1.0 / (1.0 - beta_two**adam_step)
    stepped = params - scale_one * moment_one / (jnp.sqrt(moment_two * scale_two) + adam_eps)
    keep = visible_ref[...] > 0
    out_params[...] = jnp.where(keep, stepped, params)
    out_first[...] = jnp.where(keep, moment_one, adam_m)
    out_second[...] = jnp.where(keep, moment_two, adam_v)


def body(
    params, adam_m, adam_v, visible, cameras, send_index, send_count, tile_lists, tile_pos, target
):
    shards = lax.axis_size("space")
    views = lax.axis_size("view")
    tiles, width = tile_lists.shape[1:]
    slots = send_index.shape[2]
    nparam, owned = params.shape
    if slots != 64 * shards or shards % 2 or nparam != 59:
        return plain_body(
            params,
            adam_m,
            adam_v,
            visible,
            cameras,
            send_index,
            send_count,
            tile_lists,
            tile_pos,
            target,
        )
    center_y = 8.0 * (tiles * shards) / 64.0
    target = jnp.transpose(target, (1, 0, 2))
    vmem = pl.BlockSpec(memory_space=pltpu.VMEM)
    smem = pl.BlockSpec(memory_space=pltpu.SMEM)
    box = pltpu.VMEM((shards, 8, 128), f32)
    image, total = pl.pallas_call(
        functools.partial(step_kernel, shards, views, center_y),
        out_shape=(
            jax.ShapeDtypeStruct(target.shape, f32),
            jax.ShapeDtypeStruct((24, owned), f32),
        ),
        in_specs=[pl.BlockSpec(memory_space=pltpu.HBM), smem, vmem, smem, vmem, smem, vmem],
        out_specs=(vmem, vmem),
        scratch_shapes=[
            pltpu.VMEM((nparam, owned), f32),
            pltpu.VMEM((64, owned), f32),
            pltpu.VMEM((64, slots), f32),
            pltpu.VMEM((16, slots), f32),
            box,
            box,
            box,
            box,
            pltpu.VMEM((views, 16, owned), f32),
            pltpu.VMEM((owned, slots), bf16),
            pltpu.VMEM((tiles, slots, width), bf16),
            pltpu.VMEM((3, width // 2, width // 2), bf16),
            pltpu.VMEM((tiles, 40, width), f32),
            pltpu.VMEM((tiles * 256, width), f32),
            pltpu.VMEM((tiles * 256, width), f32),
            pltpu.VMEM((tiles * 256, width), f32),
            pltpu.VMEM((tiles * 256, width), bf16),
            pltpu.VMEM((tiles * 256, width), bf16),
            pltpu.VMEM((tiles * 256, width), bf16),
            pltpu.VMEM((tiles * 256, width), bf16),
            pltpu.SemaphoreType.DMA,
            pltpu.SemaphoreType.DMA((shards - 1,)),
            pltpu.SemaphoreType.DMA((shards - 1,)),
            pltpu.SemaphoreType.DMA((shards - 1,)),
            pltpu.SemaphoreType.DMA((shards - 1,)),
            pltpu.SemaphoreType.DMA((views - 1,)),
            pltpu.SemaphoreType.DMA((views - 1,)),
        ],
        compiler_params=pltpu.CompilerParams(
            collective_id=0, has_side_effects=True, vmem_limit_bytes=40 * 1024 * 1024
        ),
        cost_estimate=pl.CostEstimate(
            flops=16 * 10**9, bytes_accessed=8 * 10**6, transcendentals=10**6
        ),
        name="step",
    )(params, cameras, send_index, send_count, tile_lists, tile_pos, target)
    like = jax.ShapeDtypeStruct(params.shape, f32)
    image, *updated = pl.pallas_call(
        update_kernel,
        out_shape=(jax.ShapeDtypeStruct(target.shape, f32), like, like, like),
        in_specs=[vmem] * 6,
        out_specs=(vmem,) * 4,
        scratch_shapes=[pltpu.VMEM((64, owned), f32)],
        compiler_params=pltpu.CompilerParams(vmem_limit_bytes=16 * 1024 * 1024),
        name="update",
    )(params, adam_m, adam_v, visible.reshape(1, owned), total, image)
    return jnp.transpose(image, (1, 0, 2)), *updated


def solution(mesh):
    placed = (
        P(None, "space"),
        P(None, "space"),
        P(None, "space"),
        P("space"),
        P("view", None),
        P("view", "space", None),
        P("view", "space", None),
        P("view", "space", None),
        P("view", "space"),
        P("view", None, "space"),
    )
    return jax.shard_map(
        body,
        mesh=mesh,
        in_specs=placed,
        out_specs=(P("view", None, "space"), P(None, "space"), P(None, "space"), P(None, "space")),
        check_vma=False,
    )
```

```python
import functools

import jax
import jax.numpy as jnp
from jax import lax
from jax.experimental import pallas as pl
from jax.experimental.pallas import tpu as pltpu
from jax.sharding import PartitionSpec as P

focal_len = 1000.0
center_x = 512.0
harm_zero = 0.28209479177387814
harm_one = 0.4886025119029199
harm_two = (
    1.0925484305920792,
    -1.0925484305920792,
    0.31539156525252005,
    -1.0925484305920792,
    0.5462742152960396,
)
harm_three = (
    -0.5900435899266435,
    2.890611442640554,
    -0.4570457994644658,
    0.3731763325901154,
    -0.4570457994644658,
    1.445305721320277,
    -0.5900435899266435,
)
beta_one = 0.9
beta_two = 0.99
learn_rate = 0.05
adam_eps = 1e-08
adam_step = 100.0


def project(gauss, camera, center_y):
    rotation = [[camera[3 * i + j] for j in range(3)] for i in range(3)]
    offset = [camera[9 + i] for i in range(3)]
    centre = [gauss[i] for i in range(3)]
    viewed = [sum((rotation[i][j] * centre[j] for j in range(3))) + offset[i] for i in range(3)]
    inverse = 1.0 / viewed[2]
    screen_x = focal_len * viewed[0] * inverse + center_x
    screen_y = focal_len * viewed[1] * inverse + center_y
    scales = [jnp.exp(gauss[3 + i]) for i in range(3)]
    length = jnp.sqrt(
        gauss[6] * gauss[6] + gauss[7] * gauss[7] + gauss[8] * gauss[8] + gauss[9] * gauss[9]
    )
    quat_w, quat_x, quat_y, quat_z = [gauss[6 + i] / length for i in range(4)]
    spin = [
        [
            1.0 - 2.0 * (quat_y * quat_y + quat_z * quat_z),
            2.0 * (quat_x * quat_y - quat_w * quat_z),
            2.0 * (quat_x * quat_z + quat_w * quat_y),
        ],
        [
            2.0 * (quat_x * quat_y + quat_w * quat_z),
            1.0 - 2.0 * (quat_x * quat_x + quat_z * quat_z),
            2.0 * (quat_y * quat_z - quat_w * quat_x),
        ],
        [
            2.0 * (quat_x * quat_z - quat_w * quat_y),
            2.0 * (quat_y * quat_z + quat_w * quat_x),
            1.0 - 2.0 * (quat_x * quat_x + quat_y * quat_y),
        ],
    ]
    factor = [[spin[i][j] * scales[j] for j in range(3)] for i in range(3)]
    sigma = [
        [sum((factor[i][j] * factor[k][j] for j in range(3))) for k in range(3)] for i in range(3)
    ]
    near = focal_len * inverse
    lean_x = -focal_len * viewed[0] * inverse * inverse
    lean_y = -focal_len * viewed[1] * inverse * inverse
    jacob = [
        [near * rotation[0][j] + lean_x * rotation[2][j] for j in range(3)],
        [near * rotation[1][j] + lean_y * rotation[2][j] for j in range(3)],
    ]
    halfway = [
        [sum((jacob[a][i] * sigma[i][k] for i in range(3))) for k in range(3)] for a in range(2)
    ]
    upper = sum((halfway[0][k] * jacob[0][k] for k in range(3))) + 0.3
    middle = sum((halfway[0][k] * jacob[1][k] for k in range(3)))
    lower = sum((halfway[1][k] * jacob[1][k] for k in range(3))) + 0.3
    determinant = upper * lower - middle * middle
    conic_a = lower / determinant
    conic_b = -middle / determinant
    conic_c = upper / determinant
    opacity = jax.nn.sigmoid(gauss[10])
    camera_pos = [-sum((rotation[i][j] * offset[i] for i in range(3))) for j in range(3)]
    toward = [centre[j] - camera_pos[j] for j in range(3)]
    reach = jnp.sqrt(toward[0] * toward[0] + toward[1] * toward[1] + toward[2] * toward[2])
    unit_x = toward[0] / reach
    unit_y = toward[1] / reach
    unit_z = toward[2] / reach
    square_x = unit_x * unit_x
    square_y = unit_y * unit_y
    square_z = unit_z * unit_z
    basis = [
        harm_zero + 0.0 * unit_x,
        -harm_one * unit_y,
        harm_one * unit_z,
        -harm_one * unit_x,
        harm_two[0] * unit_x * unit_y,
        harm_two[1] * unit_y * unit_z,
        harm_two[2] * (2.0 * square_z - square_x - square_y),
        harm_two[3] * unit_x * unit_z,
        harm_two[4] * (square_x - square_y),
        harm_three[0] * unit_y * (3.0 * square_x - square_y),
        harm_three[1] * unit_x * unit_y * unit_z,
        harm_three[2] * unit_y * (4.0 * square_z - square_x - square_y),
        harm_three[3] * unit_z * (2.0 * square_z - 3.0 * square_x - 3.0 * square_y),
        harm_three[4] * unit_x * (4.0 * square_z - square_x - square_y),
        harm_three[5] * unit_z * (square_x - square_y),
        harm_three[6] * unit_x * (square_x - 3.0 * square_y),
    ]
    colors = [0.5 + sum((basis[k] * gauss[11 + 16 * c + k] for k in range(16))) for c in range(3)]
    return jnp.stack(
        [
            screen_x,
            screen_y,
            conic_a,
            conic_b,
            conic_c,
            opacity,
            colors[0],
            colors[1],
            colors[2],
            viewed[2],
            inverse,
        ]
    )


def shade_tile(entries, valid, tile):
    lane = jnp.arange(256, dtype=jnp.int32)
    column = tile % 64 * 16 + lane % 16
    height = tile // 64 * 16 + lane // 16
    pixel_x = column.astype(entries.dtype) + 0.5
    pixel_y = height.astype(entries.dtype) + 0.5
    apart_x = pixel_x[:, None] - entries[0][None, :]
    apart_y = pixel_y[:, None] - entries[1][None, :]
    quad = (
        entries[2][None, :] * apart_x * apart_x
        + 2.0 * entries[3][None, :] * apart_x * apart_y
        + entries[4][None, :] * apart_y * apart_y
    )
    alpha = entries[5][None, :] * jnp.exp(-0.5 * quad) * valid[None, :]
    keeping = jnp.log1p(-alpha)
    weight = alpha * jnp.exp(jnp.cumsum(keeping, axis=1) - keeping)
    feats = entries[6:11]
    return lax.dot_general(feats, weight, (((1,), (1,)), ((), ())), precision=lax.Precision.HIGHEST)


def adam_update(params, adam_m, adam_v, grad, visible):
    moment_one = beta_one * adam_m + (1.0 - beta_one) * grad
    moment_two = beta_two * adam_v + (1.0 - beta_two) * grad * grad
    first_hat = moment_one / (1.0 - beta_one**adam_step)
    second_hat = moment_two / (1.0 - beta_two**adam_step)
    stepped = params - learn_rate * first_hat / (jnp.sqrt(second_hat) + adam_eps)
    keep = (visible > 0)[None, :]
    return (
        jnp.where(keep, stepped, params),
        jnp.where(keep, moment_one, adam_m),
        jnp.where(keep, moment_two, adam_v),
    )


def composite(buffer, block_entries, block_usable, block_places):

    def one_block(item):
        entries, usable, places = item
        return jax.vmap(shade_tile, in_axes=(1, 0, 0))(buffer[:, entries], usable, places)

    return lax.map(jax.checkpoint(one_block), (block_entries, block_usable, block_places))


def plain_body(
    params, adam_m, adam_v, visible, cameras, send_index, send_count, tile_lists, tile_pos, target
):
    shards = lax.axis_size("space")
    tile_count = tile_lists.shape[1]
    list_width = tile_lists.shape[2]
    center_y = 8.0 * (tile_count * shards) / 64.0
    camera = cameras[0]
    route = send_index[0, 0]
    slot_width = route.shape[0] // shards
    slot_grid = jnp.arange(route.shape[0], dtype=jnp.int32).reshape(shards, slot_width) % slot_width
    in_use = (slot_grid < send_count[0, 0][:, None]).reshape(-1).astype(jnp.float32)

    def outgoing(gauss):
        return project(gauss, camera, center_y)[:, route] * in_use[None, :]

    sending, pull_send = jax.vjp(outgoing, params)
    arrived = lax.all_to_all(sending, "space", split_axis=1, concat_axis=1, tiled=True)
    per_block = 2
    block_count = tile_count // per_block
    lists = tile_lists[0]
    block_usable = (lists >= 0).astype(jnp.float32).reshape(block_count, per_block, list_width)
    block_entries = jnp.maximum(lists, 0).reshape(block_count, per_block, list_width)
    block_places = tile_pos[0].reshape(block_count, per_block)

    def draw_tiles(buffer):
        return composite(buffer, block_entries, block_usable, block_places).reshape(
            tile_count, 5, 256
        )

    tiles, pull_tiles = jax.vjp(draw_tiles, arrived)
    image = jnp.transpose(tiles, (1, 0, 2)).reshape(5, tile_count * 256)
    residue = (image - target[0]).reshape(5, tile_count, 256)
    (record_grad,) = pull_tiles(jnp.transpose(residue, (1, 0, 2)))
    returned = lax.all_to_all(record_grad, "space", split_axis=1, concat_axis=1, tiled=True)
    (grad,) = pull_send(returned)
    total = lax.psum(grad, "view")
    new_params, new_m, new_v = adam_update(params, adam_m, adam_v, total, visible)
    return (image[None], new_params, new_m, new_v)


f32 = jnp.float32
bf16 = jnp.bfloat16
MESH_ID = pl.DeviceIdType.MESH


def harmonics(unit_x, unit_y, unit_z):
    square_x = unit_x * unit_x
    square_y = unit_y * unit_y
    square_z = unit_z * unit_z
    return [
        jnp.full_like(unit_x, harm_zero),
        -harm_one * unit_y,
        harm_one * unit_z,
        -harm_one * unit_x,
        harm_two[0] * unit_x * unit_y,
        harm_two[1] * unit_y * unit_z,
        harm_two[2] * (2.0 * square_z - square_x - square_y),
        harm_two[3] * unit_x * unit_z,
        harm_two[4] * (square_x - square_y),
        harm_three[0] * unit_y * (3.0 * square_x - square_y),
        harm_three[1] * unit_x * unit_y * unit_z,
        harm_three[2] * unit_y * (4.0 * square_z - square_x - square_y),
        harm_three[3] * unit_z * (2.0 * square_z - 3.0 * square_x - 3.0 * square_y),
        harm_three[4] * unit_x * (4.0 * square_z - square_x - square_y),
        harm_three[5] * unit_z * (square_x - square_y),
        harm_three[6] * unit_x * (square_x - 3.0 * square_y),
    ]


def camera_centre(camera):
    return [-sum(camera[3 * i + j] * camera[9 + i] for i in range(3)) for j in range(3)]


def geometry(gauss, camera, center_y):
    rotation = [[camera[3 * i + j] for j in range(3)] for i in range(3)]
    offset = [camera[9 + i] for i in range(3)]
    centre = gauss[0:3]
    viewed = [sum(rotation[i][j] * centre[j] for j in range(3)) + offset[i] for i in range(3)]
    inverse = 1.0 / viewed[2]
    near = focal_len * inverse
    ratio_x = viewed[0] * inverse
    ratio_y = viewed[1] * inverse
    screen_x = focal_len * ratio_x + center_x
    screen_y = focal_len * ratio_y + center_y
    scales = [jnp.exp(2.0 * gauss[3 + i]) for i in range(3)]
    squares = [gauss[6 + i] * gauss[6 + i] for i in range(4)]
    double = 2.0 / (squares[0] + squares[1] + squares[2] + squares[3])
    qw, qx, qy, qz = gauss[6:10]
    dx, dy, dz = double * qx, double * qy, double * qz
    xx, yy, zz = dx * qx, dy * qy, dz * qz
    xy, xz, yz = dx * qy, dx * qz, dy * qz
    wx, wy, wz = dx * qw, dy * qw, dz * qw
    spin = [
        [1.0 - (yy + zz), xy - wz, xz + wy],
        [xy + wz, 1.0 - (xx + zz), yz - wx],
        [xz - wy, yz + wx, 1.0 - (xx + yy)],
    ]
    jacob = [
        [near * (rotation[0][j] - ratio_x * rotation[2][j]) for j in range(3)],
        [near * (rotation[1][j] - ratio_y * rotation[2][j]) for j in range(3)],
    ]
    turned = [[sum(jacob[a][i] * spin[i][k] for i in range(3)) for k in range(3)] for a in range(2)]
    scaled = [turned[0][k] * scales[k] for k in range(3)]
    upper = sum(scaled[k] * turned[0][k] for k in range(3)) + 0.3
    middle = sum(scaled[k] * turned[1][k] for k in range(3))
    lower = sum(turned[1][k] * scales[k] * turned[1][k] for k in range(3)) + 0.3
    over = 1.0 / (upper * lower - middle * middle)
    position = camera_centre(camera)
    toward = [centre[j] - position[j] for j in range(3)]
    reach = 1.0 / jnp.sqrt(toward[0] * toward[0] + toward[1] * toward[1] + toward[2] * toward[2])
    basis = harmonics(toward[0] * reach, toward[1] * reach, toward[2] * reach)
    return (
        screen_x,
        screen_y,
        lower * over,
        -middle * over,
        upper * over,
        viewed[2],
        inverse,
    ), basis


def halves(x):
    high = x.astype(bf16).astype(f32)
    return high, x - high


def thirds(x):
    high, rest = halves(x)
    mid, low = halves(rest)
    return jnp.concatenate([high, mid, low], axis=0).astype(bf16)


def two(x):
    high = x.astype(bf16)
    return high, (x - high.astype(f32)).astype(bf16)


def mm(a, b):
    return jnp.dot(a, b, preferred_element_type=f32)


def mm_nt(a, b):
    return lax.dot_general(a, b, (((1,), (1,)), ((), ())), preferred_element_type=f32)


def mm_tn(a, b):
    return lax.dot_general(a, b, (((0,), (0,)), ((), ())), preferred_element_type=f32)


def fold(x, count):
    rows = x.shape[0] // count
    return sum(x[rows * i : rows * (i + 1)] for i in range(count))


def pack(rows, box, shards):
    lane = lax.broadcasted_iota(jnp.int32, (8, 128), 1)
    for j in range(shards // 2):
        first = rows[0:8, 128 * j : 128 * j + 128]
        second = rows[8:16, 128 * j : 128 * j + 128]
        box[2 * j] = jnp.where(lane < 64, first, pltpu.roll(second, 64, 1))
        box[2 * j + 1] = jnp.where(lane < 64, pltpu.roll(first, 64, 1), second)


def unpack(box, shards):
    lane = lax.broadcasted_iota(jnp.int32, (8, 128), 1)
    top, bottom = [], []
    for j in range(shards // 2):
        even, odd = box[2 * j], box[2 * j + 1]
        top.append(jnp.where(lane < 64, even, pltpu.roll(odd, 64, 1)))
        bottom.append(jnp.where(lane < 64, pltpu.roll(even, 64, 1), odd))
    return jnp.concatenate([jnp.concatenate(top, 1), jnp.concatenate(bottom, 1)], 0)


def step_kernel(
    shards,
    views,
    center_y,
    params_hbm,
    camera_hbm,
    index_hbm,
    count_hbm,
    lists_hbm,
    place_hbm,
    target_hbm,
    image_ref,
    total_ref,
    held,
    camera_ref,
    index_ref,
    count_ref,
    lists_ref,
    place_ref,
    target_ref,
    wide,
    picked,
    rows,
    out_box,
    in_box,
    back_box,
    home_box,
    shared,
    pick_ref,
    list_hot,
    tri_ref,
    near_ref,
    alpha_ref,
    ratio_ref,
    sum_ref,
    part_high,
    part_low,
    weight_high,
    weight_low,
    load_sem,
    send_sem,
    recv_sem,
    send_back,
    recv_back,
    send_view,
    recv_view,
):
    me_view = lax.axis_index("view")
    me = lax.axis_index("space")
    slots = index_ref.shape[2]
    owned = params_hbm.shape[1]
    tiles = lists_ref.shape[1]
    width = lists_ref.shape[2]
    half = width // 2
    slot_width = slots // shards

    pairs = [
        (index_hbm, index_ref),
        (params_hbm, held),
        (camera_hbm, camera_ref),
        (lists_hbm, lists_ref),
        (count_hbm, count_ref),
        (place_hbm, place_ref),
        (target_hbm, target_ref),
    ]
    loads = [
        pltpu.make_async_copy(source, there, load_sem.at[i])
        for i, (source, there) in enumerate(pairs)
    ]
    for load in loads:
        load.start()
    barrier = pltpu.get_barrier_semaphore()
    for r in range(1, shards):
        pl.semaphore_signal(
            barrier, inc=1, device_id=(me_view, lax.rem(me + r, shards)), device_id_type=MESH_ID
        )
    for r in range(1, views):
        pl.semaphore_signal(
            barrier, inc=1, device_id=(lax.rem(me_view + r, views), me), device_id_type=MESH_ID
        )

    loads[0].wait()
    count_up = lax.broadcasted_iota(jnp.int32, (32, slots), 0)

    def pick_rows(i, carry):
        at = pl.multiple_of(32 * i, 32)
        pick_ref[pl.ds(at, 32)] = jnp.where(count_up + at == index_ref[0], 1.0, 0.0).astype(bf16)
        return carry

    lax.fori_loop(0, owned // 32, pick_rows, 0, unroll=True)
    wide[56:64] = jnp.zeros((8, owned), f32)
    for load in loads[1:]:
        load.wait()
    wide[0:59] = held[...]
    picked[...] = fold(mm(thirds(wide[...]), pick_ref[...]), 3)

    camera = [camera_ref[0, i] for i in range(12)]
    gauss = [picked[i : i + 1] for i in range(10)]

    def project_rows(values):
        outs, basis = geometry(values, camera, center_y)
        return outs, jnp.concatenate(basis, axis=0)

    (outs, basis), pull = jax.vjp(project_rows, gauss)
    opacity = 1.0 / (1.0 + jnp.exp(-picked[10:11]))
    rows[...] = jnp.zeros_like(rows)
    for i in range(5):
        rows[i : i + 1] = outs[i]
    rows[5:6] = opacity
    for c in range(3):
        rows[8 + c : 9 + c] = 0.5 + jnp.sum(
            basis * picked[11 + 16 * c : 27 + 16 * c], axis=0, keepdims=True
        )
    rows[11:12] = outs[5]
    rows[12:13] = outs[6]
    pack(rows, out_box, shards)

    pl.semaphore_wait(barrier, shards + views - 2)

    def swap(source, landing, sends, recvs):
        copies = []
        for r in range(1, shards):
            to = lax.rem(me + r, shards)
            copy = pltpu.make_async_remote_copy(
                src_ref=source.at[to],
                dst_ref=landing.at[me],
                send_sem=sends.at[r - 1],
                recv_sem=recvs.at[r - 1],
                device_id=(me_view, to),
                device_id_type=MESH_ID,
            )
            copy.start()
            copies.append(copy)
        landing[pl.ds(me, 1)] = source[pl.ds(me, 1)]
        return copies

    copies = swap(out_box, in_box, send_sem, recv_sem)

    def list_rows(i, carry):
        at = pl.multiple_of(32 * i, 32)
        for t in range(tiles):
            list_hot[t, pl.ds(at, 32)] = jnp.where(
                count_up + at == lists_ref[0, t : t + 1], 1.0, 0.0
            ).astype(bf16)
        return carry

    lax.fori_loop(0, slots // 32, list_rows, 0, unroll=True)
    first = lax.broadcasted_iota(jnp.int32, (half, half), 0)
    second = lax.broadcasted_iota(jnp.int32, (half, half), 1)
    tri_ref[0] = jnp.where(first < second, 1.0, 0.0).astype(bf16)
    tri_ref[1] = jnp.where(first > second, 1.0, 0.0).astype(bf16)
    tri_ref[2] = jnp.ones((half, half), bf16)
    pixel = lax.broadcasted_iota(jnp.int32, (16, 256), 1)
    kind = lax.broadcasted_iota(jnp.int32, (16, 256), 0)
    grid_x = (pixel % 16).astype(f32) - 7.5
    grid_y = (pixel // 16).astype(f32) - 7.5
    moments_of = jnp.where(kind == 0, 1.0, 0.0)
    for i, values in enumerate(
        [grid_x, grid_y, grid_x * grid_x, grid_x * grid_y, grid_y * grid_y]
    ):
        moments_of = jnp.where(kind == i + 1, values, moments_of)
    moments_of = moments_of.astype(bf16)
    side_x = lax.broadcasted_iota(jnp.int32, (16, 1), 0).astype(f32) - 7.5

    for copy in copies:
        copy.wait()
    arrived = thirds(unpack(in_box, shards))

    spans = [slice(256 * t, 256 * t + 256) for t in range(tiles)]
    drawn_from = []
    for t in range(tiles):
        entries = fold(mm(arrived, list_hot[t]), 3)
        place = place_ref[0, t]
        middle_x = (place % 64 * 16 + 8).astype(f32)
        middle_y = (place // 64 * 16 + 8).astype(f32)
        u = entries[0:1] - middle_x
        y = entries[1:2] - middle_y
        a, b, c = entries[2:3], entries[3:4], entries[4:5]
        drawn_from.append((u, y, a, b, c, entries[8:16]))
        apart_x = side_x - u
        near_ref[t, 0:16] = apart_x
        near_ref[t, 16:32] = (-0.5 * a) * apart_x * apart_x
        near_ref[t, 32:33] = y
        near_ref[t, 33:34] = -b
        near_ref[t, 34:35] = -0.5 * c
        near_ref[t, 35:36] = entries[5:6]

    def light(i, carry):
        at = pl.multiple_of(16 * i, 16)
        for t in range(tiles):
            apart_y = (i.astype(f32) - 7.5) - near_ref[t, 32:33]
            line = near_ref[t, 33:34] * apart_y
            shift = near_ref[t, 34:35] * apart_y * apart_y
            quad = near_ref[t, 16:32] + line * near_ref[t, 0:16] + shift
            alpha = near_ref[t, 35:36] * jnp.exp(quad)
            through = 1.0 - alpha
            keep_high, keep_low = two(jnp.log(through))
            here = pl.ds(256 * t + at, 16)
            alpha_ref[here] = alpha
            ratio_ref[here] = alpha / through
            part_high[here] = keep_high
            part_low[here] = keep_low
        return carry

    lax.fori_loop(0, 16, light, 0, unroll=True)

    def ordered_sum(order):
        whole, cut = (slice(0, half), slice(half, width))
        if order:
            whole, cut = cut, whole
        sum_ref[:, whole] = mm(part_high[:, whole], tri_ref[order]) + mm(
            part_low[:, whole], tri_ref[order]
        )
        sum_ref[:, cut] = (
            mm(part_high[:, cut], tri_ref[order])
            + mm(part_low[:, cut], tri_ref[order])
            + mm(part_high[:, whole], tri_ref[2])
            + mm(part_low[:, whole], tri_ref[2])
        )

    ordered_sum(0)
    steps = 16 * tiles

    def weigh(i, carry):
        here = pl.ds(pl.multiple_of(16 * i, 16), 16)
        weight = alpha_ref[here] * jnp.exp(sum_ref[here])
        alpha_ref[here] = weight
        weight_high[here], weight_low[here] = two(weight)
        return carry

    lax.fori_loop(0, steps, weigh, 0, unroll=True)

    feat_grads = []
    for t in range(tiles):
        feat_high, feat_low = halves(drawn_from[t][5])
        feat_two = jnp.concatenate([feat_high, feat_low], 0).astype(bf16)
        drawn = fold(
            mm_nt(feat_two, weight_high[spans[t]]) + mm_nt(feat_two, weight_low[spans[t]]), 2
        )
        for ch in range(5):
            image_ref[ch, :, spans[t]] = drawn[ch : ch + 1]
        shown = jnp.concatenate(
            [target_ref[ch, :, spans[t]] for ch in range(5)] + [jnp.zeros((3, 256), f32)], 0
        )
        res_high, res_low = halves(drawn - shown)
        res_two = jnp.concatenate([res_high, res_low], 0)
        sum_ref[spans[t]] = mm_tn(
            jnp.concatenate([res_two, res_two], 0).astype(bf16),
            jnp.concatenate([feat_high, feat_high, feat_low, feat_low], 0).astype(bf16),
        )
        res_two = res_two.astype(bf16)
        feat_grads.append(
            fold(mm(res_two, weight_high[spans[t]]) + mm(res_two, weight_low[spans[t]]), 2)
        )

    def pull_back(i, carry):
        here = pl.ds(pl.multiple_of(16 * i, 16), 16)
        part = alpha_ref[here] * sum_ref[here]
        alpha_ref[here] = part
        part_high[here], part_low[here] = two(part)
        return carry

    lax.fori_loop(0, steps, pull_back, 0, unroll=True)
    ordered_sum(1)

    def slope_of(i, carry):
        here = pl.ds(pl.multiple_of(16 * i, 16), 16)
        part_high[here], part_low[here] = two(alpha_ref[here] - sum_ref[here] * ratio_ref[here])
        return carry

    lax.fori_loop(0, steps, slope_of, 0, unroll=True)

    returning = jnp.zeros((16, slots), f32)
    for t in range(tiles):
        u, y, a, b, c, _ = drawn_from[t]
        moments = mm(moments_of, part_high[spans[t]]) + mm(moments_of, part_low[spans[t]])
        m, mx, my, mxx, mxy, myy = [moments[i : i + 1] for i in range(6)]
        sx = mx - u * m
        sy = my - y * m
        sxx = mxx - u * mx - u * sx
        sxy = mxy - u * my - y * sx
        syy = myy - y * my - y * sy
        zero = jnp.zeros((2, width), f32)
        entry_grad = jnp.concatenate(
            [
                a * sx + b * sy,
                b * sx + c * sy,
                -0.5 * sxx,
                -sxy,
                -0.5 * syy,
                m,
                zero,
                feat_grads[t],
            ],
            0,
        )
        returning = returning + fold(mm_nt(thirds(entry_grad), list_hot[t]), 3)

    rows[...] = returning
    pack(rows, back_box, shards)
    copies = swap(back_box, home_box, send_back, recv_back)
    lane = lax.broadcasted_iota(jnp.int32, (1, slots), 1)
    used = jnp.zeros((1, slots), f32)
    for d in range(shards):
        begin = slot_width * d
        inside = (lane >= begin) & (lane < begin + count_ref[0, 0, d])
        used = jnp.where(inside, 1.0, used)
    for copy in copies:
        copy.wait()

    rows[...] = unpack(home_box, shards)
    spread = sum(
        picked[11 + 16 * c : 27 + 16 * c] * rows[8 + c : 9 + c] for c in range(3)
    )
    cotangents = tuple(rows[i : i + 1] for i in range(5)) + (rows[11:12], rows[12:13])
    (gauss_grad,) = pull((cotangents, spread))
    logit_grad = rows[5:6] * (1.0 - opacity)
    colour_grad = rows[8:11]
    for i in range(10):
        rows[i : i + 1] = gauss_grad[i]
    rows[10:11] = logit_grad
    rows[11:14] = colour_grad
    rows[14:15] = used
    rows[15:16] = jnp.zeros((1, slots), f32)
    own = fold(mm_nt(thirds(rows[...]), pick_ref[...]), 3)
    position = camera_centre(camera)
    far = lax.broadcasted_iota(jnp.int32, (1, owned), 1)
    last = jnp.where(far == 0, position[0], jnp.where(far == 1, position[1], position[2]))
    shared[pl.ds(me_view, 1)] = jnp.concatenate([own[0:15], last], 0)[None]
    copies = []
    for r in range(1, views):
        copy = pltpu.make_async_remote_copy(
            src_ref=shared.at[me_view],
            dst_ref=shared.at[me_view],
            send_sem=send_view.at[r - 1],
            recv_sem=recv_view.at[r - 1],
            device_id=(lax.rem(me_view + r, views), me),
            device_id_type=MESH_ID,
        )
        copy.start()
        copies.append(copy)
    for copy in copies:
        copy.wait()
    total_ref[0:16] = sum(shared[w] for w in range(views))
    for j in range(3):
        total_ref[15 + j : 16 + j] = sum(
            shared[w, 14:15] * shared[w, 15:16, j : j + 1] for w in range(views)
        )
    total_ref[18:24] = jnp.zeros((6, owned), f32)


def update_kernel(
    params_ref,
    first_ref,
    second_ref,
    visible_ref,
    total_ref,
    drawn_ref,
    image_ref,
    out_params,
    out_first,
    out_second,
    grad,
):
    image_ref[...] = drawn_ref[...]
    seen = total_ref[14:15] > 0.0
    toward = [params_ref[j : j + 1] - total_ref[15 + j : 16 + j] for j in range(3)]
    square = toward[0] * toward[0] + toward[1] * toward[1] + toward[2] * toward[2]
    reach = 1.0 / jnp.sqrt(jnp.where(seen, square, 1.0))
    basis = jnp.concatenate(harmonics(toward[0] * reach, toward[1] * reach, toward[2] * reach), 0)
    basis = jnp.where(seen, basis, 0.0)
    grad[0:11] = total_ref[0:11]
    for c in range(3):
        grad[11 + 16 * c : 27 + 16 * c] = basis * total_ref[11 + c : 12 + c]
    values = grad[0:59]
    params, adam_m, adam_v = params_ref[...], first_ref[...], second_ref[...]
    moment_one = beta_one * adam_m + (1.0 - beta_one) * values
    moment_two = beta_two * adam_v + (1.0 - beta_two) * values * values
    scale_one = learn_rate / (1.0 - beta_one**adam_step)
    scale_two = 1.0 / (1.0 - beta_two**adam_step)
    stepped = params - scale_one * moment_one / (jnp.sqrt(moment_two * scale_two) + adam_eps)
    keep = visible_ref[...] > 0
    out_params[...] = jnp.where(keep, stepped, params)
    out_first[...] = jnp.where(keep, moment_one, adam_m)
    out_second[...] = jnp.where(keep, moment_two, adam_v)


def body(
    params, adam_m, adam_v, visible, cameras, send_index, send_count, tile_lists, tile_pos, target
):
    shards = lax.axis_size("space")
    views = lax.axis_size("view")
    tiles, width = tile_lists.shape[1:]
    slots = send_index.shape[2]
    nparam, owned = params.shape
    if slots != 64 * shards or shards % 2 or nparam != 59:
        return plain_body(
            params,
            adam_m,
            adam_v,
            visible,
            cameras,
            send_index,
            send_count,
            tile_lists,
            tile_pos,
            target,
        )
    center_y = 8.0 * (tiles * shards) / 64.0
    target = jnp.transpose(target, (1, 0, 2))
    vmem = pl.BlockSpec(memory_space=pltpu.VMEM)
    box = pltpu.VMEM((shards, 8, 128), f32)
    image, total = pl.pallas_call(
        functools.partial(step_kernel, shards, views, center_y),
        out_shape=(
            pltpu.VMEM(target.shape, f32),
            pltpu.VMEM((24, owned), f32),
        ),
        in_specs=[pl.BlockSpec(memory_space=pl.ANY)] * 7,
        out_specs=(vmem, vmem),
        scratch_shapes=[
            pltpu.VMEM((nparam, owned), f32),
            pltpu.SMEM(cameras.shape, f32),
            pltpu.VMEM(send_index.shape, jnp.int32),
            pltpu.SMEM(send_count.shape, jnp.int32),
            pltpu.VMEM(tile_lists.shape, jnp.int32),
            pltpu.SMEM(tile_pos.shape, jnp.int32),
            pltpu.VMEM(target.shape, f32),
            pltpu.VMEM((64, owned), f32),
            pltpu.VMEM((64, slots), f32),
            pltpu.VMEM((16, slots), f32),
            box,
            box,
            box,
            box,
            pltpu.VMEM((views, 16, owned), f32),
            pltpu.VMEM((owned, slots), bf16),
            pltpu.VMEM((tiles, slots, width), bf16),
            pltpu.VMEM((3, width // 2, width // 2), bf16),
            pltpu.VMEM((tiles, 40, width), f32),
            pltpu.VMEM((tiles * 256, width), f32),
            pltpu.VMEM((tiles * 256, width), f32),
            pltpu.VMEM((tiles * 256, width), f32),
            pltpu.VMEM((tiles * 256, width), bf16),
            pltpu.VMEM((tiles * 256, width), bf16),
            pltpu.VMEM((tiles * 256, width), bf16),
            pltpu.VMEM((tiles * 256, width), bf16),
            pltpu.SemaphoreType.DMA((7,)),
            pltpu.SemaphoreType.DMA((shards - 1,)),
            pltpu.SemaphoreType.DMA((shards - 1,)),
            pltpu.SemaphoreType.DMA((shards - 1,)),
            pltpu.SemaphoreType.DMA((shards - 1,)),
            pltpu.SemaphoreType.DMA((views - 1,)),
            pltpu.SemaphoreType.DMA((views - 1,)),
        ],
        compiler_params=pltpu.CompilerParams(
            collective_id=0, has_side_effects=True, vmem_limit_bytes=56 * 1024 * 1024
        ),
        cost_estimate=pl.CostEstimate(
            flops=16 * 10**9, bytes_accessed=8 * 10**6, transcendentals=10**6
        ),
        name="step",
    )(params, cameras, send_index, send_count, tile_lists, tile_pos, target)
    like = jax.ShapeDtypeStruct(params.shape, f32)
    image, *updated = pl.pallas_call(
        update_kernel,
        out_shape=(jax.ShapeDtypeStruct(target.shape, f32), like, like, like),
        in_specs=[vmem] * 6,
        out_specs=(vmem,) * 4,
        scratch_shapes=[pltpu.VMEM((64, owned), f32)],
        compiler_params=pltpu.CompilerParams(vmem_limit_bytes=16 * 1024 * 1024),
        name="update",
    )(params, adam_m, adam_v, visible.reshape(1, owned), total, image)
    return jnp.transpose(image, (1, 0, 2)), *updated


def solution(mesh):
    placed = (
        P(None, "space"),
        P(None, "space"),
        P(None, "space"),
        P("space"),
        P("view", None),
        P("view", "space", None),
        P("view", "space", None),
        P("view", "space", None),
        P("view", "space"),
        P("view", None, "space"),
    )
    return jax.shard_map(
        body,
        mesh=mesh,
        in_specs=placed,
        out_specs=(P("view", None, "space"), P(None, "space"), P(None, "space"), P(None, "space")),
        check_vma=False,
    )
```

```python
import functools

import jax
import jax.numpy as jnp
from jax import lax
from jax.experimental import pallas as pl
from jax.experimental.pallas import tpu as pltpu
from jax.sharding import PartitionSpec as P

focal_len = 1000.0
center_x = 512.0
harm_zero = 0.28209479177387814
harm_one = 0.4886025119029199
harm_two = (
    1.0925484305920792,
    -1.0925484305920792,
    0.31539156525252005,
    -1.0925484305920792,
    0.5462742152960396,
)
harm_three = (
    -0.5900435899266435,
    2.890611442640554,
    -0.4570457994644658,
    0.3731763325901154,
    -0.4570457994644658,
    1.445305721320277,
    -0.5900435899266435,
)
beta_one = 0.9
beta_two = 0.99
learn_rate = 0.05
adam_eps = 1e-08
adam_step = 100.0


def project(gauss, camera, center_y):
    rotation = [[camera[3 * i + j] for j in range(3)] for i in range(3)]
    offset = [camera[9 + i] for i in range(3)]
    centre = [gauss[i] for i in range(3)]
    viewed = [sum((rotation[i][j] * centre[j] for j in range(3))) + offset[i] for i in range(3)]
    inverse = 1.0 / viewed[2]
    screen_x = focal_len * viewed[0] * inverse + center_x
    screen_y = focal_len * viewed[1] * inverse + center_y
    scales = [jnp.exp(gauss[3 + i]) for i in range(3)]
    length = jnp.sqrt(
        gauss[6] * gauss[6] + gauss[7] * gauss[7] + gauss[8] * gauss[8] + gauss[9] * gauss[9]
    )
    quat_w, quat_x, quat_y, quat_z = [gauss[6 + i] / length for i in range(4)]
    spin = [
        [
            1.0 - 2.0 * (quat_y * quat_y + quat_z * quat_z),
            2.0 * (quat_x * quat_y - quat_w * quat_z),
            2.0 * (quat_x * quat_z + quat_w * quat_y),
        ],
        [
            2.0 * (quat_x * quat_y + quat_w * quat_z),
            1.0 - 2.0 * (quat_x * quat_x + quat_z * quat_z),
            2.0 * (quat_y * quat_z - quat_w * quat_x),
        ],
        [
            2.0 * (quat_x * quat_z - quat_w * quat_y),
            2.0 * (quat_y * quat_z + quat_w * quat_x),
            1.0 - 2.0 * (quat_x * quat_x + quat_y * quat_y),
        ],
    ]
    factor = [[spin[i][j] * scales[j] for j in range(3)] for i in range(3)]
    sigma = [
        [sum((factor[i][j] * factor[k][j] for j in range(3))) for k in range(3)] for i in range(3)
    ]
    near = focal_len * inverse
    lean_x = -focal_len * viewed[0] * inverse * inverse
    lean_y = -focal_len * viewed[1] * inverse * inverse
    jacob = [
        [near * rotation[0][j] + lean_x * rotation[2][j] for j in range(3)],
        [near * rotation[1][j] + lean_y * rotation[2][j] for j in range(3)],
    ]
    halfway = [
        [sum((jacob[a][i] * sigma[i][k] for i in range(3))) for k in range(3)] for a in range(2)
    ]
    upper = sum((halfway[0][k] * jacob[0][k] for k in range(3))) + 0.3
    middle = sum((halfway[0][k] * jacob[1][k] for k in range(3)))
    lower = sum((halfway[1][k] * jacob[1][k] for k in range(3))) + 0.3
    determinant = upper * lower - middle * middle
    conic_a = lower / determinant
    conic_b = -middle / determinant
    conic_c = upper / determinant
    opacity = jax.nn.sigmoid(gauss[10])
    camera_pos = [-sum((rotation[i][j] * offset[i] for i in range(3))) for j in range(3)]
    toward = [centre[j] - camera_pos[j] for j in range(3)]
    reach = jnp.sqrt(toward[0] * toward[0] + toward[1] * toward[1] + toward[2] * toward[2])
    unit_x = toward[0] / reach
    unit_y = toward[1] / reach
    unit_z = toward[2] / reach
    square_x = unit_x * unit_x
    square_y = unit_y * unit_y
    square_z = unit_z * unit_z
    basis = [
        harm_zero + 0.0 * unit_x,
        -harm_one * unit_y,
        harm_one * unit_z,
        -harm_one * unit_x,
        harm_two[0] * unit_x * unit_y,
        harm_two[1] * unit_y * unit_z,
        harm_two[2] * (2.0 * square_z - square_x - square_y),
        harm_two[3] * unit_x * unit_z,
        harm_two[4] * (square_x - square_y),
        harm_three[0] * unit_y * (3.0 * square_x - square_y),
        harm_three[1] * unit_x * unit_y * unit_z,
        harm_three[2] * unit_y * (4.0 * square_z - square_x - square_y),
        harm_three[3] * unit_z * (2.0 * square_z - 3.0 * square_x - 3.0 * square_y),
        harm_three[4] * unit_x * (4.0 * square_z - square_x - square_y),
        harm_three[5] * unit_z * (square_x - square_y),
        harm_three[6] * unit_x * (square_x - 3.0 * square_y),
    ]
    colors = [0.5 + sum((basis[k] * gauss[11 + 16 * c + k] for k in range(16))) for c in range(3)]
    return jnp.stack(
        [
            screen_x,
            screen_y,
            conic_a,
            conic_b,
            conic_c,
            opacity,
            colors[0],
            colors[1],
            colors[2],
            viewed[2],
            inverse,
        ]
    )


def shade_tile(entries, valid, tile):
    lane = jnp.arange(256, dtype=jnp.int32)
    column = tile % 64 * 16 + lane % 16
    height = tile // 64 * 16 + lane // 16
    pixel_x = column.astype(entries.dtype) + 0.5
    pixel_y = height.astype(entries.dtype) + 0.5
    apart_x = pixel_x[:, None] - entries[0][None, :]
    apart_y = pixel_y[:, None] - entries[1][None, :]
    quad = (
        entries[2][None, :] * apart_x * apart_x
        + 2.0 * entries[3][None, :] * apart_x * apart_y
        + entries[4][None, :] * apart_y * apart_y
    )
    alpha = entries[5][None, :] * jnp.exp(-0.5 * quad) * valid[None, :]
    keeping = jnp.log1p(-alpha)
    weight = alpha * jnp.exp(jnp.cumsum(keeping, axis=1) - keeping)
    feats = entries[6:11]
    return lax.dot_general(feats, weight, (((1,), (1,)), ((), ())), precision=lax.Precision.HIGHEST)


def adam_update(params, adam_m, adam_v, grad, visible):
    moment_one = beta_one * adam_m + (1.0 - beta_one) * grad
    moment_two = beta_two * adam_v + (1.0 - beta_two) * grad * grad
    first_hat = moment_one / (1.0 - beta_one**adam_step)
    second_hat = moment_two / (1.0 - beta_two**adam_step)
    stepped = params - learn_rate * first_hat / (jnp.sqrt(second_hat) + adam_eps)
    keep = (visible > 0)[None, :]
    return (
        jnp.where(keep, stepped, params),
        jnp.where(keep, moment_one, adam_m),
        jnp.where(keep, moment_two, adam_v),
    )


def composite(buffer, block_entries, block_usable, block_places):

    def one_block(item):
        entries, usable, places = item
        return jax.vmap(shade_tile, in_axes=(1, 0, 0))(buffer[:, entries], usable, places)

    return lax.map(jax.checkpoint(one_block), (block_entries, block_usable, block_places))


def plain_body(
    params, adam_m, adam_v, visible, cameras, send_index, send_count, tile_lists, tile_pos, target
):
    shards = lax.axis_size("space")
    tile_count = tile_lists.shape[1]
    list_width = tile_lists.shape[2]
    center_y = 8.0 * (tile_count * shards) / 64.0
    camera = cameras[0]
    route = send_index[0, 0]
    slot_width = route.shape[0] // shards
    slot_grid = jnp.arange(route.shape[0], dtype=jnp.int32).reshape(shards, slot_width) % slot_width
    in_use = (slot_grid < send_count[0, 0][:, None]).reshape(-1).astype(jnp.float32)

    def outgoing(gauss):
        return project(gauss, camera, center_y)[:, route] * in_use[None, :]

    sending, pull_send = jax.vjp(outgoing, params)
    arrived = lax.all_to_all(sending, "space", split_axis=1, concat_axis=1, tiled=True)
    per_block = 2
    block_count = tile_count // per_block
    lists = tile_lists[0]
    block_usable = (lists >= 0).astype(jnp.float32).reshape(block_count, per_block, list_width)
    block_entries = jnp.maximum(lists, 0).reshape(block_count, per_block, list_width)
    block_places = tile_pos[0].reshape(block_count, per_block)

    def draw_tiles(buffer):
        return composite(buffer, block_entries, block_usable, block_places).reshape(
            tile_count, 5, 256
        )

    tiles, pull_tiles = jax.vjp(draw_tiles, arrived)
    image = jnp.transpose(tiles, (1, 0, 2)).reshape(5, tile_count * 256)
    residue = (image - target[0]).reshape(5, tile_count, 256)
    (record_grad,) = pull_tiles(jnp.transpose(residue, (1, 0, 2)))
    returned = lax.all_to_all(record_grad, "space", split_axis=1, concat_axis=1, tiled=True)
    (grad,) = pull_send(returned)
    total = lax.psum(grad, "view")
    new_params, new_m, new_v = adam_update(params, adam_m, adam_v, total, visible)
    return (image[None], new_params, new_m, new_v)


f32 = jnp.float32
bf16 = jnp.bfloat16
MESH_ID = pl.DeviceIdType.MESH


def harmonics(unit_x, unit_y, unit_z):
    square_x = unit_x * unit_x
    square_y = unit_y * unit_y
    square_z = unit_z * unit_z
    return [
        jnp.full_like(unit_x, harm_zero),
        -harm_one * unit_y,
        harm_one * unit_z,
        -harm_one * unit_x,
        harm_two[0] * unit_x * unit_y,
        harm_two[1] * unit_y * unit_z,
        harm_two[2] * (2.0 * square_z - square_x - square_y),
        harm_two[3] * unit_x * unit_z,
        harm_two[4] * (square_x - square_y),
        harm_three[0] * unit_y * (3.0 * square_x - square_y),
        harm_three[1] * unit_x * unit_y * unit_z,
        harm_three[2] * unit_y * (4.0 * square_z - square_x - square_y),
        harm_three[3] * unit_z * (2.0 * square_z - 3.0 * square_x - 3.0 * square_y),
        harm_three[4] * unit_x * (4.0 * square_z - square_x - square_y),
        harm_three[5] * unit_z * (square_x - square_y),
        harm_three[6] * unit_x * (square_x - 3.0 * square_y),
    ]


def camera_centre(camera):
    return [-sum(camera[3 * i + j] * camera[9 + i] for i in range(3)) for j in range(3)]


def geometry(gauss, camera, center_y):
    rotation = [[camera[3 * i + j] for j in range(3)] for i in range(3)]
    offset = [camera[9 + i] for i in range(3)]
    centre = gauss[0:3]
    viewed = [sum(rotation[i][j] * centre[j] for j in range(3)) + offset[i] for i in range(3)]
    inverse = 1.0 / viewed[2]
    near = focal_len * inverse
    ratio_x = viewed[0] * inverse
    ratio_y = viewed[1] * inverse
    screen_x = focal_len * ratio_x + center_x
    screen_y = focal_len * ratio_y + center_y
    scales = [jnp.exp(2.0 * gauss[3 + i]) for i in range(3)]
    squares = [gauss[6 + i] * gauss[6 + i] for i in range(4)]
    double = 2.0 / (squares[0] + squares[1] + squares[2] + squares[3])
    qw, qx, qy, qz = gauss[6:10]
    dx, dy, dz = double * qx, double * qy, double * qz
    xx, yy, zz = dx * qx, dy * qy, dz * qz
    xy, xz, yz = dx * qy, dx * qz, dy * qz
    wx, wy, wz = dx * qw, dy * qw, dz * qw
    spin = [
        [1.0 - (yy + zz), xy - wz, xz + wy],
        [xy + wz, 1.0 - (xx + zz), yz - wx],
        [xz - wy, yz + wx, 1.0 - (xx + yy)],
    ]
    jacob = [
        [near * (rotation[0][j] - ratio_x * rotation[2][j]) for j in range(3)],
        [near * (rotation[1][j] - ratio_y * rotation[2][j]) for j in range(3)],
    ]
    turned = [[sum(jacob[a][i] * spin[i][k] for i in range(3)) for k in range(3)] for a in range(2)]
    scaled = [turned[0][k] * scales[k] for k in range(3)]
    upper = sum(scaled[k] * turned[0][k] for k in range(3)) + 0.3
    middle = sum(scaled[k] * turned[1][k] for k in range(3))
    lower = sum(turned[1][k] * scales[k] * turned[1][k] for k in range(3)) + 0.3
    over = 1.0 / (upper * lower - middle * middle)
    position = camera_centre(camera)
    toward = [centre[j] - position[j] for j in range(3)]
    reach = 1.0 / jnp.sqrt(toward[0] * toward[0] + toward[1] * toward[1] + toward[2] * toward[2])
    basis = harmonics(toward[0] * reach, toward[1] * reach, toward[2] * reach)
    return (
        screen_x,
        screen_y,
        lower * over,
        -middle * over,
        upper * over,
        viewed[2],
        inverse,
    ), basis


def halves(x):
    high = x.astype(bf16).astype(f32)
    return high, x - high


def thirds(x):
    high, rest = halves(x)
    mid, low = halves(rest)
    return jnp.concatenate([high, mid, low], axis=0).astype(bf16)


def two(x):
    high = x.astype(bf16)
    return high, (x - high.astype(f32)).astype(bf16)


def mm(a, b):
    return jnp.dot(a, b, preferred_element_type=f32)


def mm_nt(a, b):
    return lax.dot_general(a, b, (((1,), (1,)), ((), ())), preferred_element_type=f32)


def mm_tn(a, b):
    return lax.dot_general(a, b, (((0,), (0,)), ((), ())), preferred_element_type=f32)


def fold(x, count):
    rows = x.shape[0] // count
    return sum(x[rows * i : rows * (i + 1)] for i in range(count))


def pack(rows, box, shards):
    lane = lax.broadcasted_iota(jnp.int32, (8, 128), 1)
    for j in range(shards // 2):
        first = rows[0:8, 128 * j : 128 * j + 128]
        second = rows[8:16, 128 * j : 128 * j + 128]
        box[2 * j] = jnp.where(lane < 64, first, pltpu.roll(second, 64, 1))
        box[2 * j + 1] = jnp.where(lane < 64, pltpu.roll(first, 64, 1), second)


def unpack(box, shards):
    lane = lax.broadcasted_iota(jnp.int32, (8, 128), 1)
    top, bottom = [], []
    for j in range(shards // 2):
        even, odd = box[2 * j], box[2 * j + 1]
        top.append(jnp.where(lane < 64, even, pltpu.roll(odd, 64, 1)))
        bottom.append(jnp.where(lane < 64, pltpu.roll(even, 64, 1), odd))
    return jnp.concatenate([jnp.concatenate(top, 1), jnp.concatenate(bottom, 1)], 0)


def step_kernel(
    shards,
    views,
    center_y,
    params_hbm,
    camera_hbm,
    index_hbm,
    count_hbm,
    lists_hbm,
    place_hbm,
    target_hbm,
    image_ref,
    total_ref,
    held,
    camera_ref,
    index_ref,
    count_ref,
    lists_ref,
    place_ref,
    target_ref,
    wide,
    picked,
    rows,
    out_box,
    in_box,
    back_box,
    home_box,
    shared,
    others,
    pick_ref,
    list_hot,
    tri_ref,
    near_ref,
    alpha_ref,
    ratio_ref,
    sum_ref,
    part_high,
    part_low,
    weight_high,
    weight_low,
    load_sem,
    send_sem,
    recv_sem,
    send_back,
    recv_back,
    send_view,
    recv_view,
    send_index,
    recv_index,
):
    me_view = lax.axis_index("view")
    me = lax.axis_index("space")
    slots = index_ref.shape[2]
    owned = params_hbm.shape[1]
    tiles = lists_ref.shape[1]
    width = lists_ref.shape[2]
    half = width // 2
    slot_width = slots // shards

    pairs = [
        (index_hbm, index_ref),
        (params_hbm, held),
        (camera_hbm, camera_ref),
        (lists_hbm, lists_ref),
        (count_hbm, count_ref),
        (place_hbm, place_ref),
        (target_hbm, target_ref),
    ]
    loads = [
        pltpu.make_async_copy(source, there, load_sem.at[i])
        for i, (source, there) in enumerate(pairs)
    ]
    for load in loads:
        load.start()
    barrier = pltpu.get_barrier_semaphore()
    for r in range(1, shards):
        pl.semaphore_signal(
            barrier, inc=1, device_id=(me_view, lax.rem(me + r, shards)), device_id_type=MESH_ID
        )
    for r in range(1, views):
        pl.semaphore_signal(
            barrier, inc=1, device_id=(lax.rem(me_view + r, views), me), device_id_type=MESH_ID
        )

    loads[0].wait()
    count_up = lax.broadcasted_iota(jnp.int32, (32, slots), 0)

    def pick_rows(turn, wanted):
        def some(i, carry):
            at = pl.multiple_of(32 * i, 32)
            pick_ref[turn, pl.ds(at, 32)] = jnp.where(count_up + at == wanted, 1.0, 0.0).astype(
                bf16
            )
            return carry

        lax.fori_loop(0, owned // 32, some, 0, unroll=True)

    pick_rows(0, index_ref[0])
    wide[56:64] = jnp.zeros((8, owned), f32)
    for load in loads[1:]:
        load.wait()
    wide[0:59] = held[...]
    picked[...] = fold(mm(thirds(wide[...]), pick_ref[0]), 3)

    camera = [camera_ref[0, i] for i in range(12)]
    gauss = [picked[i : i + 1] for i in range(10)]

    def project_rows(values):
        outs, basis = geometry(values, camera, center_y)
        return outs, jnp.concatenate(basis, axis=0)

    (outs, basis), pull = jax.vjp(project_rows, gauss)
    opacity = 1.0 / (1.0 + jnp.exp(-picked[10:11]))
    rows[...] = jnp.zeros_like(rows)
    for i in range(5):
        rows[i : i + 1] = outs[i]
    rows[5:6] = opacity
    for c in range(3):
        rows[8 + c : 9 + c] = 0.5 + jnp.sum(
            basis * picked[11 + 16 * c : 27 + 16 * c], axis=0, keepdims=True
        )
    rows[11:12] = outs[5]
    rows[12:13] = outs[6]
    pack(rows, out_box, shards)

    pl.semaphore_wait(barrier, shards + views - 2)

    def swap(source, landing, sends, recvs):
        copies = []
        for r in range(1, shards):
            to = lax.rem(me + r, shards)
            copy = pltpu.make_async_remote_copy(
                src_ref=source.at[to],
                dst_ref=landing.at[me],
                send_sem=sends.at[r - 1],
                recv_sem=recvs.at[r - 1],
                device_id=(me_view, to),
                device_id_type=MESH_ID,
            )
            copy.start()
            copies.append(copy)
        landing[pl.ds(me, 1)] = source[pl.ds(me, 1)]
        return copies

    def tell(source, landing, sends, recvs):
        copies = []
        for r in range(1, views):
            copy = pltpu.make_async_remote_copy(
                src_ref=source,
                dst_ref=landing.at[r - 1],
                send_sem=sends.at[r - 1],
                recv_sem=recvs.at[r - 1],
                device_id=(lax.rem(me_view + r, views), me),
                device_id_type=MESH_ID,
            )
            copy.start()
            copies.append(copy)
        return copies

    copies = swap(out_box, in_box, send_sem, recv_sem)
    numbers = tell(index_ref.at[0], others, send_index, recv_index)

    def list_rows(i, carry):
        at = pl.multiple_of(32 * i, 32)
        for t in range(tiles):
            list_hot[t, pl.ds(at, 32)] = jnp.where(
                count_up + at == lists_ref[0, t : t + 1], 1.0, 0.0
            ).astype(bf16)
        return carry

    lax.fori_loop(0, slots // 32, list_rows, 0, unroll=True)
    first = lax.broadcasted_iota(jnp.int32, (half, half), 0)
    second = lax.broadcasted_iota(jnp.int32, (half, half), 1)
    tri_ref[0] = jnp.where(first < second, 1.0, 0.0).astype(bf16)
    tri_ref[1] = jnp.where(first > second, 1.0, 0.0).astype(bf16)
    tri_ref[2] = jnp.ones((half, half), bf16)
    pixel = lax.broadcasted_iota(jnp.int32, (16, 256), 1)
    kind = lax.broadcasted_iota(jnp.int32, (16, 256), 0)
    grid_x = (pixel % 16).astype(f32) - 7.5
    grid_y = (pixel // 16).astype(f32) - 7.5
    moments_of = jnp.where(kind == 0, 1.0, 0.0)
    for i, values in enumerate(
        [grid_x, grid_y, grid_x * grid_x, grid_x * grid_y, grid_y * grid_y]
    ):
        moments_of = jnp.where(kind == i + 1, values, moments_of)
    moments_of = moments_of.astype(bf16)
    side_x = lax.broadcasted_iota(jnp.int32, (16, 1), 0).astype(f32) - 7.5
    for copy in numbers:
        copy.wait()
    for turn in range(1, views // 2):
        pick_rows(turn, others[turn - 1, 0])

    for copy in copies:
        copy.wait()
    arrived = thirds(unpack(in_box, shards))

    spans = [slice(256 * t, 256 * t + 256) for t in range(tiles)]
    drawn_from = []
    for t in range(tiles):
        entries = fold(mm(arrived, list_hot[t]), 3)
        place = place_ref[0, t]
        middle_x = (place % 64 * 16 + 8).astype(f32)
        middle_y = (place // 64 * 16 + 8).astype(f32)
        u = entries[0:1] - middle_x
        y = entries[1:2] - middle_y
        a, b, c = entries[2:3], entries[3:4], entries[4:5]
        drawn_from.append((u, y, a, b, c, entries[8:16]))
        apart_x = side_x - u
        near_ref[t, 0:16] = apart_x
        near_ref[t, 16:32] = (-0.5 * a) * apart_x * apart_x
        near_ref[t, 32:33] = y
        near_ref[t, 33:34] = -b
        near_ref[t, 34:35] = -0.5 * c
        near_ref[t, 35:36] = entries[5:6]

    def light(i, carry):
        at = pl.multiple_of(16 * i, 16)
        for t in range(tiles):
            apart_y = (i.astype(f32) - 7.5) - near_ref[t, 32:33]
            line = near_ref[t, 33:34] * apart_y
            shift = near_ref[t, 34:35] * apart_y * apart_y
            quad = near_ref[t, 16:32] + line * near_ref[t, 0:16] + shift
            alpha = near_ref[t, 35:36] * jnp.exp(quad)
            through = 1.0 - alpha
            keep_high, keep_low = two(jnp.log(through))
            here = pl.ds(256 * t + at, 16)
            alpha_ref[here] = alpha
            inverse = pl.reciprocal(through, approx=True)
            ratio_ref[here] = alpha * (inverse * (2.0 - through * inverse))
            part_high[here] = keep_high
            part_low[here] = keep_low
        return carry

    lax.fori_loop(0, 16, light, 0, unroll=True)

    def ordered_sum(order):
        whole, cut = (slice(0, half), slice(half, width))
        if order:
            whole, cut = cut, whole
        sum_ref[:, whole] = mm(part_high[:, whole], tri_ref[order]) + mm(
            part_low[:, whole], tri_ref[order]
        )
        sum_ref[:, cut] = (
            mm(part_high[:, cut], tri_ref[order])
            + mm(part_low[:, cut], tri_ref[order])
            + mm(part_high[:, whole], tri_ref[2])
            + mm(part_low[:, whole], tri_ref[2])
        )

    ordered_sum(0)
    steps = 16 * tiles

    def weigh(i, carry):
        here = pl.ds(pl.multiple_of(16 * i, 16), 16)
        weight = alpha_ref[here] * jnp.exp(sum_ref[here])
        alpha_ref[here] = weight
        weight_high[here], weight_low[here] = two(weight)
        return carry

    lax.fori_loop(0, steps, weigh, 0, unroll=True)

    feat_grads = []
    for t in range(tiles):
        feat_high, feat_low = halves(drawn_from[t][5])
        feat_two = jnp.concatenate([feat_high, feat_low], 0).astype(bf16)
        drawn = fold(
            mm_nt(feat_two, weight_high[spans[t]]) + mm_nt(feat_two, weight_low[spans[t]]), 2
        )
        for ch in range(5):
            image_ref[ch, :, spans[t]] = drawn[ch : ch + 1]
        shown = jnp.concatenate(
            [target_ref[ch, :, spans[t]] for ch in range(5)] + [jnp.zeros((3, 256), f32)], 0
        )
        res_high, res_low = halves(drawn - shown)
        res_two = jnp.concatenate([res_high, res_low], 0)
        sum_ref[spans[t]] = mm_tn(
            jnp.concatenate([res_two, res_two], 0).astype(bf16),
            jnp.concatenate([feat_high, feat_high, feat_low, feat_low], 0).astype(bf16),
        )
        res_two = res_two.astype(bf16)
        feat_grads.append(
            fold(mm(res_two, weight_high[spans[t]]) + mm(res_two, weight_low[spans[t]]), 2)
        )

    def pull_back(i, carry):
        here = pl.ds(pl.multiple_of(16 * i, 16), 16)
        part = alpha_ref[here] * sum_ref[here]
        alpha_ref[here] = part
        part_high[here], part_low[here] = two(part)
        return carry

    lax.fori_loop(0, steps, pull_back, 0, unroll=True)
    ordered_sum(1)

    def slope_of(i, carry):
        here = pl.ds(pl.multiple_of(16 * i, 16), 16)
        part_high[here], part_low[here] = two(alpha_ref[here] - sum_ref[here] * ratio_ref[here])
        return carry

    lax.fori_loop(0, steps, slope_of, 0, unroll=True)

    returning = jnp.zeros((16, slots), f32)
    for t in range(tiles):
        u, y, a, b, c, _ = drawn_from[t]
        moments = mm(moments_of, part_high[spans[t]]) + mm(moments_of, part_low[spans[t]])
        m, mx, my, mxx, mxy, myy = [moments[i : i + 1] for i in range(6)]
        sx = mx - u * m
        sy = my - y * m
        sxx = mxx - u * mx - u * sx
        sxy = mxy - u * my - y * sx
        syy = myy - y * my - y * sy
        zero = jnp.zeros((2, width), f32)
        entry_grad = jnp.concatenate(
            [
                a * sx + b * sy,
                b * sx + c * sy,
                -0.5 * sxx,
                -sxy,
                -0.5 * syy,
                m,
                zero,
                feat_grads[t],
            ],
            0,
        )
        returning = returning + fold(mm_nt(thirds(entry_grad), list_hot[t]), 3)

    rows[...] = returning
    pack(rows, back_box, shards)
    copies = swap(back_box, home_box, send_back, recv_back)
    lane = lax.broadcasted_iota(jnp.int32, (1, slots), 1)
    used = jnp.zeros((1, slots), f32)
    for d in range(shards):
        begin = slot_width * d
        inside = (lane >= begin) & (lane < begin + count_ref[0, 0, d])
        used = jnp.where(inside, 1.0, used)
    for turn in range(views // 2, views):
        pick_rows(turn, others[turn - 1, 0])
    for copy in copies:
        copy.wait()

    rows[...] = unpack(home_box, shards)
    spread = sum(
        picked[11 + 16 * c : 27 + 16 * c] * rows[8 + c : 9 + c] for c in range(3)
    )
    cotangents = tuple(rows[i : i + 1] for i in range(5)) + (rows[11:12], rows[12:13])
    (gauss_grad,) = pull((cotangents, spread))
    logit_grad = rows[5:6] * (1.0 - opacity)
    colour_grad = rows[8:11]
    for i in range(10):
        rows[i : i + 1] = gauss_grad[i]
    rows[10:11] = logit_grad
    rows[11:14] = colour_grad
    rows[14:15] = used
    position = camera_centre(camera)
    rows[15:16] = jnp.where(lane == 0, position[0], jnp.where(lane == 1, position[1], position[2]))
    copies = tell(rows, shared, send_view, recv_view)

    def at_home(sent, turn):
        own = fold(mm_nt(thirds(sent), pick_ref[turn]), 3)
        seen = own[14:15]
        return own, [seen * sent[15:16, j : j + 1] for j in range(3)]

    total, centre = at_home(rows[...], 0)
    for r in range(1, views):
        copies[r - 1].wait()
        own, placed = at_home(shared[r - 1], r)
        total = total + own
        centre = [centre[j] + placed[j] for j in range(3)]
    total_ref[0:16] = total
    for j in range(3):
        total_ref[15 + j : 16 + j] = centre[j]
    total_ref[18:24] = jnp.zeros((6, owned), f32)


def update_kernel(
    params_ref,
    first_ref,
    second_ref,
    visible_ref,
    total_ref,
    drawn_ref,
    image_ref,
    out_params,
    out_first,
    out_second,
    grad,
):
    image_ref[...] = drawn_ref[...]
    seen = total_ref[14:15] > 0.0
    toward = [params_ref[j : j + 1] - total_ref[15 + j : 16 + j] for j in range(3)]
    square = toward[0] * toward[0] + toward[1] * toward[1] + toward[2] * toward[2]
    reach = 1.0 / jnp.sqrt(jnp.where(seen, square, 1.0))
    basis = jnp.concatenate(harmonics(toward[0] * reach, toward[1] * reach, toward[2] * reach), 0)
    basis = jnp.where(seen, basis, 0.0)
    grad[0:11] = total_ref[0:11]
    for c in range(3):
        grad[11 + 16 * c : 27 + 16 * c] = basis * total_ref[11 + c : 12 + c]
    values = grad[0:59]
    params, adam_m, adam_v = params_ref[...], first_ref[...], second_ref[...]
    moment_one = beta_one * adam_m + (1.0 - beta_one) * values
    moment_two = beta_two * adam_v + (1.0 - beta_two) * values * values
    scale_one = learn_rate / (1.0 - beta_one**adam_step)
    scale_two = 1.0 / (1.0 - beta_two**adam_step)
    stepped = params - scale_one * moment_one / (jnp.sqrt(moment_two * scale_two) + adam_eps)
    keep = visible_ref[...] > 0
    out_params[...] = jnp.where(keep, stepped, params)
    out_first[...] = jnp.where(keep, moment_one, adam_m)
    out_second[...] = jnp.where(keep, moment_two, adam_v)


def body(
    params, adam_m, adam_v, visible, cameras, send_index, send_count, tile_lists, tile_pos, target
):
    shards = lax.axis_size("space")
    views = lax.axis_size("view")
    tiles, width = tile_lists.shape[1:]
    slots = send_index.shape[2]
    nparam, owned = params.shape
    if slots != 64 * shards or shards % 2 or nparam != 59:
        return plain_body(
            params,
            adam_m,
            adam_v,
            visible,
            cameras,
            send_index,
            send_count,
            tile_lists,
            tile_pos,
            target,
        )
    center_y = 8.0 * (tiles * shards) / 64.0
    target = jnp.transpose(target, (1, 0, 2))
    vmem = pl.BlockSpec(memory_space=pltpu.VMEM)
    box = pltpu.VMEM((shards, 8, 128), f32)
    image, total = pl.pallas_call(
        functools.partial(step_kernel, shards, views, center_y),
        out_shape=(
            pltpu.VMEM(target.shape, f32),
            pltpu.VMEM((24, owned), f32),
        ),
        in_specs=[pl.BlockSpec(memory_space=pl.ANY)] * 7,
        out_specs=(vmem, vmem),
        scratch_shapes=[
            pltpu.VMEM((nparam, owned), f32),
            pltpu.SMEM(cameras.shape, f32),
            pltpu.VMEM(send_index.shape, jnp.int32),
            pltpu.SMEM(send_count.shape, jnp.int32),
            pltpu.VMEM(tile_lists.shape, jnp.int32),
            pltpu.SMEM(tile_pos.shape, jnp.int32),
            pltpu.VMEM(target.shape, f32),
            pltpu.VMEM((64, owned), f32),
            pltpu.VMEM((64, slots), f32),
            pltpu.VMEM((16, slots), f32),
            box,
            box,
            box,
            box,
            pltpu.VMEM((views - 1, 16, slots), f32),
            pltpu.VMEM((views - 1,) + send_index.shape[1:], jnp.int32),
            pltpu.VMEM((views, owned, slots), bf16),
            pltpu.VMEM((tiles, slots, width), bf16),
            pltpu.VMEM((3, width // 2, width // 2), bf16),
            pltpu.VMEM((tiles, 40, width), f32),
            pltpu.VMEM((tiles * 256, width), f32),
            pltpu.VMEM((tiles * 256, width), f32),
            pltpu.VMEM((tiles * 256, width), f32),
            pltpu.VMEM((tiles * 256, width), bf16),
            pltpu.VMEM((tiles * 256, width), bf16),
            pltpu.VMEM((tiles * 256, width), bf16),
            pltpu.VMEM((tiles * 256, width), bf16),
            pltpu.SemaphoreType.DMA((7,)),
            pltpu.SemaphoreType.DMA((shards - 1,)),
            pltpu.SemaphoreType.DMA((shards - 1,)),
            pltpu.SemaphoreType.DMA((shards - 1,)),
            pltpu.SemaphoreType.DMA((shards - 1,)),
            pltpu.SemaphoreType.DMA((views - 1,)),
            pltpu.SemaphoreType.DMA((views - 1,)),
            pltpu.SemaphoreType.DMA((views - 1,)),
            pltpu.SemaphoreType.DMA((views - 1,)),
        ],
        compiler_params=pltpu.CompilerParams(
            collective_id=0, has_side_effects=True, vmem_limit_bytes=56 * 1024 * 1024
        ),
        cost_estimate=pl.CostEstimate(
            flops=16 * 10**9, bytes_accessed=8 * 10**6, transcendentals=10**6
        ),
        name="step",
    )(params, cameras, send_index, send_count, tile_lists, tile_pos, target)
    like = jax.ShapeDtypeStruct(params.shape, f32)
    image, *updated = pl.pallas_call(
        update_kernel,
        out_shape=(jax.ShapeDtypeStruct(target.shape, f32), like, like, like),
        in_specs=[vmem] * 6,
        out_specs=(vmem,) * 4,
        scratch_shapes=[pltpu.VMEM((64, owned), f32)],
        compiler_params=pltpu.CompilerParams(vmem_limit_bytes=16 * 1024 * 1024),
        name="update",
    )(params, adam_m, adam_v, visible.reshape(1, owned), total, image)
    return jnp.transpose(image, (1, 0, 2)), *updated


def solution(mesh):
    placed = (
        P(None, "space"),
        P(None, "space"),
        P(None, "space"),
        P("space"),
        P("view", None),
        P("view", "space", None),
        P("view", "space", None),
        P("view", "space", None),
        P("view", "space"),
        P("view", None, "space"),
    )
    return jax.shard_map(
        body,
        mesh=mesh,
        in_specs=placed,
        out_specs=(P("view", None, "space"), P(None, "space"), P(None, "space"), P(None, "space")),
        check_vma=False,
    )
```

```python
import functools

import jax
import jax.numpy as jnp
from jax import lax
from jax.experimental import pallas as pl
from jax.experimental.pallas import tpu as pltpu
from jax.sharding import PartitionSpec as P

focal_len = 1000.0
center_x = 512.0
harm_zero = 0.28209479177387814
harm_one = 0.4886025119029199
harm_two = (
    1.0925484305920792,
    -1.0925484305920792,
    0.31539156525252005,
    -1.0925484305920792,
    0.5462742152960396,
)
harm_three = (
    -0.5900435899266435,
    2.890611442640554,
    -0.4570457994644658,
    0.3731763325901154,
    -0.4570457994644658,
    1.445305721320277,
    -0.5900435899266435,
)
beta_one = 0.9
beta_two = 0.99
learn_rate = 0.05
adam_eps = 1e-08
adam_step = 100.0


def project(gauss, camera, center_y):
    rotation = [[camera[3 * i + j] for j in range(3)] for i in range(3)]
    offset = [camera[9 + i] for i in range(3)]
    centre = [gauss[i] for i in range(3)]
    viewed = [sum((rotation[i][j] * centre[j] for j in range(3))) + offset[i] for i in range(3)]
    inverse = 1.0 / viewed[2]
    screen_x = focal_len * viewed[0] * inverse + center_x
    screen_y = focal_len * viewed[1] * inverse + center_y
    scales = [jnp.exp(gauss[3 + i]) for i in range(3)]
    length = jnp.sqrt(
        gauss[6] * gauss[6] + gauss[7] * gauss[7] + gauss[8] * gauss[8] + gauss[9] * gauss[9]
    )
    quat_w, quat_x, quat_y, quat_z = [gauss[6 + i] / length for i in range(4)]
    spin = [
        [
            1.0 - 2.0 * (quat_y * quat_y + quat_z * quat_z),
            2.0 * (quat_x * quat_y - quat_w * quat_z),
            2.0 * (quat_x * quat_z + quat_w * quat_y),
        ],
        [
            2.0 * (quat_x * quat_y + quat_w * quat_z),
            1.0 - 2.0 * (quat_x * quat_x + quat_z * quat_z),
            2.0 * (quat_y * quat_z - quat_w * quat_x),
        ],
        [
            2.0 * (quat_x * quat_z - quat_w * quat_y),
            2.0 * (quat_y * quat_z + quat_w * quat_x),
            1.0 - 2.0 * (quat_x * quat_x + quat_y * quat_y),
        ],
    ]
    factor = [[spin[i][j] * scales[j] for j in range(3)] for i in range(3)]
    sigma = [
        [sum((factor[i][j] * factor[k][j] for j in range(3))) for k in range(3)] for i in range(3)
    ]
    near = focal_len * inverse
    lean_x = -focal_len * viewed[0] * inverse * inverse
    lean_y = -focal_len * viewed[1] * inverse * inverse
    jacob = [
        [near * rotation[0][j] + lean_x * rotation[2][j] for j in range(3)],
        [near * rotation[1][j] + lean_y * rotation[2][j] for j in range(3)],
    ]
    halfway = [
        [sum((jacob[a][i] * sigma[i][k] for i in range(3))) for k in range(3)] for a in range(2)
    ]
    upper = sum((halfway[0][k] * jacob[0][k] for k in range(3))) + 0.3
    middle = sum((halfway[0][k] * jacob[1][k] for k in range(3)))
    lower = sum((halfway[1][k] * jacob[1][k] for k in range(3))) + 0.3
    determinant = upper * lower - middle * middle
    conic_a = lower / determinant
    conic_b = -middle / determinant
    conic_c = upper / determinant
    opacity = jax.nn.sigmoid(gauss[10])
    camera_pos = [-sum((rotation[i][j] * offset[i] for i in range(3))) for j in range(3)]
    toward = [centre[j] - camera_pos[j] for j in range(3)]
    reach = jnp.sqrt(toward[0] * toward[0] + toward[1] * toward[1] + toward[2] * toward[2])
    unit_x = toward[0] / reach
    unit_y = toward[1] / reach
    unit_z = toward[2] / reach
    square_x = unit_x * unit_x
    square_y = unit_y * unit_y
    square_z = unit_z * unit_z
    basis = [
        harm_zero + 0.0 * unit_x,
        -harm_one * unit_y,
        harm_one * unit_z,
        -harm_one * unit_x,
        harm_two[0] * unit_x * unit_y,
        harm_two[1] * unit_y * unit_z,
        harm_two[2] * (2.0 * square_z - square_x - square_y),
        harm_two[3] * unit_x * unit_z,
        harm_two[4] * (square_x - square_y),
        harm_three[0] * unit_y * (3.0 * square_x - square_y),
        harm_three[1] * unit_x * unit_y * unit_z,
        harm_three[2] * unit_y * (4.0 * square_z - square_x - square_y),
        harm_three[3] * unit_z * (2.0 * square_z - 3.0 * square_x - 3.0 * square_y),
        harm_three[4] * unit_x * (4.0 * square_z - square_x - square_y),
        harm_three[5] * unit_z * (square_x - square_y),
        harm_three[6] * unit_x * (square_x - 3.0 * square_y),
    ]
    colors = [0.5 + sum((basis[k] * gauss[11 + 16 * c + k] for k in range(16))) for c in range(3)]
    return jnp.stack(
        [
            screen_x,
            screen_y,
            conic_a,
            conic_b,
            conic_c,
            opacity,
            colors[0],
            colors[1],
            colors[2],
            viewed[2],
            inverse,
        ]
    )


def shade_tile(entries, valid, tile):
    lane = jnp.arange(256, dtype=jnp.int32)
    column = tile % 64 * 16 + lane % 16
    height = tile // 64 * 16 + lane // 16
    pixel_x = column.astype(entries.dtype) + 0.5
    pixel_y = height.astype(entries.dtype) + 0.5
    apart_x = pixel_x[:, None] - entries[0][None, :]
    apart_y = pixel_y[:, None] - entries[1][None, :]
    quad = (
        entries[2][None, :] * apart_x * apart_x
        + 2.0 * entries[3][None, :] * apart_x * apart_y
        + entries[4][None, :] * apart_y * apart_y
    )
    alpha = entries[5][None, :] * jnp.exp(-0.5 * quad) * valid[None, :]
    keeping = jnp.log1p(-alpha)
    weight = alpha * jnp.exp(jnp.cumsum(keeping, axis=1) - keeping)
    feats = entries[6:11]
    return lax.dot_general(feats, weight, (((1,), (1,)), ((), ())), precision=lax.Precision.HIGHEST)


def adam_update(params, adam_m, adam_v, grad, visible):
    moment_one = beta_one * adam_m + (1.0 - beta_one) * grad
    moment_two = beta_two * adam_v + (1.0 - beta_two) * grad * grad
    first_hat = moment_one / (1.0 - beta_one**adam_step)
    second_hat = moment_two / (1.0 - beta_two**adam_step)
    stepped = params - learn_rate * first_hat / (jnp.sqrt(second_hat) + adam_eps)
    keep = (visible > 0)[None, :]
    return (
        jnp.where(keep, stepped, params),
        jnp.where(keep, moment_one, adam_m),
        jnp.where(keep, moment_two, adam_v),
    )


def composite(buffer, block_entries, block_usable, block_places):

    def one_block(item):
        entries, usable, places = item
        return jax.vmap(shade_tile, in_axes=(1, 0, 0))(buffer[:, entries], usable, places)

    return lax.map(jax.checkpoint(one_block), (block_entries, block_usable, block_places))


def plain_body(
    params, adam_m, adam_v, visible, cameras, send_index, send_count, tile_lists, tile_pos, target
):
    shards = lax.axis_size("space")
    tile_count = tile_lists.shape[1]
    list_width = tile_lists.shape[2]
    center_y = 8.0 * (tile_count * shards) / 64.0
    camera = cameras[0]
    route = send_index[0, 0]
    slot_width = route.shape[0] // shards
    slot_grid = jnp.arange(route.shape[0], dtype=jnp.int32).reshape(shards, slot_width) % slot_width
    in_use = (slot_grid < send_count[0, 0][:, None]).reshape(-1).astype(jnp.float32)

    def outgoing(gauss):
        return project(gauss, camera, center_y)[:, route] * in_use[None, :]

    sending, pull_send = jax.vjp(outgoing, params)
    arrived = lax.all_to_all(sending, "space", split_axis=1, concat_axis=1, tiled=True)
    per_block = 2
    block_count = tile_count // per_block
    lists = tile_lists[0]
    block_usable = (lists >= 0).astype(jnp.float32).reshape(block_count, per_block, list_width)
    block_entries = jnp.maximum(lists, 0).reshape(block_count, per_block, list_width)
    block_places = tile_pos[0].reshape(block_count, per_block)

    def draw_tiles(buffer):
        return composite(buffer, block_entries, block_usable, block_places).reshape(
            tile_count, 5, 256
        )

    tiles, pull_tiles = jax.vjp(draw_tiles, arrived)
    image = jnp.transpose(tiles, (1, 0, 2)).reshape(5, tile_count * 256)
    residue = (image - target[0]).reshape(5, tile_count, 256)
    (record_grad,) = pull_tiles(jnp.transpose(residue, (1, 0, 2)))
    returned = lax.all_to_all(record_grad, "space", split_axis=1, concat_axis=1, tiled=True)
    (grad,) = pull_send(returned)
    total = lax.psum(grad, "view")
    new_params, new_m, new_v = adam_update(params, adam_m, adam_v, total, visible)
    return (image[None], new_params, new_m, new_v)


f32 = jnp.float32
bf16 = jnp.bfloat16
MESH_ID = pl.DeviceIdType.MESH


def harmonics(unit_x, unit_y, unit_z):
    square_x = unit_x * unit_x
    square_y = unit_y * unit_y
    square_z = unit_z * unit_z
    return [
        jnp.full_like(unit_x, harm_zero),
        -harm_one * unit_y,
        harm_one * unit_z,
        -harm_one * unit_x,
        harm_two[0] * unit_x * unit_y,
        harm_two[1] * unit_y * unit_z,
        harm_two[2] * (2.0 * square_z - square_x - square_y),
        harm_two[3] * unit_x * unit_z,
        harm_two[4] * (square_x - square_y),
        harm_three[0] * unit_y * (3.0 * square_x - square_y),
        harm_three[1] * unit_x * unit_y * unit_z,
        harm_three[2] * unit_y * (4.0 * square_z - square_x - square_y),
        harm_three[3] * unit_z * (2.0 * square_z - 3.0 * square_x - 3.0 * square_y),
        harm_three[4] * unit_x * (4.0 * square_z - square_x - square_y),
        harm_three[5] * unit_z * (square_x - square_y),
        harm_three[6] * unit_x * (square_x - 3.0 * square_y),
    ]


def camera_centre(camera):
    return [-sum(camera[3 * i + j] * camera[9 + i] for i in range(3)) for j in range(3)]


def geometry(gauss, camera, center_y):
    rotation = [[camera[3 * i + j] for j in range(3)] for i in range(3)]
    offset = [camera[9 + i] for i in range(3)]
    centre = gauss[0:3]
    viewed = [sum(rotation[i][j] * centre[j] for j in range(3)) + offset[i] for i in range(3)]
    inverse = 1.0 / viewed[2]
    near = focal_len * inverse
    ratio_x = viewed[0] * inverse
    ratio_y = viewed[1] * inverse
    screen_x = focal_len * ratio_x + center_x
    screen_y = focal_len * ratio_y + center_y
    scales = [jnp.exp(2.0 * gauss[3 + i]) for i in range(3)]
    squares = [gauss[6 + i] * gauss[6 + i] for i in range(4)]
    double = 2.0 / (squares[0] + squares[1] + squares[2] + squares[3])
    qw, qx, qy, qz = gauss[6:10]
    dx, dy, dz = double * qx, double * qy, double * qz
    xx, yy, zz = dx * qx, dy * qy, dz * qz
    xy, xz, yz = dx * qy, dx * qz, dy * qz
    wx, wy, wz = dx * qw, dy * qw, dz * qw
    spin = [
        [1.0 - (yy + zz), xy - wz, xz + wy],
        [xy + wz, 1.0 - (xx + zz), yz - wx],
        [xz - wy, yz + wx, 1.0 - (xx + yy)],
    ]
    jacob = [
        [near * (rotation[0][j] - ratio_x * rotation[2][j]) for j in range(3)],
        [near * (rotation[1][j] - ratio_y * rotation[2][j]) for j in range(3)],
    ]
    turned = [[sum(jacob[a][i] * spin[i][k] for i in range(3)) for k in range(3)] for a in range(2)]
    scaled = [turned[0][k] * scales[k] for k in range(3)]
    upper = sum(scaled[k] * turned[0][k] for k in range(3)) + 0.3
    middle = sum(scaled[k] * turned[1][k] for k in range(3))
    lower = sum(turned[1][k] * scales[k] * turned[1][k] for k in range(3)) + 0.3
    over = 1.0 / (upper * lower - middle * middle)
    position = camera_centre(camera)
    toward = [centre[j] - position[j] for j in range(3)]
    reach = 1.0 / jnp.sqrt(toward[0] * toward[0] + toward[1] * toward[1] + toward[2] * toward[2])
    basis = harmonics(toward[0] * reach, toward[1] * reach, toward[2] * reach)
    return (
        screen_x,
        screen_y,
        lower * over,
        -middle * over,
        upper * over,
        viewed[2],
        inverse,
    ), basis


def halves(x):
    high = x.astype(bf16).astype(f32)
    return high, x - high


def thirds(x):
    high, rest = halves(x)
    mid, low = halves(rest)
    return jnp.concatenate([high, mid, low], axis=0).astype(bf16)


def two(x):
    high = x.astype(bf16)
    return high, (x - high.astype(f32)).astype(bf16)


def mm(a, b):
    return jnp.dot(a, b, preferred_element_type=f32)


def mm_nt(a, b):
    return lax.dot_general(a, b, (((1,), (1,)), ((), ())), preferred_element_type=f32)


def mm_tn(a, b):
    return lax.dot_general(a, b, (((0,), (0,)), ((), ())), preferred_element_type=f32)


def fold(x, count):
    rows = x.shape[0] // count
    return sum(x[rows * i : rows * (i + 1)] for i in range(count))


def pack(rows, box, shards):
    lane = lax.broadcasted_iota(jnp.int32, (8, 128), 1)
    for j in range(shards // 2):
        first = rows[0:8, 128 * j : 128 * j + 128]
        second = rows[8:16, 128 * j : 128 * j + 128]
        box[2 * j] = jnp.where(lane < 64, first, pltpu.roll(second, 64, 1))
        box[2 * j + 1] = jnp.where(lane < 64, pltpu.roll(first, 64, 1), second)


def unpack(box, shards):
    lane = lax.broadcasted_iota(jnp.int32, (8, 128), 1)
    top, bottom = [], []
    for j in range(shards // 2):
        even, odd = box[2 * j], box[2 * j + 1]
        top.append(jnp.where(lane < 64, even, pltpu.roll(odd, 64, 1)))
        bottom.append(jnp.where(lane < 64, pltpu.roll(even, 64, 1), odd))
    return jnp.concatenate([jnp.concatenate(top, 1), jnp.concatenate(bottom, 1)], 0)


def step_kernel(
    shards,
    views,
    center_y,
    params_hbm,
    camera_hbm,
    index_hbm,
    count_hbm,
    lists_hbm,
    place_hbm,
    target_hbm,
    image_ref,
    total_ref,
    held,
    camera_ref,
    index_ref,
    count_ref,
    lists_ref,
    place_ref,
    target_ref,
    wide,
    picked,
    rows,
    out_box,
    in_box,
    back_box,
    home_box,
    shared,
    others,
    pick_ref,
    list_hot,
    tri_ref,
    near_ref,
    alpha_ref,
    ratio_ref,
    sum_ref,
    part_high,
    part_low,
    weight_high,
    weight_low,
    load_sem,
    send_sem,
    recv_sem,
    send_back,
    recv_back,
    send_view,
    recv_view,
    send_index,
    recv_index,
):
    me_view = lax.axis_index("view")
    me = lax.axis_index("space")
    slots = index_ref.shape[2]
    owned = params_hbm.shape[1]
    tiles = lists_ref.shape[1]
    width = lists_ref.shape[2]
    half = width // 2
    slot_width = slots // shards

    pairs = [
        (index_hbm, index_ref),
        (params_hbm, held),
        (camera_hbm, camera_ref),
        (lists_hbm, lists_ref),
        (count_hbm, count_ref),
        (place_hbm, place_ref),
        (target_hbm, target_ref),
    ]
    loads = [
        pltpu.make_async_copy(source, there, load_sem.at[i])
        for i, (source, there) in enumerate(pairs)
    ]
    for load in loads:
        load.start()
    barrier = pltpu.get_barrier_semaphore()
    for r in range(1, shards):
        pl.semaphore_signal(
            barrier, inc=1, device_id=(me_view, lax.rem(me + r, shards)), device_id_type=MESH_ID
        )
    for r in range(1, views):
        pl.semaphore_signal(
            barrier, inc=1, device_id=(lax.rem(me_view + r, views), me), device_id_type=MESH_ID
        )

    loads[0].wait()
    count_up = lax.broadcasted_iota(jnp.int32, (32, slots), 0)

    def pick_rows(turn, wanted):
        def some(i, carry):
            at = pl.multiple_of(32 * i, 32)
            pick_ref[turn, pl.ds(at, 32)] = jnp.where(count_up + at == wanted, 1.0, 0.0).astype(
                bf16
            )
            return carry

        lax.fori_loop(0, owned // 32, some, 0, unroll=True)

    pick_rows(0, index_ref[0])
    wide[56:64] = jnp.zeros((8, owned), f32)
    for load in loads[1:]:
        load.wait()
    wide[0:59] = held[...]
    picked[...] = fold(mm(thirds(wide[...]), pick_ref[0]), 3)

    camera = [camera_ref[0, i] for i in range(12)]
    gauss = [picked[i : i + 1] for i in range(10)]

    def project_rows(values):
        outs, basis = geometry(values, camera, center_y)
        return outs, jnp.concatenate(basis, axis=0)

    outs, basis = project_rows(gauss)
    opacity = 1.0 / (1.0 + jnp.exp(-picked[10:11]))
    rows[...] = jnp.zeros_like(rows)
    for i in range(5):
        rows[i : i + 1] = outs[i]
    rows[5:6] = opacity
    for c in range(3):
        rows[8 + c : 9 + c] = 0.5 + jnp.sum(
            basis * picked[11 + 16 * c : 27 + 16 * c], axis=0, keepdims=True
        )
    rows[11:12] = outs[5]
    rows[12:13] = outs[6]
    pack(rows, out_box, shards)

    pl.semaphore_wait(barrier, shards + views - 2)

    def swap(source, landing, sends, recvs):
        copies = []
        for r in range(1, shards):
            to = lax.rem(me + r, shards)
            copy = pltpu.make_async_remote_copy(
                src_ref=source.at[to],
                dst_ref=landing.at[me],
                send_sem=sends.at[r - 1],
                recv_sem=recvs.at[r - 1],
                device_id=(me_view, to),
                device_id_type=MESH_ID,
            )
            copy.start()
            copies.append(copy)
        landing[pl.ds(me, 1)] = source[pl.ds(me, 1)]
        return copies

    def tell(source, landing, sends, recvs):
        copies = []
        for r in range(1, views):
            copy = pltpu.make_async_remote_copy(
                src_ref=source,
                dst_ref=landing.at[r - 1],
                send_sem=sends.at[r - 1],
                recv_sem=recvs.at[r - 1],
                device_id=(lax.rem(me_view + r, views), me),
                device_id_type=MESH_ID,
            )
            copy.start()
            copies.append(copy)
        return copies

    copies = swap(out_box, in_box, send_sem, recv_sem)
    numbers = tell(index_ref.at[0], others, send_index, recv_index)

    _, pull = jax.vjp(project_rows, gauss)
    def list_rows(i, carry):
        at = pl.multiple_of(32 * i, 32)
        for t in range(tiles):
            list_hot[t, pl.ds(at, 32)] = jnp.where(
                count_up + at == lists_ref[0, t : t + 1], 1.0, 0.0
            ).astype(bf16)
        return carry

    lax.fori_loop(0, slots // 32, list_rows, 0, unroll=True)
    first = lax.broadcasted_iota(jnp.int32, (half, half), 0)
    second = lax.broadcasted_iota(jnp.int32, (half, half), 1)
    tri_ref[0] = jnp.where(first < second, 1.0, 0.0).astype(bf16)
    tri_ref[1] = jnp.where(first > second, 1.0, 0.0).astype(bf16)
    tri_ref[2] = jnp.ones((half, half), bf16)
    pixel = lax.broadcasted_iota(jnp.int32, (16, 256), 1)
    kind = lax.broadcasted_iota(jnp.int32, (16, 256), 0)
    grid_x = (pixel % 16).astype(f32) - 7.5
    grid_y = (pixel // 16).astype(f32) - 7.5
    moments_of = jnp.where(kind == 0, 1.0, 0.0)
    for i, values in enumerate(
        [grid_x, grid_y, grid_x * grid_x, grid_x * grid_y, grid_y * grid_y]
    ):
        moments_of = jnp.where(kind == i + 1, values, moments_of)
    moments_of = moments_of.astype(bf16)
    side_x = lax.broadcasted_iota(jnp.int32, (16, 1), 0).astype(f32) - 7.5
    for copy in numbers:
        copy.wait()
    for turn in range(1, views // 2):
        pick_rows(turn, others[turn - 1, 0])

    for copy in copies:
        copy.wait()
    arrived = thirds(unpack(in_box, shards))

    spans = [slice(256 * t, 256 * t + 256) for t in range(tiles)]
    drawn_from = []
    for t in range(tiles):
        entries = fold(mm(arrived, list_hot[t]), 3)
        place = place_ref[0, t]
        middle_x = (place % 64 * 16 + 8).astype(f32)
        middle_y = (place // 64 * 16 + 8).astype(f32)
        u = entries[0:1] - middle_x
        y = entries[1:2] - middle_y
        a, b, c = entries[2:3], entries[3:4], entries[4:5]
        drawn_from.append((u, y, a, b, c, entries[8:16]))
        apart_x = side_x - u
        near_ref[t, 0:16] = apart_x
        near_ref[t, 16:32] = (-0.5 * a) * apart_x * apart_x
        near_ref[t, 32:33] = y
        near_ref[t, 33:34] = -b
        near_ref[t, 34:35] = -0.5 * c
        near_ref[t, 35:36] = entries[5:6]

    def light(i, carry):
        at = pl.multiple_of(16 * i, 16)
        for t in range(tiles):
            apart_y = (i.astype(f32) - 7.5) - near_ref[t, 32:33]
            line = near_ref[t, 33:34] * apart_y
            shift = near_ref[t, 34:35] * apart_y * apart_y
            quad = near_ref[t, 16:32] + line * near_ref[t, 0:16] + shift
            alpha = near_ref[t, 35:36] * jnp.exp(quad)
            through = 1.0 - alpha
            keep_high, keep_low = two(jnp.log(through))
            here = pl.ds(256 * t + at, 16)
            alpha_ref[here] = alpha
            inverse = pl.reciprocal(through, approx=True)
            ratio_ref[here] = alpha * (inverse * (2.0 - through * inverse))
            part_high[here] = keep_high
            part_low[here] = keep_low
        return carry

    lax.fori_loop(0, 16, light, 0, unroll=True)

    def ordered_sum(order):
        whole, cut = (slice(0, half), slice(half, width))
        if order:
            whole, cut = cut, whole
        sum_ref[:, whole] = mm(part_high[:, whole], tri_ref[order]) + mm(
            part_low[:, whole], tri_ref[order]
        )
        sum_ref[:, cut] = (
            mm(part_high[:, cut], tri_ref[order])
            + mm(part_low[:, cut], tri_ref[order])
            + mm(part_high[:, whole], tri_ref[2])
            + mm(part_low[:, whole], tri_ref[2])
        )

    ordered_sum(0)
    steps = 16 * tiles

    def weigh(i, carry):
        here = pl.ds(pl.multiple_of(16 * i, 16), 16)
        weight = alpha_ref[here] * jnp.exp(sum_ref[here])
        alpha_ref[here] = weight
        weight_high[here], weight_low[here] = two(weight)
        return carry

    lax.fori_loop(0, steps, weigh, 0, unroll=True)

    feat_grads = []
    for t in range(tiles):
        feat_high, feat_low = halves(drawn_from[t][5])
        feat_two = jnp.concatenate([feat_high, feat_low], 0).astype(bf16)
        drawn = fold(
            mm_nt(feat_two, weight_high[spans[t]]) + mm_nt(feat_two, weight_low[spans[t]]), 2
        )
        for ch in range(5):
            image_ref[ch, :, spans[t]] = drawn[ch : ch + 1]
        shown = jnp.concatenate(
            [target_ref[ch, :, spans[t]] for ch in range(5)] + [jnp.zeros((3, 256), f32)], 0
        )
        res_high, res_low = halves(drawn - shown)
        res_two = jnp.concatenate([res_high, res_low], 0)
        sum_ref[spans[t]] = mm_tn(
            jnp.concatenate([res_two, res_two], 0).astype(bf16),
            jnp.concatenate([feat_high, feat_high, feat_low, feat_low], 0).astype(bf16),
        )
        res_two = res_two.astype(bf16)
        feat_grads.append(
            fold(mm(res_two, weight_high[spans[t]]) + mm(res_two, weight_low[spans[t]]), 2)
        )

    def pull_back(i, carry):
        here = pl.ds(pl.multiple_of(16 * i, 16), 16)
        part = alpha_ref[here] * sum_ref[here]
        alpha_ref[here] = part
        part_high[here], part_low[here] = two(part)
        return carry

    lax.fori_loop(0, steps, pull_back, 0, unroll=True)
    ordered_sum(1)

    def slope_of(i, carry):
        here = pl.ds(pl.multiple_of(16 * i, 16), 16)
        part_high[here], part_low[here] = two(alpha_ref[here] - sum_ref[here] * ratio_ref[here])
        return carry

    lax.fori_loop(0, steps, slope_of, 0, unroll=True)

    returning = jnp.zeros((16, slots), f32)
    for t in range(tiles):
        u, y, a, b, c, _ = drawn_from[t]
        moments = mm(moments_of, part_high[spans[t]]) + mm(moments_of, part_low[spans[t]])
        m, mx, my, mxx, mxy, myy = [moments[i : i + 1] for i in range(6)]
        sx = mx - u * m
        sy = my - y * m
        sxx = mxx - u * mx - u * sx
        sxy = mxy - u * my - y * sx
        syy = myy - y * my - y * sy
        zero = jnp.zeros((2, width), f32)
        entry_grad = jnp.concatenate(
            [
                a * sx + b * sy,
                b * sx + c * sy,
                -0.5 * sxx,
                -sxy,
                -0.5 * syy,
                m,
                zero,
                feat_grads[t],
            ],
            0,
        )
        returning = returning + fold(mm_nt(thirds(entry_grad), list_hot[t]), 3)

    rows[...] = returning
    pack(rows, back_box, shards)
    copies = swap(back_box, home_box, send_back, recv_back)
    lane = lax.broadcasted_iota(jnp.int32, (1, slots), 1)
    used = jnp.zeros((1, slots), f32)
    for d in range(shards):
        begin = slot_width * d
        inside = (lane >= begin) & (lane < begin + count_ref[0, 0, d])
        used = jnp.where(inside, 1.0, used)
    for turn in range(views // 2, views):
        pick_rows(turn, others[turn - 1, 0])
    for copy in copies:
        copy.wait()

    rows[...] = unpack(home_box, shards)
    spread = sum(
        picked[11 + 16 * c : 27 + 16 * c] * rows[8 + c : 9 + c] for c in range(3)
    )
    cotangents = tuple(rows[i : i + 1] for i in range(5)) + (rows[11:12], rows[12:13])
    (gauss_grad,) = pull((cotangents, spread))
    logit_grad = rows[5:6] * (1.0 - opacity)
    colour_grad = rows[8:11]
    for i in range(10):
        rows[i : i + 1] = gauss_grad[i]
    rows[10:11] = logit_grad
    rows[11:14] = colour_grad
    rows[14:15] = used
    position = camera_centre(camera)
    rows[15:16] = jnp.where(lane == 0, position[0], jnp.where(lane == 1, position[1], position[2]))
    copies = tell(rows, shared, send_view, recv_view)

    def at_home(sent, turn):
        own = fold(mm_nt(thirds(sent), pick_ref[turn]), 3)
        seen = own[14:15]
        return own, [seen * sent[15:16, j : j + 1] for j in range(3)]

    total, centre = at_home(rows[...], 0)
    for r in range(1, views):
        copies[r - 1].wait()
        own, placed = at_home(shared[r - 1], r)
        total = total + own
        centre = [centre[j] + placed[j] for j in range(3)]
    total_ref[0:16] = total
    for j in range(3):
        total_ref[15 + j : 16 + j] = centre[j]
    total_ref[18:24] = jnp.zeros((6, owned), f32)


def update_kernel(
    params_ref,
    first_ref,
    second_ref,
    visible_ref,
    total_ref,
    drawn_ref,
    image_ref,
    out_params,
    out_first,
    out_second,
    grad,
    made_params,
    made_first,
    made_second,
    sems,
):
    image_ref[...] = drawn_ref[...]
    seen = total_ref[14:15] > 0.0
    toward = [params_ref[j : j + 1] - total_ref[15 + j : 16 + j] for j in range(3)]
    square = toward[0] * toward[0] + toward[1] * toward[1] + toward[2] * toward[2]
    reach = 1.0 / jnp.sqrt(jnp.where(seen, square, 1.0))
    basis = jnp.concatenate(harmonics(toward[0] * reach, toward[1] * reach, toward[2] * reach), 0)
    basis = jnp.where(seen, basis, 0.0)
    grad[0:11] = total_ref[0:11]
    for c in range(3):
        grad[11 + 16 * c : 27 + 16 * c] = basis * total_ref[11 + c : 12 + c]
    scale_one = learn_rate / (1.0 - beta_one**adam_step)
    scale_two = 1.0 / (1.0 - beta_two**adam_step)
    keep = visible_ref[...] > 0
    copies = []
    for block in range(2):
        part = slice(0, 32) if block == 0 else slice(32, params_ref.shape[0])
        values = grad[part]
        params, adam_m, adam_v = params_ref[part], first_ref[part], second_ref[part]
        moment_one = beta_one * adam_m + (1.0 - beta_one) * values
        moment_two = beta_two * adam_v + (1.0 - beta_two) * values * values
        stepped = params - scale_one * moment_one / (jnp.sqrt(moment_two * scale_two) + adam_eps)
        made_first[part] = jnp.where(keep, moment_one, adam_m)
        made_second[part] = jnp.where(keep, moment_two, adam_v)
        made_params[part] = jnp.where(keep, stepped, params)
        for i, (made, out) in enumerate(
            [(made_first, out_first), (made_second, out_second), (made_params, out_params)]
        ):
            copy = pltpu.make_async_copy(made.at[part], out.at[part], sems.at[3 * block + i])
            copy.start()
            copies.append(copy)
    for copy in copies:
        copy.wait()


def body(
    params, adam_m, adam_v, visible, cameras, send_index, send_count, tile_lists, tile_pos, target
):
    shards = lax.axis_size("space")
    views = lax.axis_size("view")
    tiles, width = tile_lists.shape[1:]
    slots = send_index.shape[2]
    nparam, owned = params.shape
    if slots != 64 * shards or shards % 2 or nparam != 59:
        return plain_body(
            params,
            adam_m,
            adam_v,
            visible,
            cameras,
            send_index,
            send_count,
            tile_lists,
            tile_pos,
            target,
        )
    center_y = 8.0 * (tiles * shards) / 64.0
    target = jnp.transpose(target, (1, 0, 2))
    vmem = pl.BlockSpec(memory_space=pltpu.VMEM)
    box = pltpu.VMEM((shards, 8, 128), f32)
    image, total = pl.pallas_call(
        functools.partial(step_kernel, shards, views, center_y),
        out_shape=(
            pltpu.VMEM(target.shape, f32),
            pltpu.VMEM((24, owned), f32),
        ),
        in_specs=[pl.BlockSpec(memory_space=pl.ANY)] * 7,
        out_specs=(vmem, vmem),
        scratch_shapes=[
            pltpu.VMEM((nparam, owned), f32),
            pltpu.SMEM(cameras.shape, f32),
            pltpu.VMEM(send_index.shape, jnp.int32),
            pltpu.SMEM(send_count.shape, jnp.int32),
            pltpu.VMEM(tile_lists.shape, jnp.int32),
            pltpu.SMEM(tile_pos.shape, jnp.int32),
            pltpu.VMEM(target.shape, f32),
            pltpu.VMEM((64, owned), f32),
            pltpu.VMEM((64, slots), f32),
            pltpu.VMEM((16, slots), f32),
            box,
            box,
            box,
            box,
            pltpu.VMEM((views - 1, 16, slots), f32),
            pltpu.VMEM((views - 1,) + send_index.shape[1:], jnp.int32),
            pltpu.VMEM((views, owned, slots), bf16),
            pltpu.VMEM((tiles, slots, width), bf16),
            pltpu.VMEM((3, width // 2, width // 2), bf16),
            pltpu.VMEM((tiles, 40, width), f32),
            pltpu.VMEM((tiles * 256, width), f32),
            pltpu.VMEM((tiles * 256, width), f32),
            pltpu.VMEM((tiles * 256, width), f32),
            pltpu.VMEM((tiles * 256, width), bf16),
            pltpu.VMEM((tiles * 256, width), bf16),
            pltpu.VMEM((tiles * 256, width), bf16),
            pltpu.VMEM((tiles * 256, width), bf16),
            pltpu.SemaphoreType.DMA((7,)),
            pltpu.SemaphoreType.DMA((shards - 1,)),
            pltpu.SemaphoreType.DMA((shards - 1,)),
            pltpu.SemaphoreType.DMA((shards - 1,)),
            pltpu.SemaphoreType.DMA((shards - 1,)),
            pltpu.SemaphoreType.DMA((views - 1,)),
            pltpu.SemaphoreType.DMA((views - 1,)),
            pltpu.SemaphoreType.DMA((views - 1,)),
            pltpu.SemaphoreType.DMA((views - 1,)),
        ],
        compiler_params=pltpu.CompilerParams(
            collective_id=0, has_side_effects=True, vmem_limit_bytes=56 * 1024 * 1024
        ),
        cost_estimate=pl.CostEstimate(
            flops=16 * 10**9, bytes_accessed=8 * 10**6, transcendentals=10**6
        ),
        name="step",
    )(params, cameras, send_index, send_count, tile_lists, tile_pos, target)
    like = jax.ShapeDtypeStruct(params.shape, f32)
    image, *updated = pl.pallas_call(
        update_kernel,
        out_shape=(jax.ShapeDtypeStruct(target.shape, f32), like, like, like),
        in_specs=[vmem] * 6,
        out_specs=(vmem,) + (pl.BlockSpec(memory_space=pl.ANY),) * 3,
        scratch_shapes=[
            pltpu.VMEM((64, owned), f32),
            pltpu.VMEM(params.shape, f32),
            pltpu.VMEM(params.shape, f32),
            pltpu.VMEM(params.shape, f32),
            pltpu.SemaphoreType.DMA((6,)),
        ],
        compiler_params=pltpu.CompilerParams(vmem_limit_bytes=16 * 1024 * 1024),
        name="update",
    )(params, adam_m, adam_v, visible.reshape(1, owned), total, image)
    return jnp.transpose(image, (1, 0, 2)), *updated


def solution(mesh):
    placed = (
        P(None, "space"),
        P(None, "space"),
        P(None, "space"),
        P("space"),
        P("view", None),
        P("view", "space", None),
        P("view", "space", None),
        P("view", "space", None),
        P("view", "space"),
        P("view", None, "space"),
    )
    return jax.shard_map(
        body,
        mesh=mesh,
        in_specs=placed,
        out_specs=(P("view", None, "space"), P(None, "space"), P(None, "space"), P(None, "space")),
        check_vma=False,
    )
```

```python
import functools

import jax
import jax.numpy as jnp
from jax import lax
from jax.experimental import pallas as pl
from jax.experimental.pallas import tpu as pltpu
from jax.sharding import PartitionSpec as P

focal_len = 1000.0
center_x = 512.0
harm_zero = 0.28209479177387814
harm_one = 0.4886025119029199
harm_two = (
    1.0925484305920792,
    -1.0925484305920792,
    0.31539156525252005,
    -1.0925484305920792,
    0.5462742152960396,
)
harm_three = (
    -0.5900435899266435,
    2.890611442640554,
    -0.4570457994644658,
    0.3731763325901154,
    -0.4570457994644658,
    1.445305721320277,
    -0.5900435899266435,
)
beta_one = 0.9
beta_two = 0.99
learn_rate = 0.05
adam_eps = 1e-08
adam_step = 100.0


def project(gauss, camera, center_y):
    rotation = [[camera[3 * i + j] for j in range(3)] for i in range(3)]
    offset = [camera[9 + i] for i in range(3)]
    centre = [gauss[i] for i in range(3)]
    viewed = [sum((rotation[i][j] * centre[j] for j in range(3))) + offset[i] for i in range(3)]
    inverse = 1.0 / viewed[2]
    screen_x = focal_len * viewed[0] * inverse + center_x
    screen_y = focal_len * viewed[1] * inverse + center_y
    scales = [jnp.exp(gauss[3 + i]) for i in range(3)]
    length = jnp.sqrt(
        gauss[6] * gauss[6] + gauss[7] * gauss[7] + gauss[8] * gauss[8] + gauss[9] * gauss[9]
    )
    quat_w, quat_x, quat_y, quat_z = [gauss[6 + i] / length for i in range(4)]
    spin = [
        [
            1.0 - 2.0 * (quat_y * quat_y + quat_z * quat_z),
            2.0 * (quat_x * quat_y - quat_w * quat_z),
            2.0 * (quat_x * quat_z + quat_w * quat_y),
        ],
        [
            2.0 * (quat_x * quat_y + quat_w * quat_z),
            1.0 - 2.0 * (quat_x * quat_x + quat_z * quat_z),
            2.0 * (quat_y * quat_z - quat_w * quat_x),
        ],
        [
            2.0 * (quat_x * quat_z - quat_w * quat_y),
            2.0 * (quat_y * quat_z + quat_w * quat_x),
            1.0 - 2.0 * (quat_x * quat_x + quat_y * quat_y),
        ],
    ]
    factor = [[spin[i][j] * scales[j] for j in range(3)] for i in range(3)]
    sigma = [
        [sum((factor[i][j] * factor[k][j] for j in range(3))) for k in range(3)] for i in range(3)
    ]
    near = focal_len * inverse
    lean_x = -focal_len * viewed[0] * inverse * inverse
    lean_y = -focal_len * viewed[1] * inverse * inverse
    jacob = [
        [near * rotation[0][j] + lean_x * rotation[2][j] for j in range(3)],
        [near * rotation[1][j] + lean_y * rotation[2][j] for j in range(3)],
    ]
    halfway = [
        [sum((jacob[a][i] * sigma[i][k] for i in range(3))) for k in range(3)] for a in range(2)
    ]
    upper = sum((halfway[0][k] * jacob[0][k] for k in range(3))) + 0.3
    middle = sum((halfway[0][k] * jacob[1][k] for k in range(3)))
    lower = sum((halfway[1][k] * jacob[1][k] for k in range(3))) + 0.3
    determinant = upper * lower - middle * middle
    conic_a = lower / determinant
    conic_b = -middle / determinant
    conic_c = upper / determinant
    opacity = jax.nn.sigmoid(gauss[10])
    camera_pos = [-sum((rotation[i][j] * offset[i] for i in range(3))) for j in range(3)]
    toward = [centre[j] - camera_pos[j] for j in range(3)]
    reach = jnp.sqrt(toward[0] * toward[0] + toward[1] * toward[1] + toward[2] * toward[2])
    unit_x = toward[0] / reach
    unit_y = toward[1] / reach
    unit_z = toward[2] / reach
    square_x = unit_x * unit_x
    square_y = unit_y * unit_y
    square_z = unit_z * unit_z
    basis = [
        harm_zero + 0.0 * unit_x,
        -harm_one * unit_y,
        harm_one * unit_z,
        -harm_one * unit_x,
        harm_two[0] * unit_x * unit_y,
        harm_two[1] * unit_y * unit_z,
        harm_two[2] * (2.0 * square_z - square_x - square_y),
        harm_two[3] * unit_x * unit_z,
        harm_two[4] * (square_x - square_y),
        harm_three[0] * unit_y * (3.0 * square_x - square_y),
        harm_three[1] * unit_x * unit_y * unit_z,
        harm_three[2] * unit_y * (4.0 * square_z - square_x - square_y),
        harm_three[3] * unit_z * (2.0 * square_z - 3.0 * square_x - 3.0 * square_y),
        harm_three[4] * unit_x * (4.0 * square_z - square_x - square_y),
        harm_three[5] * unit_z * (square_x - square_y),
        harm_three[6] * unit_x * (square_x - 3.0 * square_y),
    ]
    colors = [0.5 + sum((basis[k] * gauss[11 + 16 * c + k] for k in range(16))) for c in range(3)]
    return jnp.stack(
        [
            screen_x,
            screen_y,
            conic_a,
            conic_b,
            conic_c,
            opacity,
            colors[0],
            colors[1],
            colors[2],
            viewed[2],
            inverse,
        ]
    )


def shade_tile(entries, valid, tile):
    lane = jnp.arange(256, dtype=jnp.int32)
    column = tile % 64 * 16 + lane % 16
    height = tile // 64 * 16 + lane // 16
    pixel_x = column.astype(entries.dtype) + 0.5
    pixel_y = height.astype(entries.dtype) + 0.5
    apart_x = pixel_x[:, None] - entries[0][None, :]
    apart_y = pixel_y[:, None] - entries[1][None, :]
    quad = (
        entries[2][None, :] * apart_x * apart_x
        + 2.0 * entries[3][None, :] * apart_x * apart_y
        + entries[4][None, :] * apart_y * apart_y
    )
    alpha = entries[5][None, :] * jnp.exp(-0.5 * quad) * valid[None, :]
    keeping = jnp.log1p(-alpha)
    weight = alpha * jnp.exp(jnp.cumsum(keeping, axis=1) - keeping)
    feats = entries[6:11]
    return lax.dot_general(feats, weight, (((1,), (1,)), ((), ())), precision=lax.Precision.HIGHEST)


def adam_update(params, adam_m, adam_v, grad, visible):
    moment_one = beta_one * adam_m + (1.0 - beta_one) * grad
    moment_two = beta_two * adam_v + (1.0 - beta_two) * grad * grad
    first_hat = moment_one / (1.0 - beta_one**adam_step)
    second_hat = moment_two / (1.0 - beta_two**adam_step)
    stepped = params - learn_rate * first_hat / (jnp.sqrt(second_hat) + adam_eps)
    keep = (visible > 0)[None, :]
    return (
        jnp.where(keep, stepped, params),
        jnp.where(keep, moment_one, adam_m),
        jnp.where(keep, moment_two, adam_v),
    )


def composite(buffer, block_entries, block_usable, block_places):

    def one_block(item):
        entries, usable, places = item
        return jax.vmap(shade_tile, in_axes=(1, 0, 0))(buffer[:, entries], usable, places)

    return lax.map(jax.checkpoint(one_block), (block_entries, block_usable, block_places))


def plain_body(
    params, adam_m, adam_v, visible, cameras, send_index, send_count, tile_lists, tile_pos, target
):
    shards = lax.axis_size("space")
    tile_count = tile_lists.shape[1]
    list_width = tile_lists.shape[2]
    center_y = 8.0 * (tile_count * shards) / 64.0
    camera = cameras[0]
    route = send_index[0, 0]
    slot_width = route.shape[0] // shards
    slot_grid = jnp.arange(route.shape[0], dtype=jnp.int32).reshape(shards, slot_width) % slot_width
    in_use = (slot_grid < send_count[0, 0][:, None]).reshape(-1).astype(jnp.float32)

    def outgoing(gauss):
        return project(gauss, camera, center_y)[:, route] * in_use[None, :]

    sending, pull_send = jax.vjp(outgoing, params)
    arrived = lax.all_to_all(sending, "space", split_axis=1, concat_axis=1, tiled=True)
    per_block = 2
    block_count = tile_count // per_block
    lists = tile_lists[0]
    block_usable = (lists >= 0).astype(jnp.float32).reshape(block_count, per_block, list_width)
    block_entries = jnp.maximum(lists, 0).reshape(block_count, per_block, list_width)
    block_places = tile_pos[0].reshape(block_count, per_block)

    def draw_tiles(buffer):
        return composite(buffer, block_entries, block_usable, block_places).reshape(
            tile_count, 5, 256
        )

    tiles, pull_tiles = jax.vjp(draw_tiles, arrived)
    image = jnp.transpose(tiles, (1, 0, 2)).reshape(5, tile_count * 256)
    residue = (image - target[0]).reshape(5, tile_count, 256)
    (record_grad,) = pull_tiles(jnp.transpose(residue, (1, 0, 2)))
    returned = lax.all_to_all(record_grad, "space", split_axis=1, concat_axis=1, tiled=True)
    (grad,) = pull_send(returned)
    total = lax.psum(grad, "view")
    new_params, new_m, new_v = adam_update(params, adam_m, adam_v, total, visible)
    return (image[None], new_params, new_m, new_v)


f32 = jnp.float32
bf16 = jnp.bfloat16
MESH_ID = pl.DeviceIdType.MESH


def harmonics(unit_x, unit_y, unit_z):
    square_x = unit_x * unit_x
    square_y = unit_y * unit_y
    square_z = unit_z * unit_z
    return [
        jnp.full_like(unit_x, harm_zero),
        -harm_one * unit_y,
        harm_one * unit_z,
        -harm_one * unit_x,
        harm_two[0] * unit_x * unit_y,
        harm_two[1] * unit_y * unit_z,
        harm_two[2] * (2.0 * square_z - square_x - square_y),
        harm_two[3] * unit_x * unit_z,
        harm_two[4] * (square_x - square_y),
        harm_three[0] * unit_y * (3.0 * square_x - square_y),
        harm_three[1] * unit_x * unit_y * unit_z,
        harm_three[2] * unit_y * (4.0 * square_z - square_x - square_y),
        harm_three[3] * unit_z * (2.0 * square_z - 3.0 * square_x - 3.0 * square_y),
        harm_three[4] * unit_x * (4.0 * square_z - square_x - square_y),
        harm_three[5] * unit_z * (square_x - square_y),
        harm_three[6] * unit_x * (square_x - 3.0 * square_y),
    ]


def camera_centre(camera):
    return [-sum(camera[3 * i + j] * camera[9 + i] for i in range(3)) for j in range(3)]


def geometry(gauss, camera, center_y):
    rotation = [[camera[3 * i + j] for j in range(3)] for i in range(3)]
    offset = [camera[9 + i] for i in range(3)]
    centre = gauss[0:3]
    viewed = [sum(rotation[i][j] * centre[j] for j in range(3)) + offset[i] for i in range(3)]
    inverse = 1.0 / viewed[2]
    near = focal_len * inverse
    ratio_x = viewed[0] * inverse
    ratio_y = viewed[1] * inverse
    screen_x = focal_len * ratio_x + center_x
    screen_y = focal_len * ratio_y + center_y
    scales = [jnp.exp(2.0 * gauss[3 + i]) for i in range(3)]
    squares = [gauss[6 + i] * gauss[6 + i] for i in range(4)]
    double = 2.0 / (squares[0] + squares[1] + squares[2] + squares[3])
    qw, qx, qy, qz = gauss[6:10]
    dx, dy, dz = double * qx, double * qy, double * qz
    xx, yy, zz = dx * qx, dy * qy, dz * qz
    xy, xz, yz = dx * qy, dx * qz, dy * qz
    wx, wy, wz = dx * qw, dy * qw, dz * qw
    spin = [
        [1.0 - (yy + zz), xy - wz, xz + wy],
        [xy + wz, 1.0 - (xx + zz), yz - wx],
        [xz - wy, yz + wx, 1.0 - (xx + yy)],
    ]
    jacob = [
        [near * (rotation[0][j] - ratio_x * rotation[2][j]) for j in range(3)],
        [near * (rotation[1][j] - ratio_y * rotation[2][j]) for j in range(3)],
    ]
    turned = [[sum(jacob[a][i] * spin[i][k] for i in range(3)) for k in range(3)] for a in range(2)]
    scaled = [turned[0][k] * scales[k] for k in range(3)]
    upper = sum(scaled[k] * turned[0][k] for k in range(3)) + 0.3
    middle = sum(scaled[k] * turned[1][k] for k in range(3))
    lower = sum(turned[1][k] * scales[k] * turned[1][k] for k in range(3)) + 0.3
    over = 1.0 / (upper * lower - middle * middle)
    position = camera_centre(camera)
    toward = [centre[j] - position[j] for j in range(3)]
    reach = 1.0 / jnp.sqrt(toward[0] * toward[0] + toward[1] * toward[1] + toward[2] * toward[2])
    basis = harmonics(toward[0] * reach, toward[1] * reach, toward[2] * reach)
    return (
        screen_x,
        screen_y,
        lower * over,
        -middle * over,
        upper * over,
        viewed[2],
        inverse,
    ), basis


def halves(x):
    high = x.astype(bf16).astype(f32)
    return high, x - high


def thirds(x):
    high, rest = halves(x)
    mid, low = halves(rest)
    return jnp.concatenate([high, mid, low], axis=0).astype(bf16)


def two(x):
    high = x.astype(bf16)
    return high, (x - high.astype(f32)).astype(bf16)


def mm(a, b):
    return jnp.dot(a, b, preferred_element_type=f32)


def mm_nt(a, b):
    return lax.dot_general(a, b, (((1,), (1,)), ((), ())), preferred_element_type=f32)


def mm_tn(a, b):
    return lax.dot_general(a, b, (((0,), (0,)), ((), ())), preferred_element_type=f32)


def fold(x, count):
    rows = x.shape[0] // count
    return sum(x[rows * i : rows * (i + 1)] for i in range(count))


def pack(rows, box, shards):
    lane = lax.broadcasted_iota(jnp.int32, (8, 128), 1)
    for j in range(shards // 2):
        first = rows[0:8, 128 * j : 128 * j + 128]
        second = rows[8:16, 128 * j : 128 * j + 128]
        box[2 * j] = jnp.where(lane < 64, first, pltpu.roll(second, 64, 1))
        box[2 * j + 1] = jnp.where(lane < 64, pltpu.roll(first, 64, 1), second)


def unpack(box, shards):
    lane = lax.broadcasted_iota(jnp.int32, (8, 128), 1)
    top, bottom = [], []
    for j in range(shards // 2):
        even, odd = box[2 * j], box[2 * j + 1]
        top.append(jnp.where(lane < 64, even, pltpu.roll(odd, 64, 1)))
        bottom.append(jnp.where(lane < 64, pltpu.roll(even, 64, 1), odd))
    return jnp.concatenate([jnp.concatenate(top, 1), jnp.concatenate(bottom, 1)], 0)


def step_kernel(
    shards,
    views,
    center_y,
    params_hbm,
    camera_hbm,
    index_hbm,
    count_hbm,
    lists_hbm,
    place_hbm,
    target_hbm,
    image_ref,
    total_ref,
    held,
    camera_ref,
    index_ref,
    count_ref,
    lists_ref,
    place_ref,
    target_ref,
    wide,
    picked,
    rows,
    out_box,
    in_box,
    back_box,
    home_box,
    shared,
    others,
    pick_ref,
    home_hot,
    list_hot,
    list_back,
    tri_ref,
    near_ref,
    alpha_ref,
    ratio_ref,
    sum_ref,
    part_high,
    part_low,
    weight_high,
    weight_low,
    load_sem,
    send_sem,
    recv_sem,
    send_back,
    recv_back,
    send_view,
    recv_view,
    send_index,
    recv_index,
):
    me_view = lax.axis_index("view")
    me = lax.axis_index("space")
    slots = index_ref.shape[2]
    owned = params_hbm.shape[1]
    tiles = lists_ref.shape[1]
    width = lists_ref.shape[2]
    half = width // 2
    slot_width = slots // shards

    pairs = [
        (index_hbm, index_ref),
        (params_hbm, held),
        (camera_hbm, camera_ref),
        (lists_hbm, lists_ref),
        (count_hbm, count_ref),
        (place_hbm, place_ref),
        (target_hbm, target_ref),
    ]
    loads = [
        pltpu.make_async_copy(source, there, load_sem.at[i])
        for i, (source, there) in enumerate(pairs)
    ]
    for load in loads:
        load.start()
    barrier = pltpu.get_barrier_semaphore()
    for r in range(1, shards):
        pl.semaphore_signal(
            barrier, inc=1, device_id=(me_view, lax.rem(me + r, shards)), device_id_type=MESH_ID
        )
    for r in range(1, views):
        pl.semaphore_signal(
            barrier, inc=1, device_id=(lax.rem(me_view + r, views), me), device_id_type=MESH_ID
        )

    loads[0].wait()
    count_up = lax.broadcasted_iota(jnp.int32, (32, slots), 0)

    def pick_rows(i, carry):
        at = pl.multiple_of(32 * i, 32)
        pick_ref[pl.ds(at, 32)] = jnp.where(count_up + at == index_ref[0], 1.0, 0.0).astype(bf16)
        return carry

    lax.fori_loop(0, owned // 32, pick_rows, 0, unroll=True)

    def turned(table, wanted, columns):
        column = jnp.transpose(jnp.broadcast_to(wanted.astype(f32), (8, wanted.shape[1])))
        across = lax.broadcasted_iota(jnp.int32, (32, columns), 1).astype(f32)
        for i in range(wanted.shape[1] // 32):
            part = slice(32 * i, 32 * i + 32)
            table[part] = jnp.where(across == column[part, 0:1], 1.0, 0.0).astype(bf16)

    wide[56:64] = jnp.zeros((8, owned), f32)
    for load in loads[1:]:
        load.wait()
    wide[0:59] = held[...]
    picked[...] = fold(mm(thirds(wide[...]), pick_ref[...]), 3)

    camera = [camera_ref[0, i] for i in range(12)]
    gauss = [picked[i : i + 1] for i in range(10)]

    def project_rows(values):
        outs, basis = geometry(values, camera, center_y)
        return outs, jnp.concatenate(basis, axis=0)

    outs, basis = project_rows(gauss)
    opacity = 1.0 / (1.0 + jnp.exp(-picked[10:11]))
    rows[...] = jnp.zeros_like(rows)
    for i in range(5):
        rows[i : i + 1] = outs[i]
    rows[5:6] = opacity
    for c in range(3):
        rows[8 + c : 9 + c] = 0.5 + jnp.sum(
            basis * picked[11 + 16 * c : 27 + 16 * c], axis=0, keepdims=True
        )
    rows[11:12] = outs[5]
    rows[12:13] = outs[6]
    pack(rows, out_box, shards)

    pl.semaphore_wait(barrier, shards + views - 2)

    def swap(source, landing, sends, recvs):
        copies = []
        for r in range(1, shards):
            to = lax.rem(me + r, shards)
            copy = pltpu.make_async_remote_copy(
                src_ref=source.at[to],
                dst_ref=landing.at[me],
                send_sem=sends.at[r - 1],
                recv_sem=recvs.at[r - 1],
                device_id=(me_view, to),
                device_id_type=MESH_ID,
            )
            copy.start()
            copies.append(copy)
        landing[pl.ds(me, 1)] = source[pl.ds(me, 1)]
        return copies

    def tell(source, landing, sends, recvs):
        copies = []
        for r in range(1, views):
            copy = pltpu.make_async_remote_copy(
                src_ref=source,
                dst_ref=landing.at[r - 1],
                send_sem=sends.at[r - 1],
                recv_sem=recvs.at[r - 1],
                device_id=(lax.rem(me_view + r, views), me),
                device_id_type=MESH_ID,
            )
            copy.start()
            copies.append(copy)
        return copies

    copies = swap(out_box, in_box, send_sem, recv_sem)
    numbers = tell(index_ref.at[0], others, send_index, recv_index)

    _, pull = jax.vjp(project_rows, gauss)
    def list_rows(i, carry):
        at = pl.multiple_of(32 * i, 32)
        for t in range(tiles):
            list_hot[t, pl.ds(at, 32)] = jnp.where(
                count_up + at == lists_ref[0, t : t + 1], 1.0, 0.0
            ).astype(bf16)
        return carry

    lax.fori_loop(0, slots // 32, list_rows, 0, unroll=True)
    first = lax.broadcasted_iota(jnp.int32, (half, half), 0)
    second = lax.broadcasted_iota(jnp.int32, (half, half), 1)
    tri_ref[0] = jnp.where(first < second, 1.0, 0.0).astype(bf16)
    tri_ref[1] = jnp.where(first > second, 1.0, 0.0).astype(bf16)
    tri_ref[2] = jnp.ones((half, half), bf16)
    pixel = lax.broadcasted_iota(jnp.int32, (16, 256), 1)
    kind = lax.broadcasted_iota(jnp.int32, (16, 256), 0)
    grid_x = (pixel % 16).astype(f32) - 7.5
    grid_y = (pixel // 16).astype(f32) - 7.5
    moments_of = jnp.where(kind == 0, 1.0, 0.0)
    for i, values in enumerate(
        [grid_x, grid_y, grid_x * grid_x, grid_x * grid_y, grid_y * grid_y]
    ):
        moments_of = jnp.where(kind == i + 1, values, moments_of)
    moments_of = moments_of.astype(bf16)
    side_x = lax.broadcasted_iota(jnp.int32, (16, 1), 0).astype(f32) - 7.5
    for t in range(tiles):
        turned(list_back.at[t], lists_ref[0, t : t + 1], slots)
    for copy in numbers:
        copy.wait()

    for copy in copies:
        copy.wait()
    arrived = thirds(unpack(in_box, shards))

    spans = [slice(256 * t, 256 * t + 256) for t in range(tiles)]
    drawn_from = []
    for t in range(tiles):
        entries = fold(mm(arrived, list_hot[t]), 3)
        place = place_ref[0, t]
        middle_x = (place % 64 * 16 + 8).astype(f32)
        middle_y = (place // 64 * 16 + 8).astype(f32)
        u = entries[0:1] - middle_x
        y = entries[1:2] - middle_y
        a, b, c = entries[2:3], entries[3:4], entries[4:5]
        drawn_from.append((u, y, a, b, c, entries[8:16]))
        apart_x = side_x - u
        near_ref[t, 0:16] = apart_x
        near_ref[t, 16:32] = (-0.5 * a) * apart_x * apart_x
        near_ref[t, 32:33] = y
        near_ref[t, 33:34] = -b
        near_ref[t, 34:35] = -0.5 * c
        near_ref[t, 35:36] = entries[5:6]

    def light(i, carry):
        at = pl.multiple_of(16 * i, 16)
        for t in range(tiles):
            apart_y = (i.astype(f32) - 7.5) - near_ref[t, 32:33]
            line = near_ref[t, 33:34] * apart_y
            shift = near_ref[t, 34:35] * apart_y * apart_y
            quad = near_ref[t, 16:32] + line * near_ref[t, 0:16] + shift
            alpha = near_ref[t, 35:36] * jnp.exp(quad)
            through = 1.0 - alpha
            keep_high, keep_low = two(jnp.log(through))
            here = pl.ds(256 * t + at, 16)
            alpha_ref[here] = alpha
            inverse = pl.reciprocal(through, approx=True)
            ratio_ref[here] = alpha * (inverse * (2.0 - through * inverse))
            part_high[here] = keep_high
            part_low[here] = keep_low
        return carry

    lax.fori_loop(0, 16, light, 0, unroll=True)

    def ordered_sum(order):
        whole, cut = (slice(0, half), slice(half, width))
        if order:
            whole, cut = cut, whole
        sum_ref[:, whole] = mm(part_high[:, whole], tri_ref[order]) + mm(
            part_low[:, whole], tri_ref[order]
        )
        sum_ref[:, cut] = (
            mm(part_high[:, cut], tri_ref[order])
            + mm(part_low[:, cut], tri_ref[order])
            + mm(part_high[:, whole], tri_ref[2])
            + mm(part_low[:, whole], tri_ref[2])
        )

    ordered_sum(0)
    steps = 16 * tiles

    def weigh(i, carry):
        here = pl.ds(pl.multiple_of(16 * i, 16), 16)
        weight = alpha_ref[here] * jnp.exp(sum_ref[here])
        alpha_ref[here] = weight
        weight_high[here], weight_low[here] = two(weight)
        return carry

    lax.fori_loop(0, steps, weigh, 0, unroll=True)

    feat_grads = []
    for t in range(tiles):
        feat_high, feat_low = halves(drawn_from[t][5])
        feat_two = jnp.concatenate([feat_high, feat_low], 0).astype(bf16)
        drawn = fold(
            mm_nt(feat_two, weight_high[spans[t]]) + mm_nt(feat_two, weight_low[spans[t]]), 2
        )
        for ch in range(5):
            image_ref[ch, :, spans[t]] = drawn[ch : ch + 1]
        shown = jnp.concatenate(
            [target_ref[ch, :, spans[t]] for ch in range(5)] + [jnp.zeros((3, 256), f32)], 0
        )
        res_high, res_low = halves(drawn - shown)
        res_two = jnp.concatenate([res_high, res_low], 0)
        sum_ref[spans[t]] = mm_tn(
            jnp.concatenate([res_two, res_two], 0).astype(bf16),
            jnp.concatenate([feat_high, feat_high, feat_low, feat_low], 0).astype(bf16),
        )
        res_two = res_two.astype(bf16)
        feat_grads.append(
            fold(mm(res_two, weight_high[spans[t]]) + mm(res_two, weight_low[spans[t]]), 2)
        )

    def pull_back(i, carry):
        here = pl.ds(pl.multiple_of(16 * i, 16), 16)
        part = alpha_ref[here] * sum_ref[here]
        alpha_ref[here] = part
        part_high[here], part_low[here] = two(part)
        return carry

    lax.fori_loop(0, steps, pull_back, 0, unroll=True)
    ordered_sum(1)

    def slope_of(i, carry):
        here = pl.ds(pl.multiple_of(16 * i, 16), 16)
        part_high[here], part_low[here] = two(alpha_ref[here] - sum_ref[here] * ratio_ref[here])
        return carry

    lax.fori_loop(0, steps, slope_of, 0, unroll=True)

    returning = jnp.zeros((16, slots), f32)
    for t in range(tiles):
        u, y, a, b, c, _ = drawn_from[t]
        moments = mm(moments_of, part_high[spans[t]]) + mm(moments_of, part_low[spans[t]])
        m, mx, my, mxx, mxy, myy = [moments[i : i + 1] for i in range(6)]
        sx = mx - u * m
        sy = my - y * m
        sxx = mxx - u * mx - u * sx
        sxy = mxy - u * my - y * sx
        syy = myy - y * my - y * sy
        zero = jnp.zeros((2, width), f32)
        entry_grad = jnp.concatenate(
            [
                a * sx + b * sy,
                b * sx + c * sy,
                -0.5 * sxx,
                -sxy,
                -0.5 * syy,
                m,
                zero,
                feat_grads[t],
            ],
            0,
        )
        returning = returning + fold(mm(thirds(entry_grad), list_back[t]), 3)

    rows[...] = returning
    pack(rows, back_box, shards)
    copies = swap(back_box, home_box, send_back, recv_back)
    lane = lax.broadcasted_iota(jnp.int32, (1, slots), 1)
    used = jnp.zeros((1, slots), f32)
    for d in range(shards):
        begin = slot_width * d
        inside = (lane >= begin) & (lane < begin + count_ref[0, 0, d])
        used = jnp.where(inside, 1.0, used)
    for r in range(1, views):
        turned(home_hot.at[r - 1], others[r - 1], owned)
    for copy in copies:
        copy.wait()

    rows[...] = unpack(home_box, shards)
    spread = sum(
        picked[11 + 16 * c : 27 + 16 * c] * rows[8 + c : 9 + c] for c in range(3)
    )
    cotangents = tuple(rows[i : i + 1] for i in range(5)) + (rows[11:12], rows[12:13])
    (gauss_grad,) = pull((cotangents, spread))
    logit_grad = rows[5:6] * (1.0 - opacity)
    colour_grad = rows[8:11]
    for i in range(10):
        rows[i : i + 1] = gauss_grad[i]
    rows[10:11] = logit_grad
    rows[11:14] = colour_grad
    rows[14:15] = used
    position = camera_centre(camera)
    rows[15:16] = jnp.where(lane == 0, position[0], jnp.where(lane == 1, position[1], position[2]))
    copies = tell(rows, shared, send_view, recv_view)

    def at_home(sent, r):
        parts = thirds(sent)
        own = fold(mm(parts, home_hot[r - 1]) if r else mm_nt(parts, pick_ref[...]), 3)
        seen = own[14:15]
        return own, [seen * sent[15:16, j : j + 1] for j in range(3)]

    total, centre = at_home(rows[...], 0)
    for r in range(1, views):
        copies[r - 1].wait()
        own, placed = at_home(shared[r - 1], r)
        total = total + own
        centre = [centre[j] + placed[j] for j in range(3)]
    total_ref[0:16] = total
    for j in range(3):
        total_ref[15 + j : 16 + j] = centre[j]
    total_ref[18:24] = jnp.zeros((6, owned), f32)


def update_kernel(
    params_ref,
    first_ref,
    second_ref,
    visible_ref,
    total_ref,
    drawn_ref,
    image_ref,
    out_params,
    out_first,
    out_second,
    grad,
):
    image_ref[...] = drawn_ref[...]
    seen = total_ref[14:15] > 0.0
    toward = [params_ref[j : j + 1] - total_ref[15 + j : 16 + j] for j in range(3)]
    square = toward[0] * toward[0] + toward[1] * toward[1] + toward[2] * toward[2]
    reach = 1.0 / jnp.sqrt(jnp.where(seen, square, 1.0))
    basis = jnp.concatenate(harmonics(toward[0] * reach, toward[1] * reach, toward[2] * reach), 0)
    basis = jnp.where(seen, basis, 0.0)
    grad[0:11] = total_ref[0:11]
    for c in range(3):
        grad[11 + 16 * c : 27 + 16 * c] = basis * total_ref[11 + c : 12 + c]
    values = grad[0:59]
    params, adam_m, adam_v = params_ref[...], first_ref[...], second_ref[...]
    moment_one = beta_one * adam_m + (1.0 - beta_one) * values
    moment_two = beta_two * adam_v + (1.0 - beta_two) * values * values
    scale_one = learn_rate / (1.0 - beta_one**adam_step)
    scale_two = 1.0 / (1.0 - beta_two**adam_step)
    stepped = params - scale_one * moment_one / (jnp.sqrt(moment_two * scale_two) + adam_eps)
    keep = visible_ref[...] > 0
    out_params[...] = jnp.where(keep, stepped, params)
    out_first[...] = jnp.where(keep, moment_one, adam_m)
    out_second[...] = jnp.where(keep, moment_two, adam_v)


def body(
    params, adam_m, adam_v, visible, cameras, send_index, send_count, tile_lists, tile_pos, target
):
    shards = lax.axis_size("space")
    views = lax.axis_size("view")
    tiles, width = tile_lists.shape[1:]
    slots = send_index.shape[2]
    nparam, owned = params.shape
    if slots != 64 * shards or shards % 2 or nparam != 59:
        return plain_body(
            params,
            adam_m,
            adam_v,
            visible,
            cameras,
            send_index,
            send_count,
            tile_lists,
            tile_pos,
            target,
        )
    center_y = 8.0 * (tiles * shards) / 64.0
    target = jnp.transpose(target, (1, 0, 2))
    vmem = pl.BlockSpec(memory_space=pltpu.VMEM)
    box = pltpu.VMEM((shards, 8, 128), f32)
    image, total = pl.pallas_call(
        functools.partial(step_kernel, shards, views, center_y),
        out_shape=(
            pltpu.VMEM(target.shape, f32),
            pltpu.VMEM((24, owned), f32),
        ),
        in_specs=[pl.BlockSpec(memory_space=pl.ANY)] * 7,
        out_specs=(vmem, vmem),
        scratch_shapes=[
            pltpu.VMEM((nparam, owned), f32),
            pltpu.SMEM(cameras.shape, f32),
            pltpu.VMEM(send_index.shape, jnp.int32),
            pltpu.SMEM(send_count.shape, jnp.int32),
            pltpu.VMEM(tile_lists.shape, jnp.int32),
            pltpu.SMEM(tile_pos.shape, jnp.int32),
            pltpu.VMEM(target.shape, f32),
            pltpu.VMEM((64, owned), f32),
            pltpu.VMEM((64, slots), f32),
            pltpu.VMEM((16, slots), f32),
            box,
            box,
            box,
            box,
            pltpu.VMEM((views - 1, 16, slots), f32),
            pltpu.VMEM((views - 1,) + send_index.shape[1:], jnp.int32),
            pltpu.VMEM((owned, slots), bf16),
            pltpu.VMEM((views - 1, slots, owned), bf16),
            pltpu.VMEM((tiles, slots, width), bf16),
            pltpu.VMEM((tiles, width, slots), bf16),
            pltpu.VMEM((3, width // 2, width // 2), bf16),
            pltpu.VMEM((tiles, 40, width), f32),
            pltpu.VMEM((tiles * 256, width), f32),
            pltpu.VMEM((tiles * 256, width), f32),
            pltpu.VMEM((tiles * 256, width), f32),
            pltpu.VMEM((tiles * 256, width), bf16),
            pltpu.VMEM((tiles * 256, width), bf16),
            pltpu.VMEM((tiles * 256, width), bf16),
            pltpu.VMEM((tiles * 256, width), bf16),
            pltpu.SemaphoreType.DMA((7,)),
            pltpu.SemaphoreType.DMA((shards - 1,)),
            pltpu.SemaphoreType.DMA((shards - 1,)),
            pltpu.SemaphoreType.DMA((shards - 1,)),
            pltpu.SemaphoreType.DMA((shards - 1,)),
            pltpu.SemaphoreType.DMA((views - 1,)),
            pltpu.SemaphoreType.DMA((views - 1,)),
            pltpu.SemaphoreType.DMA((views - 1,)),
            pltpu.SemaphoreType.DMA((views - 1,)),
        ],
        compiler_params=pltpu.CompilerParams(
            collective_id=0, has_side_effects=True, vmem_limit_bytes=56 * 1024 * 1024
        ),
        cost_estimate=pl.CostEstimate(
            flops=16 * 10**9, bytes_accessed=8 * 10**6, transcendentals=10**6
        ),
        name="step",
    )(params, cameras, send_index, send_count, tile_lists, tile_pos, target)
    like = jax.ShapeDtypeStruct(params.shape, f32)
    image, *updated = pl.pallas_call(
        update_kernel,
        out_shape=(jax.ShapeDtypeStruct(target.shape, f32), like, like, like),
        in_specs=[vmem] * 6,
        out_specs=(vmem,) * 4,
        scratch_shapes=[pltpu.VMEM((64, owned), f32)],
        compiler_params=pltpu.CompilerParams(vmem_limit_bytes=16 * 1024 * 1024),
        name="update",
    )(params, adam_m, adam_v, visible.reshape(1, owned), total, image)
    return jnp.transpose(image, (1, 0, 2)), *updated


def solution(mesh):
    placed = (
        P(None, "space"),
        P(None, "space"),
        P(None, "space"),
        P("space"),
        P("view", None),
        P("view", "space", None),
        P("view", "space", None),
        P("view", "space", None),
        P("view", "space"),
        P("view", None, "space"),
    )
    return jax.shard_map(
        body,
        mesh=mesh,
        in_specs=placed,
        out_specs=(P("view", None, "space"), P(None, "space"), P(None, "space"), P(None, "space")),
        check_vma=False,
    )
```
